128 devices in a mesh: tm: 4 (over z), space: 32 (over x, y, core).
Axes of the slice: x: 4, y: 4, z: 4, core: 2. Of those that a mesh axis runs over, the one named last changes fastest.
Arguments:
- thickness: float32 [4, 1024, 2048], P('tm', 'space'), may hold values from 0 to 2
- bed_class: int32 [1024, 2048], P('space'), may hold values from 0 to 15
- ice_mask: int32 [1024, 2048], P('space'), may hold values 0 or 1
- zone_index: int32 [1024, 2048], P('space'), may hold values from 0 to 7
- bed_levels: float32 [16], replicated, may hold values from -1 to 1
- balance_rates: float32 [8], replicated, may hold values from -0.3 to 0.3
Outputs:
- end_state: float32 [4, 1024, 2048], P('tm', 'space')
- next_start: float32 [4, 1024, 2048], P('tm', 'space')
The draws below stay inside these ranges and needn't reach their ends.
All inputs are finite; a program needn't handle non-finite values. No bound on the sum of `ice_mask` on one device may be relied on, other than what follows from the above.
Results may differ from the reference program's by a relative error of at most 0.0001.
Values sent between devices are 32-bit elements; how exact they have to be, the bound alone decides.
No kernel may reach another device: no remote copies, remote signals or barrier semaphores. Data moves between devices by JAX's collectives and lax.ppermute only.
A program may use at most 128 MiB of HBM per device.

```python
import jax
import jax.numpy as jnp

NY = 2048
FSTEPS = 4
CSTEPS = 2
NCLASS = 16
NZONE = 8
SLICES = 4
NX = 1024
N_TM = 4


def with_ends(values, stream_key, least, largest):
    shape = values.shape
    place = [jax.random.randint(jax.random.fold_in(stream_key, axis), (), 0, shape[axis]) for axis in range(len(shape))]
    values = values.at[tuple(place)].set(least)
    longest = shape.index(max(shape))
    place[longest] = (place[longest] + 1) % shape[longest]
    return values.at[tuple(place)].set(largest)


def steps_of(stream_key, dims, cuts, low, largest):
    gain, own = 1.0, jax.random.fold_in(stream_key, 6)
    for position, shards_of in cuts:
        draws = jnp.exp(jax.random.uniform(jax.random.fold_in(own, position), (shards_of,), jnp.float32, low / len(cuts), largest / len(cuts)))
        gain = gain * jnp.repeat(draws, dims[position] // shards_of).reshape([-1 if axis == position else 1 for axis in range(len(dims))])
    return gain


def setup_inputs(seed: int = 0) -> dict:
    splits = jax.random.split(jax.random.key(seed), 7)
    return {
        "thickness": jnp.clip(2.0 * jax.random.uniform(splits[0], (SLICES, NX, NY), jnp.float32) ** steps_of(splits[0], (SLICES, NX, NY), ((0, 4), (1, 32)), -0.2, 0.2), 0.0, 2.0),
        "bed_class": with_ends(jax.random.randint(splits[1], (NX, NY), 0, NCLASS), jax.random.fold_in(splits[1], 1), 0, NCLASS - 1).astype(jnp.int32),
        "ice_mask": with_ends((jax.random.randint(splits[2], (NX, NY), 0, 4) < 3).astype(jnp.int32), jax.random.fold_in(splits[2], 1), 0, 1),
        "zone_index": with_ends(jax.random.randint(splits[3], (NX, NY), 0, NZONE), jax.random.fold_in(splits[3], 1), 0, NZONE - 1).astype(jnp.int32),
        "bed_levels": jnp.clip(jax.random.uniform(splits[4], (NCLASS,), jnp.float32, -1.0, 1.0), -1.0, 1.0),
        "balance_rates": jnp.clip(jax.random.uniform(splits[5], (NZONE,), jnp.float32, -0.3, 0.3), -0.3, 0.3),
    }


glen_factor = 0.5
diff_cap = 1.0
time_step = 0.2


def lookup(index, table):
    result = jnp.zeros(index.shape, jnp.float32)
    for entry in range(table.shape[0]):
        result = result + jnp.where(index == entry, table[entry], jnp.float32(0.0))
    return result


def restrict(field):
    row_count, col_count = field.shape
    return field.reshape(row_count // 2, 2, col_count // 2, 2).mean(axis=(1, 3))


def prolong(field):
    return jnp.repeat(jnp.repeat(field, 2, axis=0), 2, axis=1)


def flow_step(thick, ground, cover, supply, spacing, tau):
    surface = ground + thick
    slope_x = (surface[2:, 1:-1] - surface[:-2, 1:-1]) / (2.0 * spacing)
    slope_y = (surface[1:-1, 2:] - surface[1:-1, :-2]) / (2.0 * spacing)
    inner = thick[1:-1, 1:-1]
    fifth = inner * inner
    fifth = fifth * fifth * inner
    diffusion = jnp.minimum(glen_factor * fifth * (slope_x * slope_x + slope_y * slope_y), diff_cap)
    level = surface[1:-1, 1:-1]
    flux_x = 0.5 * (diffusion[1:, :] + diffusion[:-1, :]) * (level[1:, :] - level[:-1, :]) / spacing
    flux_y = 0.5 * (diffusion[:, 1:] + diffusion[:, :-1]) * (level[:, 1:] - level[:, :-1]) / spacing
    flux_x = flux_x[:, 1:-1]
    flux_y = flux_y[1:-1, :]
    spread = (flux_x[1:, :] - flux_x[:-1, :] + flux_y[:, 1:] - flux_y[:, :-1]) / spacing
    updated = thick[2:-2, 2:-2] + tau * (spread + supply[2:-2, 2:-2])
    return jnp.maximum(updated, 0.0) * cover[2:-2, 2:-2]


def run_global(field, ground, cover, supply, count, spacing, tau):
    padding = ((2, 2), (2, 2))
    ground_pad = jnp.pad(ground, padding)
    cover_pad = jnp.pad(cover, padding)
    supply_pad = jnp.pad(supply, padding)
    for sweep in range(count):
        field = flow_step(jnp.pad(field, padding), ground_pad, cover_pad, supply_pad, spacing, tau)
    return field


def reference(thickness, bed_class, ice_mask, zone_index, bed_levels, balance_rates):
    ground = lookup(bed_class, bed_levels)
    supply = lookup(zone_index, balance_rates)
    cover = ice_mask.astype(jnp.float32)
    coarse_ground = restrict(ground)
    coarse_cover = restrict(cover)
    coarse_supply = restrict(supply)
    coarse_tau = time_step * FSTEPS / CSTEPS
    fine_ends = []
    previous = []
    jumps = []
    for member in range(N_TM):
        fine_end = run_global(thickness[member], ground, cover, supply, FSTEPS, 1.0, time_step)
        earlier = run_global(restrict(thickness[member]), coarse_ground, coarse_cover, coarse_supply, CSTEPS, 2.0, coarse_tau)
        fine_ends.append(fine_end)
        previous.append(earlier)
        jumps.append(restrict(fine_end) - earlier)
    current = restrict(thickness[0])
    ends = []
    for member in range(N_TM):
        propagated = run_global(current, coarse_ground, coarse_cover, coarse_supply, CSTEPS, 2.0, coarse_tau)
        ends.append(fine_ends[member] + prolong(propagated - previous[member]))
        current = propagated + jumps[member]
    end_state = jnp.stack(ends)
    next_start = jnp.concatenate([thickness[:1], end_state[:-1]], axis=0)
    return end_state, next_start
```

```python
import jax
import jax.numpy as jnp
from jax import lax
from jax.experimental import pallas as pl
from jax.experimental.pallas import tpu as pltpu
from jax.sharding import PartitionSpec as P

ROWS = 32
CH = 16
CROWS = ROWS // 2
CCH = CH // 2
HALO = 8
WIN = ROWS + 2 * HALO
CHALO = 12
CWIN = CROWS + 2 * CHALO
F32 = jnp.float32
BF16 = jnp.bfloat16
VMEM_LIMIT = 40 * 1024 * 1024

FINE_GAIN, FINE_CAP = 0.5 / 4.0 * 0.1, 0.1
COARSE_GAIN, COARSE_CAP = 0.5 / 16.0 * 0.05, 0.05
FINE_TAU, COARSE_TAU = 0.2, 0.4


def column_masks(chunks):
    lane = lax.broadcasted_iota(jnp.int32, (chunks, 128), 1)
    sub = lax.broadcasted_iota(jnp.int32, (chunks, 128), 0)
    return (
        lane == 0,
        (lane == 0) & (sub == 0),
        lane == 127,
        (lane == 127) & (sub == chunks - 1),
    )


def from_left(x, masks, fill):
    a = pltpu.roll(x, 1, axis=2)
    b = pltpu.roll(a, 1, axis=1)
    return jnp.where(masks[1][None], fill, jnp.where(masks[0][None], b, a))


def from_right(x, masks, fill):
    chunks = x.shape[1]
    a = pltpu.roll(x, 127, axis=2)
    b = pltpu.roll(a, chunks - 1, axis=1)
    return jnp.where(masks[3][None], fill, jnp.where(masks[2][None], b, a))


def flow(h, s, d, dy, g, c, ta, lo, hi, masks, gain, cap, block, emit):
    for a in range(lo - 1, hi + 1, block):
        b = min(a + block, hi + 1)
        level = s[a:b]
        right = from_right(level, masks, 0.0)
        left = from_left(level, masks, 0.0)
        sx = s[a + 1 : b + 1] - s[a - 1 : b - 1]
        sy = right - left
        t = h[a:b]
        t2 = t * t
        fifth = t2 * t2 * t
        d[a:b] = jnp.minimum(fifth * gain * (sx * sx + sy * sy), cap)
        dy[a:b] = right - level
    for a in range(lo, hi, block):
        b = min(a + block, hi)
        dd = d[a - 1 : b + 1]
        ss = s[a - 1 : b + 1]
        fx = (dd[1:] + dd[:-1]) * (ss[1:] - ss[:-1])
        mid = dd[1:-1]
        fy = (mid + from_right(mid, masks, 0.0)) * dy[a:b]
        fy_left = from_left(fy, masks, mid * ss[1:-1])
        new = h[a:b] + (fx[1:] - fx[:-1] + fy - fy_left + ta[a:b])
        emit(a, b, jnp.maximum(new, 0.0) * c[a:b])


def split3(x):
    hi = x.astype(BF16)
    r = x - hi.astype(F32)
    mid = r.astype(BF16)
    lo = (r - mid.astype(F32)).astype(BF16)
    return hi, mid, lo


def times(x, m):
    parts = [jnp.dot(p, m, preferred_element_type=F32) for p in split3(x)]
    return parts[0] + (parts[1] + parts[2])


def restrict_mats():
    i = lax.broadcasted_iota(jnp.int32, (128, 128), 0)
    j = lax.broadcasted_iota(jnp.int32, (128, 128), 1)
    half = lax.shift_right_logical(i, 1)
    lo = jnp.where(j == half, 0.25, 0.0).astype(BF16)
    hi = jnp.where(j == half + 64, 0.25, 0.0).astype(BF16)
    return lo, hi


def prolong_mats():
    i = lax.broadcasted_iota(jnp.int32, (128, 128), 0)
    j = lax.broadcasted_iota(jnp.int32, (128, 128), 1)
    half = lax.shift_right_logical(j, 1)
    lo = jnp.where(i == half, 1.0, 0.0).astype(BF16)
    hi = jnp.where(i == half + 64, 1.0, 0.0).astype(BF16)
    return lo, hi


def restrict(x, pair, mats):
    n = x.shape[0] // 2
    y = x.reshape(n, 2, CH, 128)
    pair[0 : n * CH] = (y[:, 0] + y[:, 1]).reshape(n * CH, 128)
    even = pair[pl.ds(0, n * CCH, stride=2), :]
    odd = pair[pl.ds(1, n * CCH, stride=2), :]
    return (times(even, mats[0]) + times(odd, mats[1])).reshape(n, CCH, 128)


def look_up(index, table, size):
    values = [table[k] for k in range(size)]
    bit = 0
    while len(values) > 1:
        on = (lax.shift_right_logical(index, bit) & 1) == 1
        values = [jnp.where(on, values[k + 1], values[k]) for k in range(0, len(values), 2)]
        bit += 1
    return values[0]


def prepare_kernel(thick, bed, mask, zone, levels, rates, h, g, c, ta, up, dn, cg, cc, cta, cup, cdn, pair):
    for r in range(0, ROWS, 8):
        for k in range(CH):
            here = (slice(r, r + 8), slice(k * 128, k * 128 + 128))
            there = (pl.ds(r * CH + k, 8, stride=CH), slice(None))
            h[there] = thick[here]
            g[there] = look_up(bed[here], levels, 16)
            c[there] = mask[here].astype(F32)
            ta[there] = look_up(zone[here], rates, 8) * FINE_TAU
    at = 0
    for ref, count in ((h, 8), (g, 8), (c, 6), (ta, 6)):
        n = count * CH
        up[at : at + n] = ref[ROWS * CH - n : ROWS * CH]
        dn[at : at + n] = ref[0:n]
        at += n
    mats = restrict_mats()
    at = 0
    n = CHALO * CCH
    for ref, coarse, scale in ((g, cg, None), (c, cc, None), (ta, cta, COARSE_TAU / FINE_TAU)):
        value = restrict(ref[...].reshape(ROWS, CH, 128), pair, mats).reshape(CROWS * CCH, 128)
        if scale is not None:
            value = value * scale
        coarse[...] = value
        cup[at : at + n] = value[CROWS * CCH - n :]
        cdn[at : at + n] = value[0:n]
        at += n


def fine_kernel(place, h0, g0, c0, ta0, up, dn, cg0, cc0, cta0, end, prev, payload,
                h, s, s2, g, c, ta, d, dy, ch, cs, cs2, cg, cc, cta, pair):
    at = 0
    for ref, own, count in ((h, h0, 8), (g, g0, 8), (c, c0, 6), (ta, ta0, 6)):
        n = count * CH
        ref[HALO - count : HALO] = up[at : at + n].reshape(count, CH, 128)
        ref[HALO : HALO + ROWS] = own[...].reshape(ROWS, CH, 128)
        ref[HALO + ROWS : HALO + ROWS + count] = dn[at : at + n].reshape(count, CH, 128)
        at += n
    s[...] = g[...] + h[...]
    mats = restrict_mats()
    ch[...] = restrict(h[...], pair, mats)
    cg[0:4] = restrict(g[0:8], pair, mats)
    cg[4:20] = cg0[...].reshape(CROWS, CCH, 128)
    cg[20:24] = restrict(g[40:48], pair, mats)
    for ref, own, fine, scale in ((cc, cc0, c, None), (cta, cta0, ta, COARSE_TAU / FINE_TAU)):
        top = restrict(fine[4:8], pair, mats)
        bottom = restrict(fine[40:44], pair, mats)
        if scale is not None:
            top, bottom = top * scale, bottom * scale
        ref[2:4] = top
        ref[4:20] = own[...].reshape(CROWS, CCH, 128)
        ref[20:22] = bottom
    cs[...] = cg[...] + ch[...]
    cmasks = column_masks(CCH)

    def store_coarse(a, b, value):
        ch[a:b] = value
        cs2[a:b] = value + cg[a:b]

    def store_prev(a, b, value):
        prev[(a - 4) * CCH : (b - 4) * CCH] = value.reshape((b - a) * CCH, 128)

    cd, cdy = d.at[0:24, 0:CCH], dy.at[0:24, 0:CCH]
    flow(ch, cs, cd, cdy, cg, cc, cta, 2, 22, cmasks, COARSE_GAIN, COARSE_CAP, 8, store_coarse)
    flow(ch, cs2, cd, cdy, cg, cc, cta, 4, 20, cmasks, COARSE_GAIN, COARSE_CAP, 8, store_prev)

    masks = column_masks(CH)

    def store_in(target):
        def store(a, b, value):
            h[a:b] = value
            target[a:b] = value + g[a:b]

        return store

    def store_end(a, b, value):
        end[(a - HALO) * CH : (b - HALO) * CH] = value.reshape((b - a) * CH, 128)

    for k in range(4):
        edge = 2 * (k + 1)
        now, later = (s, s2) if k % 2 == 0 else (s2, s)
        flow(h, now, d, dy, g, c, ta, edge, WIN - edge, masks, FINE_GAIN, FINE_CAP, 4,
             store_in(later) if k < 3 else store_end)
    value = restrict(end[...].reshape(ROWS, CH, 128), pair, mats).reshape(CROWS * CCH, 128)
    first = place[0] == 0
    payload[...] = value - jnp.where(first, 0.0, prev[...])


def gather_kernel(place, d1, d2, d3, base, j1, j2, up, dn):
    m = place[0]
    base[...] = jnp.where(m == 1, d1[...], jnp.where(m == 2, d2[...], d3[...]))
    j1[...] = jnp.where(m == 2, d1[...], d2[...])
    j2[...] = d1[...]
    at = 0
    for ref, count in ((base, 12), (j1, 8), (j2, 4)):
        n = count * CCH
        up[at : at + n] = ref[CROWS * CCH - n :]
        dn[at : at + n] = ref[0:n]
        at += n


def chain_kernel(place, own, end, prev, before, base, j1, j2, up, dn, cg0, cc0, cta0, cup, cdn, out, nxt,
                 h, s, s2, g, c, ta, d, dy, jump1, jump2, fix, fixb, fine, pair):
    m = place[0]
    n = CHALO * CCH
    for at, ref, mid in ((0, g, cg0), (1, c, cc0), (2, ta, cta0)):
        ref[0:CHALO] = cup[at * n : at * n + n].reshape(CHALO, CCH, 128)
        ref[CHALO : CHALO + CROWS] = mid[...].reshape(CROWS, CCH, 128)
        ref[CHALO + CROWS : CWIN] = cdn[at * n : at * n + n].reshape(CHALO, CCH, 128)
    at = 0
    for ref, mid, count in ((h, base, 12), (jump1, j1, 8), (jump2, j2, 4)):
        k = count * CCH
        ref[CHALO - count : CHALO] = up[at : at + k].reshape(count, CCH, 128)
        ref[CHALO : CHALO + CROWS] = mid[...].reshape(CROWS, CCH, 128)
        ref[CHALO + CROWS : CHALO + CROWS + count] = dn[at : at + k].reshape(count, CCH, 128)
        at += k
    s[...] = g[...] + h[...]
    masks = column_masks(CCH)
    mats = restrict_mats()
    mine = slice(CHALO, CHALO + CROWS)
    last_prev = restrict(before[...].reshape(ROWS, CH, 128), pair, mats) - j2[...].reshape(CROWS, CCH, 128)
    fix[...] = jnp.zeros_like(fix)
    fixb[...] = jnp.zeros_like(fixb)

    def store_in(target):
        def store(a, b, value):
            h[a:b] = value
            target[a:b] = value + g[a:b]

        return store

    edge = 0
    for k, jump in ((1, jump1), (2, jump2), (3, None)):
        for now, later in ((s, s2), (s2, s)):
            edge += 2
            flow(h, now, d, dy, g, c, ta, edge, CWIN - edge, masks, COARSE_GAIN, COARSE_CAP, 8, store_in(later))

        @pl.when(m == k)
        def _():
            fix[...] = h[mine] - prev[...].reshape(CROWS, CCH, 128)

        if jump is not None:

            @pl.when(m == k + 1)
            def _():
                fixb[...] = h[mine] - last_prev

            for a in range(edge, CWIN - edge, 8):
                b = min(a + 8, CWIN - edge)
                store_in(s)(a, b, h[a:b] + jump[a:b])

    lo, hi = prolong_mats()
    for delta, field, target in ((fix, end, out), (fixb, before, nxt)):
        value = delta[...].reshape(CROWS * CCH, 128)
        pair[pl.ds(0, CROWS * CCH, stride=2), :] = times(value, lo)
        pair[pl.ds(1, CROWS * CCH, stride=2), :] = times(value, hi)
        wide = pair[0 : CROWS * CH].reshape(CROWS, 1, CH, 128)
        total = field[...].reshape(CROWS, 2, CH, 128) + wide
        fine[...] = total.reshape(ROWS * CH, 128)
        for r in range(0, ROWS, 8):
            for k in range(CH):
                target[r : r + 8, k * 128 : k * 128 + 128] = fine[pl.ds(r * CH + k, 8, stride=CH), :]

    @pl.when(m == 0)
    def _():
        nxt[...] = own[...]


def lines(n):
    return jax.ShapeDtypeStruct((n, 128), F32)


def call(kernel, ins, outs, scratch, name, smem=()):
    specs = [
        pl.BlockSpec(memory_space=pltpu.SMEM if i in smem else pltpu.VMEM) for i in range(len(ins))
    ]
    return pl.pallas_call(
        kernel,
        out_shape=outs,
        in_specs=specs,
        out_specs=[pl.BlockSpec(memory_space=pltpu.VMEM)] * len(outs),
        scratch_shapes=[pltpu.VMEM(shape, F32) for shape in scratch],
        compiler_params=pltpu.CompilerParams(vmem_limit_bytes=VMEM_LIMIT),
        name=name,
    )(*ins)


def shifted(x, axis, by):
    devices = lax.axis_size(axis)
    pairs = [(i, i + by) for i in range(devices) if 0 <= i + by < devices]
    return lax.ppermute(x, axis, pairs)


def per_device(thickness, bed_class, ice_mask, zone_index, bed_levels, balance_rates):
    own = thickness[0]
    place = lax.axis_index("tm").astype(jnp.int32).reshape(1)
    fine_lines, coarse_lines = ROWS * CH, CROWS * CCH
    edge_lines, cedge_lines = 28 * CH, 3 * CHALO * CCH
    h, g, c, ta, up, dn, cg, cc, cta, cup, cdn = call(
        prepare_kernel,
        (own, bed_class, ice_mask, zone_index, bed_levels, balance_rates),
        [lines(fine_lines)] * 4 + [lines(edge_lines)] * 2 + [lines(coarse_lines)] * 3 + [lines(cedge_lines)] * 2,
        [(ROWS * CH, 128)],
        "prepare",
        smem=(4, 5),
    )
    up, dn = shifted(up, "space", 1), shifted(dn, "space", -1)
    cup, cdn = shifted(cup, "space", 1), shifted(cdn, "space", -1)
    end, prev, payload = call(
        fine_kernel,
        (place, h, g, c, ta, up, dn, cg, cc, cta),
        [lines(fine_lines), lines(coarse_lines), lines(coarse_lines)],
        [(WIN, CH, 128)] * 8 + [(24, CCH, 128)] * 6 + [(ROWS * CH, 128)],
        "fine",
        smem=(0,),
    )
    d1, d2, d3 = (shifted(payload, "tm", k) for k in (1, 2, 3))
    before = shifted(end, "tm", 1)
    base, j1, j2, jup, jdn = call(
        gather_kernel,
        (place, d1, d2, d3),
        [lines(coarse_lines)] * 3 + [lines(24 * CCH)] * 2,
        [],
        "gather",
        smem=(0,),
    )
    jup, jdn = shifted(jup, "space", 1), shifted(jdn, "space", -1)
    out, nxt = call(
        chain_kernel,
        (place, own, end, prev, before, base, j1, j2, jup, jdn, cg, cc, cta, cup, cdn),
        [jax.ShapeDtypeStruct((ROWS, CH * 128), F32)] * 2,
        [(CWIN, CCH, 128)] * 10 + [(CROWS, CCH, 128)] * 2 + [(ROWS * CH, 128)] * 2,
        "chain",
        smem=(0,),
    )
    return out[None], nxt[None]


def solution(mesh):
    placed = (
        P("tm", "space", None),
        P("space", None),
        P("space", None),
        P("space", None),
        P(),
        P(),
    )
    return jax.shard_map(
        per_device,
        mesh=mesh,
        in_specs=placed,
        out_specs=(P("tm", "space", None), P("tm", "space", None)),
        check_vma=False,
    )
```

```python
import jax
import jax.numpy as jnp
from jax import lax
from jax.experimental import pallas as pl
from jax.experimental.pallas import tpu as pltpu
from jax.sharding import PartitionSpec as P

ROWS = 32
CH = 16
CROWS = ROWS // 2
CCH = CH // 2
HALO = 8
WIN = ROWS + 2 * HALO
RIM = 10
CHALO = 12
CWIN = CROWS + 2 * CHALO
F32 = jnp.float32
BF16 = jnp.bfloat16

FINE_GAIN, FINE_CAP = 0.5 / 4.0 * 0.1, 0.1
COARSE_GAIN, COARSE_CAP = 0.5 / 16.0 * 0.05, 0.05
FINE_TAU, COARSE_TAU = 0.2, 0.4


def column_masks(chunks):
    lane = lax.broadcasted_iota(jnp.int32, (chunks, 128), 1)
    sub = lax.broadcasted_iota(jnp.int32, (chunks, 128), 0)
    return (
        lane == 0,
        (lane == 0) & (sub == 0),
        lane == 127,
        (lane == 127) & (sub == chunks - 1),
    )


def from_left(x, masks, fill):
    a = pltpu.roll(x, 1, axis=2)
    b = pltpu.roll(a, 1, axis=1)
    return jnp.where(masks[1][None], fill, jnp.where(masks[0][None], b, a))


def from_right(x, masks, fill):
    chunks = x.shape[1]
    a = pltpu.roll(x, 127, axis=2)
    b = pltpu.roll(a, chunks - 1, axis=1)
    return jnp.where(masks[3][None], fill, jnp.where(masks[2][None], b, a))


def flow(h, s, g, c, ta, d, dy, lo, hi, masks, gain, cap, block, emit):
    for a in range(lo - 1, hi + 1, block):
        b = min(a + block, hi + 1)
        level = s[a:b]
        right = from_right(level, masks, 0.0)
        left = from_left(level, masks, 0.0)
        sx = s[a + 1 : b + 1] - s[a - 1 : b - 1]
        sy = right - left
        t = h[a:b]
        t2 = t * t
        fifth = t2 * t2 * t
        d[a:b] = jnp.minimum(fifth * gain * (sx * sx + sy * sy), cap)
        dy[a:b] = right - level
    for a in range(lo, hi, block):
        b = min(a + block, hi)
        dd = d[a - 1 : b + 1]
        ss = s[a - 1 : b + 1]
        fx = (dd[1:] + dd[:-1]) * (ss[1:] - ss[:-1])
        mid = dd[1:-1]
        fy = (mid + from_right(mid, masks, 0.0)) * dy[a:b]
        fy_left = from_left(fy, masks, mid * ss[1:-1])
        new = h[a:b] + (fx[1:] - fx[:-1] + fy - fy_left + ta[a:b])
        emit(a, b, jnp.maximum(new, 0.0) * c[a:b])


def split3(x):
    hi = x.astype(BF16)
    r = x - hi.astype(F32)
    mid = r.astype(BF16)
    lo = (r - mid.astype(F32)).astype(BF16)
    return hi, mid, lo


def times(x, m):
    parts = [jnp.dot(p, m, preferred_element_type=F32) for p in split3(x)]
    return parts[0] + (parts[1] + parts[2])


def restrict_mats():
    i = lax.broadcasted_iota(jnp.int32, (128, 128), 0)
    j = lax.broadcasted_iota(jnp.int32, (128, 128), 1)
    half = lax.shift_right_logical(i, 1)
    lo = jnp.where(j == half, 0.25, 0.0).astype(BF16)
    hi = jnp.where(j == half + 64, 0.25, 0.0).astype(BF16)
    return lo, hi


def prolong_mats():
    i = lax.broadcasted_iota(jnp.int32, (128, 128), 0)
    j = lax.broadcasted_iota(jnp.int32, (128, 128), 1)
    half = lax.shift_right_logical(j, 1)
    lo = jnp.where(i == half, 1.0, 0.0).astype(BF16)
    hi = jnp.where(i == half + 64, 1.0, 0.0).astype(BF16)
    return lo, hi


def restrict(x, pair, mats):
    n = x.shape[0] // 2
    y = x.reshape(n, 2, CH, 128)
    pair[0 : n * CH] = (y[:, 0] + y[:, 1]).reshape(n * CH, 128)
    even = pair[pl.ds(0, n * CCH, stride=2), :]
    odd = pair[pl.ds(1, n * CCH, stride=2), :]
    return (times(even, mats[0]) + times(odd, mats[1])).reshape(n, CCH, 128)


def look_up(index, table, size):
    values = [table[k] for k in range(size)]
    bit = 0
    while len(values) > 1:
        on = (lax.shift_right_logical(index, bit) & 1) == 1
        values = [jnp.where(on, values[k + 1], values[k]) for k in range(0, len(values), 2)]
        bit += 1
    return values[0]


EDGE = (8, 8, 6, 6)
EDGE_LINES = sum(EDGE) * CH
STATIC_LINES = 3 * CHALO * CCH
JUMPS = (12, 8, 4)
JUMP_LINES = sum(JUMPS) * CCH
H0, S0, G, C, TA = 0, 5, 9, 10, 11
CH0, CS0, CG, CC, CTA = 0, 2, 4, 5, 6


def fetch(pairs, sems):
    copies = [pltpu.make_async_copy(src, dst, sems.at[i]) for i, (src, dst) in enumerate(pairs)]
    for copy in copies:
        copy.start()
    return copies


def edge_kernel(space, thick, bed, mask, zone, levels, rates, off, inside,
                tv, bv, mv, zv, lev, rat, hx, gx, cx, tx, sems):
    pairs = [(levels, lev), (rates, rat)]
    for src, dst in ((bed, bv), (zone, zv), (thick, tv), (mask, mv)):
        pairs += [(src.at[0:8], dst.at[0:8]), (src.at[ROWS - 8 : ROWS], dst.at[8:16])]
    for copy in fetch(pairs, sems):
        copy.wait()
    for half in range(2):
        r = slice(half * 8, half * 8 + 8)
        for k in range(CH):
            cols = slice(k * 128, k * 128 + 128)
            there = (half, pl.ds(k, 8, stride=CH), slice(None))
            hx[there] = tv[r, cols]
            gx[there] = look_up(bv[r, cols], lev, 16)
            cx[there] = mv[r, cols].astype(F32)
            tx[there] = look_up(zv[r, cols], rat, 8) * FINE_TAU
    odd = space[0] & 1
    at = 0
    for ref, count in zip((hx, gx, cx, tx), EDGE):
        n = count * CH
        skip = (8 - count) * CH
        off[at : at + n] = ref[odd, pl.ds(odd * skip, n)]
        inside[at : at + n] = ref[1 - odd, pl.ds((1 - odd) * skip, n)]
        at += n


def inner_kernel(space, thick, bed, mask, zone, levels, rates, own, mid, rims, cstate, off, inside,
                 tv, bv, mv, zv, lev, rat, gl, cl, tl, state, d, dy, pair, sems):
    pairs = [(levels, lev), (rates, rat)]
    for r in range(0, ROWS, 8):
        for src, dst in ((bed, bv), (zone, zv), (thick, tv), (mask, mv)):
            pairs.append((src.at[r : r + 8], dst.at[r : r + 8]))
    copies = fetch(pairs, sems)
    copies[0].wait()
    copies[1].wait()
    for r in range(0, ROWS, 8):
        for copy in copies[2 + r // 2 : 6 + r // 2]:
            copy.wait()
        for k in range(CH):
            here = (slice(r, r + 8), slice(k * 128, k * 128 + 128))
            there = (pl.ds(r * CH + k, 8, stride=CH), slice(None))
            own[there] = tv[here]
            gl[there] = look_up(bv[here], lev, 16)
            cl[there] = mv[here].astype(F32)
            tl[there] = look_up(zv[here], rat, 8) * FINE_TAU
    mats = restrict_mats()
    mine = slice(HALO, HALO + ROWS)
    ratio = COARSE_TAU / FINE_TAU
    odd = space[0] & 1
    n = CHALO * CCH
    coarse = {}
    for ref, slot, cslot in ((own, H0, CH0), (gl, G, CG), (cl, C, CC), (tl, TA, CTA)):
        fine = ref[...].reshape(ROWS, CH, 128)
        state[slot, mine] = fine
        value = restrict(fine, pair, mats)
        coarse[cslot] = value * ratio if cslot == CTA else value
        cstate[cslot, 4:20] = coarse[cslot]
    cstate[CS0, 4:20] = coarse[CG] + coarse[CH0]
    state[S0, mine] = state[G, mine] + state[H0, mine]
    for at, cslot in enumerate((CG, CC, CTA)):
        off[at * n : at * n + n] = cstate[cslot, pl.ds(4 + odd * (CROWS - CHALO), CHALO)].reshape(n, 128)
        inside[at * n : at * n + n] = cstate[cslot, pl.ds(4 + (1 - odd) * (CROWS - CHALO), CHALO)].reshape(n, 128)
    coarse_steps(cstate, d, dy, ((6, 18), (8, 16)))
    fine_steps(state, d, dy, [(HALO + 2 * k, WIN - HALO - 2 * k) for k in (1, 2, 3, 4)])
    mid[...] = state[H0 + 4, 2 * HALO : WIN - 2 * HALO].reshape(16 * CH, 128)
    rims[:, 0:RIM] = state[:, HALO : HALO + RIM]
    rims[:, RIM:] = state[:, WIN - HALO - RIM : WIN - HALO]


def coarse_steps(cstate, d, dy, spans):
    masks = column_masks(CCH)
    cd, cdy = d.at[0:24, 0:CCH], dy.at[0:24, 0:CCH]
    for step, (lo, hi) in enumerate(spans):

        def emit(a, b, value, step=step):
            if step == 0:
                cstate[CH0 + 1, a:b] = value
                cstate[CS0 + 1, a:b] = value + cstate[CG, a:b]
            else:
                cstate[CH0, a:b] = value

        flow(cstate.at[CH0 + step], cstate.at[CS0 + step], cstate.at[CG], cstate.at[CC], cstate.at[CTA], cd, cdy,
             lo, hi, masks, COARSE_GAIN, COARSE_CAP, 8, emit)


def fine_steps(state, d, dy, spans):
    masks = column_masks(CH)
    for step, (lo, hi) in enumerate(spans):

        def emit(a, b, value, step=step):
            state[H0 + step + 1, a:b] = value
            if step < 3:
                state[S0 + step + 1, a:b] = value + state[G, a:b]

        flow(state.at[H0 + step], state.at[S0 + step], state.at[G], state.at[C], state.at[TA], d, dy,
             lo, hi, masks, FINE_GAIN, FINE_CAP, 4, emit)


def outer_kernel(place, space, last, off, inside, mid, rims, cstate_in, end, prev, payload, state, cstate, d, dy, pair):
    state[:, HALO : HALO + RIM] = rims[:, 0:RIM]
    state[:, WIN - HALO - RIM : WIN - HALO] = rims[:, RIM:]
    cstate[:, 4:20] = cstate_in[:, 4:20]
    odd = space[0] & 1
    at_border = (space[0] == 0) | (space[0] == last[0])
    at = 0
    for slot, count in zip((H0, G, C, TA), EDGE):
        n = count * CH
        far = jnp.where(at_border, 0.0, off[at : at + n]).reshape(count, CH, 128)
        near = inside[at : at + n].reshape(count, CH, 128)
        state[slot, HALO - count : HALO] = jnp.where(odd == 1, near, far)
        state[slot, HALO + ROWS : HALO + ROWS + count] = jnp.where(odd == 1, far, near)
        at += n
    mats = restrict_mats()
    ratio = COARSE_TAU / FINE_TAU
    for lo, clo in ((0, 0), (40, 20)):
        state[S0, lo : lo + 8] = state[G, lo : lo + 8] + state[H0, lo : lo + 8]
        ground = restrict(state[G, lo : lo + 8], pair, mats)
        thick = restrict(state[H0, lo : lo + 8], pair, mats)
        cstate[CG, clo : clo + 4] = ground
        cstate[CH0, clo : clo + 4] = thick
        cstate[CS0, clo : clo + 4] = ground + thick
    for lo, clo in ((4, 2), (40, 20)):
        cstate[CC, clo : clo + 2] = restrict(state[C, lo : lo + 4], pair, mats)
        cstate[CTA, clo : clo + 2] = restrict(state[TA, lo : lo + 4], pair, mats) * ratio
    coarse_steps(cstate, d, dy, ((2, 6), (4, 8)))
    coarse_steps(cstate, d, dy, ((18, 22), (16, 20)))
    prev[...] = cstate[CH0, 4:20].reshape(CROWS * CCH, 128)
    fine_steps(state, d, dy, [(2 * k, HALO + 2 * k) for k in (1, 2, 3, 4)])
    fine_steps(state, d, dy, [(WIN - HALO - 2 * k, WIN - 2 * k) for k in (1, 2, 3, 4)])
    end[0 : 8 * CH] = state[H0 + 4, 8:16].reshape(8 * CH, 128)
    end[8 * CH : 24 * CH] = mid[...]
    end[24 * CH : 32 * CH] = state[H0 + 4, 32:40].reshape(8 * CH, 128)
    value = restrict(end[...].reshape(ROWS, CH, 128), pair, mats).reshape(CROWS * CCH, 128)
    payload[...] = value - jnp.where(place[0] == 0, 0.0, prev[...])


def gather_kernel(place, space, d1, d2, d3, base, j1, j2, off, inside):
    m = place[0]
    base[...] = jnp.where(m == 1, d1[...], jnp.where(m == 2, d2[...], d3[...]))
    j1[...] = jnp.where(m == 2, d1[...], d2[...])
    j2[...] = d1[...]
    odd = space[0] & 1
    at = 0
    for ref, count in zip((base, j1, j2), JUMPS):
        n = count * CCH
        skip = CROWS * CCH - n
        off[at : at + n] = ref[pl.ds(odd * skip, n)]
        inside[at : at + n] = ref[pl.ds((1 - odd) * skip, n)]
        at += n


def chain_kernel(place, space, last, own, cstate, end, prev, before, base, j1, j2, off, inside, soff, sinside,
                 out_hbm, nxt_hbm, h, s, s2, g, c, ta, d, dy, jump1, jump2, fix, now_m, fine, pair, out, nxt, sems):
    m = place[0]
    odd = space[0] & 1
    at_border = (space[0] == 0) | (space[0] == last[0])
    bottom = CHALO + CROWS

    def window(ref, own, count, far_ref, near_ref, at):
        n = count * CCH
        far = jnp.where(at_border, 0.0, far_ref[at : at + n]).reshape(count, CCH, 128)
        near = near_ref[at : at + n].reshape(count, CCH, 128)
        ref[CHALO - count : CHALO] = jnp.where(odd == 1, near, far)
        ref[CHALO:bottom] = own
        ref[bottom : bottom + count] = jnp.where(odd == 1, far, near)
        return at + n

    at = 0
    for ref, slot in ((g, CG), (c, CC), (ta, CTA)):
        at = window(ref, cstate[slot, 4:20], CHALO, soff, sinside, at)
    at = 0
    for ref, held, count in zip((h, jump1, jump2), (base, j1, j2), JUMPS):
        at = window(ref, held[...].reshape(CROWS, CCH, 128), count, off, inside, at)
    s[...] = g[...] + h[...]
    masks = column_masks(CCH)
    mats = restrict_mats()
    mine = slice(CHALO, bottom)
    fix[...] = jnp.zeros_like(fix)
    now_m[...] = h[mine]
    lo_mat, hi_mat = prolong_mats()

    def spread_out(value, field, target, target_hbm, first, keep=None):
        value = value.reshape(CROWS * CCH, 128)
        pair[pl.ds(0, CROWS * CCH, stride=2), :] = times(value, lo_mat)
        pair[pl.ds(1, CROWS * CCH, stride=2), :] = times(value, hi_mat)
        wide = pair[0 : CROWS * CH].reshape(CROWS, 1, CH, 128)
        total = (field[...].reshape(CROWS, 2, CH, 128) + wide).reshape(ROWS, CH, 128)
        if keep is not None:
            total = jnp.where(m == 0, keep, total)
        fine[...] = total.reshape(ROWS * CH, 128)
        copies = []
        for r in range(0, ROWS, 8):
            for k in range(CH):
                target[r : r + 8, k * 128 : k * 128 + 128] = fine[pl.ds(r * CH + k, 8, stride=CH), :]
            copy = pltpu.make_async_copy(target.at[r : r + 8], target_hbm.at[r : r + 8], sems.at[first + r // 8])
            copy.start()
            copies.append(copy)
        return copies

    edge = 0
    waits = []
    for k, jump in ((1, jump1), (2, jump2), (3, None)):
        if k == 3:
            coarse_before = restrict(before[...].reshape(ROWS, CH, 128), pair, mats)
            waits += spread_out(now_m[...] - coarse_before, before, nxt, nxt_hbm, 0,
                                own[...].reshape(ROWS, CH, 128))
        for now, later in ((s, s2), (s2, s)):
            edge += 2

            def emit(a, b, value, later=later):
                h[a:b] = value
                later[a:b] = value + g[a:b]

            flow(h, now, g, c, ta, d, dy, edge, CWIN - edge, masks, COARSE_GAIN, COARSE_CAP, 8, emit)

        @pl.when(m == k)
        def _():
            fix[...] = h[mine] - prev[...].reshape(CROWS, CCH, 128)

        if jump is not None:
            for a in range(edge, CWIN - edge, 8):
                b = min(a + 8, CWIN - edge)
                emit_value = h[a:b] + jump[a:b]
                h[a:b] = emit_value
                s[a:b] = emit_value + g[a:b]

            @pl.when(m == k + 1)
            def _():
                now_m[...] = h[mine]

    waits += spread_out(fix[...], end, out, out_hbm, 4)
    for copy in waits:
        copy.wait()


def lines(n):
    return jax.ShapeDtypeStruct((n, 128), F32)


VMEM, SMEM, HBM = pltpu.VMEM, pltpu.SMEM, pltpu.HBM


def call(kernel, name, ins, outs, scratch=(), in_spaces=None, out_space=VMEM, limit=16):
    spaces = {"s": SMEM, "h": HBM, "v": VMEM}
    return pl.pallas_call(
        kernel,
        out_shape=outs,
        in_specs=[pl.BlockSpec(memory_space=spaces[letter]) for letter in in_spaces],
        out_specs=[pl.BlockSpec(memory_space=out_space)] * len(outs),
        scratch_shapes=[pltpu.VMEM(item, F32) if isinstance(item, tuple) else item for item in scratch],
        compiler_params=pltpu.CompilerParams(vmem_limit_bytes=limit * 2**20),
        name=name,
    )(*ins)


def shifted(x, by):
    devices = lax.axis_size("tm")
    return lax.ppermute(x, "tm", [(i, (i + by) % devices) for i in range(devices)])


def swapped(off, inside):
    devices = lax.axis_size("space")
    far = [(i, (i + 1) % devices) for i in range(1, devices, 2)]
    near = [(i, i + 1) for i in range(0, devices, 2)]
    both = [pairs + [(j, i) for i, j in pairs] for pairs in (far, near)]
    return lax.ppermute(off, "space", both[0]), lax.ppermute(inside, "space", both[1])


def per_device(thickness, bed_class, ice_mask, zone_index, bed_levels, balance_rates):
    place = lax.axis_index("tm").astype(jnp.int32).reshape(1)
    space = lax.axis_index("space").astype(jnp.int32).reshape(1)
    last = jnp.full((1,), lax.axis_size("space") - 1, jnp.int32)
    raw = (space, thickness[0], bed_class, ice_mask, zone_index, bed_levels, balance_rates)
    coarse_lines = CROWS * CCH
    tables = [pltpu.SMEM((16,), F32), pltpu.SMEM((8,), F32)]
    maps = [pltpu.VMEM((16, 2048), t) for t in (F32, jnp.int32, jnp.int32, jnp.int32)]
    whole = [pltpu.VMEM((ROWS, 2048), t) for t in (F32, jnp.int32, jnp.int32, jnp.int32)]
    off, inside = call(
        edge_kernel, "edges", raw, [lines(EDGE_LINES)] * 2,
        maps + tables + [(2, 8 * CH, 128)] * 4 + [pltpu.SemaphoreType.DMA((10,))],
        "shhhhhh", limit=54,
    )
    off, inside = swapped(off, inside)
    own, mid, rims, cstate, soff, sinside = call(
        inner_kernel, "inner", raw,
        [lines(ROWS * CH), lines(16 * CH), jax.ShapeDtypeStruct((12, 2 * RIM, CH, 128), F32)]
        + [jax.ShapeDtypeStruct((7, 24, CCH, 128), F32)] + [lines(STATIC_LINES)] * 2,
        whole + tables + [(ROWS * CH, 128)] * 3 + [(12, WIN, CH, 128)] + [(WIN, CH, 128)] * 2 + [(ROWS * CH, 128), pltpu.SemaphoreType.DMA((18,))],
        "shhhhhh",
    )
    end, prev, payload = call(
        outer_kernel, "outer", (place, space, last, off, inside, mid, rims, cstate),
        [lines(ROWS * CH)] + [lines(coarse_lines)] * 2,
        [(12, WIN, CH, 128), (7, 24, CCH, 128)] + [(WIN, CH, 128)] * 2 + [(ROWS * CH, 128)],
        "sssvvvvv",
    )
    d1, d2, d3 = (shifted(payload, k) for k in (1, 2, 3))
    base, j1, j2, off, inside = call(
        gather_kernel, "gather", (place, space, d1, d2, d3),
        [lines(coarse_lines)] * 3 + [lines(JUMP_LINES)] * 2, (), "ssvvv",
    )
    before = shifted(lax.optimization_barrier((end, d1, d2, d3))[0], 1)
    soff, sinside = swapped(soff, sinside)
    off, inside = swapped(off, inside)
    out, nxt = call(
        chain_kernel, "chain",
        (place, space, last, own, cstate, end, prev, before, base, j1, j2, off, inside, soff, sinside),
        [jax.ShapeDtypeStruct((ROWS, CH * 128), F32)] * 2,
        [(CWIN, CCH, 128)] * 10 + [(CROWS, CCH, 128)] * 2 + [(ROWS * CH, 128)] * 2
        + [(ROWS, CH * 128)] * 2 + [pltpu.SemaphoreType.DMA((8,))],
        "sss" + "v" * 12, out_space=HBM,
    )
    return out[None], nxt[None]


def solution(mesh):
    placed = (
        P("tm", "space", None),
        P("space", None),
        P("space", None),
        P("space", None),
        P(),
        P(),
    )
    return jax.shard_map(
        per_device,
        mesh=mesh,
        in_specs=placed,
        out_specs=(P("tm", "space", None), P("tm", "space", None)),
        check_vma=False,
    )
```

```python
import jax
import jax.numpy as jnp
from jax import lax
from jax.experimental import pallas as pl
from jax.experimental.pallas import tpu as pltpu
from jax.sharding import PartitionSpec as P

ROWS = 32
CH = 16
CROWS = ROWS // 2
CCH = CH // 2
HALO = 8
WIN = ROWS + 2 * HALO
RIM = 10
CHALO = 12
CWIN = CROWS + 2 * CHALO
F32 = jnp.float32
BF16 = jnp.bfloat16

FINE_GAIN, FINE_CAP = 0.5 / 4.0 * 0.1, 0.1
COARSE_GAIN, COARSE_CAP = 0.5 / 16.0 * 0.05, 0.05
FINE_TAU, COARSE_TAU = 0.2, 0.4


def column_masks(chunks):
    lane = lax.broadcasted_iota(jnp.int32, (8, 128), 1)
    sub = lax.broadcasted_iota(jnp.int32, (8, 128), 0)
    left, right = lane == 0, lane == 127
    return chunks, left, left & (sub == 0), right, right & (sub == 7)


def line_of(k):
    return (k % 2) * 8 + k // 2


def from_left(x, masks, fill):
    chunks, edge, border, _, _ = masks
    a = pltpu.roll(x, 1, axis=2)
    if chunks == CCH:
        return jnp.where(border[None], fill, jnp.where(edge[None], pltpu.roll(a, 1, axis=1), a))
    even, odd = a[:, :8], a[:, 8:]
    if not isinstance(fill, float):
        fill = fill[:, :8]
    first = jnp.where(border[None], fill, jnp.where(edge[None], pltpu.roll(odd, 1, axis=1), even))
    return jnp.concatenate([first, jnp.where(edge[None], even, odd)], axis=1)


def from_right(x, masks, fill):
    chunks, _, _, edge, border = masks
    a = pltpu.roll(x, 127, axis=2)
    if chunks == CCH:
        return jnp.where(border[None], fill, jnp.where(edge[None], pltpu.roll(a, 7, axis=1), a))
    even, odd = a[:, :8], a[:, 8:]
    second = jnp.where(border[None], fill, jnp.where(edge[None], pltpu.roll(even, 7, axis=1), odd))
    return jnp.concatenate([jnp.where(edge[None], odd, even), second], axis=1)


def flow(h, s, g, c, ta, d, dy, lo, hi, masks, gain, cap, block, emit):
    for a in range(lo - 1, hi + 1, block):
        b = min(a + block, hi + 1)
        level = s[a:b]
        right = from_right(level, masks, 0.0)
        left = from_left(level, masks, 0.0)
        sx = s[a + 1 : b + 1] - s[a - 1 : b - 1]
        sy = right - left
        t = h[a:b]
        t2 = t * t
        fifth = t2 * t2 * t
        d[a:b] = jnp.minimum(fifth * gain * (sx * sx + sy * sy), cap)
        dy[a:b] = right - level
    for a in range(lo, hi, block):
        b = min(a + block, hi)
        dd = d[a - 1 : b + 1]
        ss = s[a - 1 : b + 1]
        fx = (dd[1:] + dd[:-1]) * (ss[1:] - ss[:-1])
        mid = dd[1:-1]
        fy = (mid + from_right(mid, masks, 0.0)) * dy[a:b]
        fy_left = from_left(fy, masks, mid * ss[1:-1])
        new = h[a:b] + (fx[1:] - fx[:-1] + fy - fy_left + ta[a:b])
        emit(a, b, jnp.maximum(new, 0.0) * c[a:b])


def split3(x):
    hi = x.astype(BF16)
    r = x - hi.astype(F32)
    mid = r.astype(BF16)
    lo = (r - mid.astype(F32)).astype(BF16)
    return hi, mid, lo


def times(x, m):
    parts = [jnp.dot(p, m, preferred_element_type=F32) for p in split3(x)]
    return parts[0] + (parts[1] + parts[2])


def restrict_mats():
    i = lax.broadcasted_iota(jnp.int32, (128, 128), 0)
    j = lax.broadcasted_iota(jnp.int32, (128, 128), 1)
    half = lax.shift_right_logical(i, 1)
    lo = jnp.where(j == half, 0.25, 0.0).astype(BF16)
    hi = jnp.where(j == half + 64, 0.25, 0.0).astype(BF16)
    return lo, hi


def prolong_mats():
    i = lax.broadcasted_iota(jnp.int32, (128, 128), 0)
    j = lax.broadcasted_iota(jnp.int32, (128, 128), 1)
    half = lax.shift_right_logical(j, 1)
    lo = jnp.where(i == half, 1.0, 0.0).astype(BF16)
    hi = jnp.where(i == half + 64, 1.0, 0.0).astype(BF16)
    return lo, hi


def restrict(x, mats):
    n = x.shape[0] // 2
    y = x.reshape(n, 2, CH, 128)
    y = y[:, 0] + y[:, 1]
    even, odd = y[:, :8].reshape(n * CCH, 128), y[:, 8:].reshape(n * CCH, 128)
    return (times(even, mats[0]) + times(odd, mats[1])).reshape(n, CCH, 128)


def look_up(index, table, size):
    values = [table[k] for k in range(size)]
    bit = 0
    while len(values) > 1:
        on = (lax.shift_right_logical(index, bit) & 1) == 1
        values = [jnp.where(on, values[k + 1], values[k]) for k in range(0, len(values), 2)]
        bit += 1
    return values[0]


EDGE = (8, 8, 6, 6)
EDGE_LINES = sum(EDGE) * CH
STATIC_LINES = 3 * CHALO * CCH
JUMPS = (12, 8, 4)
JUMP_LINES = sum(JUMPS) * CCH
H0, S0, G, C, TA = 0, 5, 9, 10, 11
KEPT = (0, 1, 2, 3, 4, 9, 10, 11)
CH0, CS0, CG, CC, CTA = 0, 2, 4, 5, 6


def fetch(pairs, sems):
    copies = [pltpu.make_async_copy(src, dst, sems.at[i]) for i, (src, dst) in enumerate(pairs)]
    for copy in copies:
        copy.start()
    return copies


def edge_kernel(space, thick, bed, mask, zone, levels, rates, off, inside, tv, bv, mv, zv, tab,
                lev, rat, hx, gx, cx, tx, sems):
    pairs = [(levels, lev), (rates, rat)]
    maps = ((bed, bv), (zone, zv), (thick, tv), (mask, mv))
    for r, count in ((0, 8), (ROWS - 8, 8), (8, ROWS - 16)):
        pairs += [(src.at[r : r + count], dst.at[r : r + count]) for src, dst in maps]
    copies = fetch(pairs, sems)
    for copy in copies[:10]:
        copy.wait()
    for k in range(16):
        tab[k : k + 1] = jnp.full((1, 128), lev[k], F32)
    for k in range(8):
        tab[16 + k : 17 + k] = jnp.full((1, 128), rat[k], F32)
    for half in range(2):
        r = slice(half * (ROWS - 8), half * (ROWS - 8) + 8)
        for k in range(CH):
            cols = slice(k * 128, k * 128 + 128)
            there = (half, pl.ds(line_of(k), 8, stride=CH), slice(None))
            hx[there] = tv[r, cols]
            gx[there] = look_up(bv[r, cols], lev, 16)
            cx[there] = mv[r, cols].astype(F32)
            tx[there] = look_up(zv[r, cols], rat, 8) * FINE_TAU
    odd = space[0] & 1
    at = 0
    for ref, count in zip((hx, gx, cx, tx), EDGE):
        n = count * CH
        skip = (8 - count) * CH
        off[at : at + n] = ref[odd, pl.ds(odd * skip, n)]
        inside[at : at + n] = ref[1 - odd, pl.ds((1 - odd) * skip, n)]
        at += n
    for copy in copies[10:]:
        copy.wait()


def inner_kernel(space, tv, bv, mv, zv, tab, own, mid, rims, cstate, off, gl, cl, tl, state, d, dy):
    table = [jnp.broadcast_to(tab[k : k + 1], (8, 128)) for k in range(24)]
    lev, rat = table[:16], table[16:]
    for r in range(0, ROWS, 8):
        for k in range(CH):
            here = (slice(r, r + 8), slice(k * 128, k * 128 + 128))
            there = (pl.ds(r * CH + line_of(k), 8, stride=CH), slice(None))
            own[there] = tv[here]
            gl[there] = look_up(bv[here], lev, 16)
            cl[there] = mv[here].astype(F32)
            tl[there] = look_up(zv[here], rat, 8) * FINE_TAU
    mats = restrict_mats()
    mine = slice(HALO, HALO + ROWS)
    ratio = COARSE_TAU / FINE_TAU
    odd = space[0] & 1
    n = CHALO * CCH
    coarse = {}
    for ref, slot, cslot in ((own, H0, CH0), (gl, G, CG), (cl, C, CC), (tl, TA, CTA)):
        fine = ref[...].reshape(ROWS, CH, 128)
        state[slot, mine] = fine
        value = restrict(fine, mats)
        coarse[cslot] = value * ratio if cslot == CTA else value
        cstate[cslot, 4:20] = coarse[cslot]
    cstate[CS0, 4:20] = coarse[CG] + coarse[CH0]
    state[S0, mine] = state[G, mine] + state[H0, mine]
    for at, cslot in enumerate((CG, CC, CTA)):
        off[at * n : at * n + n] = cstate[cslot, pl.ds(4 + odd * (CROWS - CHALO), CHALO)].reshape(n, 128)
    coarse_steps(cstate, d, dy, ((6, 18), (8, 16)))
    fine_steps(state, d, dy, [(HALO + 2 * k, WIN - HALO - 2 * k) for k in (1, 2, 3, 4)])
    mid[...] = state[H0 + 4, 2 * HALO : WIN - 2 * HALO].reshape(16 * CH, 128)
    for at, slot in enumerate(KEPT):
        rims[at, 0:RIM] = state[slot, HALO : HALO + RIM]
        rims[at, RIM:] = state[slot, WIN - HALO - RIM : WIN - HALO]


def coarse_steps(cstate, d, dy, spans):
    masks = column_masks(CCH)
    cd, cdy = d.at[0:24, 0:CCH], dy.at[0:24, 0:CCH]
    for step, (lo, hi) in enumerate(spans):

        def emit(a, b, value, step=step):
            if step == 0:
                cstate[CH0 + 1, a:b] = value
                cstate[CS0 + 1, a:b] = value + cstate[CG, a:b]
            else:
                cstate[CH0, a:b] = value

        flow(cstate.at[CH0 + step], cstate.at[CS0 + step], cstate.at[CG], cstate.at[CC], cstate.at[CTA], cd, cdy,
             lo, hi, masks, COARSE_GAIN, COARSE_CAP, 8, emit)


def fine_steps(state, d, dy, spans):
    masks = column_masks(CH)
    for step, (lo, hi) in enumerate(spans):

        def emit(a, b, value, step=step):
            state[H0 + step + 1, a:b] = value
            if step < 3:
                state[S0 + step + 1, a:b] = value + state[G, a:b]

        flow(state.at[H0 + step], state.at[S0 + step], state.at[G], state.at[C], state.at[TA], d, dy,
             lo, hi, masks, FINE_GAIN, FINE_CAP, 4, emit)


def outer_kernel(place, space, last, off, inside, mid, rims, cstate_in, end, prev, payload, state, cstate, d, dy):
    for at, slot in enumerate(KEPT):
        state[slot, HALO : HALO + RIM] = rims[at, 0:RIM]
        state[slot, WIN - HALO - RIM : WIN - HALO] = rims[at, RIM:]
    for rim in (slice(HALO, HALO + RIM), slice(WIN - HALO - RIM, WIN - HALO)):
        for step in range(4):
            state[S0 + step, rim] = state[H0 + step, rim] + state[G, rim]
    cstate[:, 4:20] = cstate_in[:, 4:20]
    odd = space[0] & 1
    at_border = (space[0] == 0) | (space[0] == last[0])
    at = 0
    for slot, count in zip((H0, G, C, TA), EDGE):
        n = count * CH
        far = jnp.where(at_border, 0.0, off[at : at + n]).reshape(count, CH, 128)
        near = inside[at : at + n].reshape(count, CH, 128)
        state[slot, HALO - count : HALO] = jnp.where(odd == 1, near, far)
        state[slot, HALO + ROWS : HALO + ROWS + count] = jnp.where(odd == 1, far, near)
        at += n
    mats = restrict_mats()
    ratio = COARSE_TAU / FINE_TAU
    for lo, clo in ((0, 0), (40, 20)):
        state[S0, lo : lo + 8] = state[G, lo : lo + 8] + state[H0, lo : lo + 8]
        ground = restrict(state[G, lo : lo + 8], mats)
        thick = restrict(state[H0, lo : lo + 8], mats)
        cstate[CG, clo : clo + 4] = ground
        cstate[CH0, clo : clo + 4] = thick
        cstate[CS0, clo : clo + 4] = ground + thick
    for lo, clo in ((4, 2), (40, 20)):
        cstate[CC, clo : clo + 2] = restrict(state[C, lo : lo + 4], mats)
        cstate[CTA, clo : clo + 2] = restrict(state[TA, lo : lo + 4], mats) * ratio
    coarse_steps(cstate, d, dy, ((2, 6), (4, 8)))
    coarse_steps(cstate, d, dy, ((18, 22), (16, 20)))
    prev[...] = cstate[CH0, 4:20].reshape(CROWS * CCH, 128)
    fine_steps(state, d, dy, [(2 * k, HALO + 2 * k) for k in (1, 2, 3, 4)])
    fine_steps(state, d, dy, [(WIN - HALO - 2 * k, WIN - 2 * k) for k in (1, 2, 3, 4)])
    end[0 : 8 * CH] = state[H0 + 4, 8:16].reshape(8 * CH, 128)
    end[8 * CH : 24 * CH] = mid[...]
    end[24 * CH : 32 * CH] = state[H0 + 4, 32:40].reshape(8 * CH, 128)
    value = restrict(end[...].reshape(ROWS, CH, 128), mats).reshape(CROWS * CCH, 128)
    payload[...] = value - jnp.where(place[0] == 0, 0.0, prev[...])


def pack_kernel(source, target):
    target[...] = source[...]


def gather_kernel(place, space, cstate, d1, d2, d3, base, j1, j2, off, inside):
    m = place[0]
    base[...] = jnp.where(m == 1, d1[...], jnp.where(m == 2, d2[...], d3[...]))
    j1[...] = jnp.where(m == 2, d1[...], d2[...])
    j2[...] = d1[...]
    odd = space[0] & 1
    at = 0
    for ref, count in zip((base, j1, j2), JUMPS):
        n = count * CCH
        skip = CROWS * CCH - n
        off[at : at + n] = ref[pl.ds(odd * skip, n)]
        inside[at : at + n] = ref[pl.ds((1 - odd) * skip, n)]
        at += n
    n = CHALO * CCH
    for cslot in (CG, CC, CTA):
        inside[at : at + n] = cstate[cslot, pl.ds(4 + (1 - odd) * (CROWS - CHALO), CHALO)].reshape(n, 128)
        at += n


def chain_kernel(place, space, last, own, cstate, end, prev, before, base, j1, j2, off, inside, soff,
                 out_hbm, nxt_hbm, h, s, s2, g, c, ta, d, dy, jump1, jump2, fix, now_m, fine, out, nxt, sems):
    m = place[0]
    odd = space[0] & 1
    at_border = (space[0] == 0) | (space[0] == last[0])
    bottom = CHALO + CROWS

    def window(ref, own, count, far_ref, at, skip):
        n = count * CCH
        far = jnp.where(at_border, 0.0, far_ref[at : at + n]).reshape(count, CCH, 128)
        near = inside[skip + at : skip + at + n].reshape(count, CCH, 128)
        ref[CHALO - count : CHALO] = jnp.where(odd == 1, near, far)
        ref[CHALO:bottom] = own
        ref[bottom : bottom + count] = jnp.where(odd == 1, far, near)
        return at + n

    at = 0
    for ref, slot in ((g, CG), (c, CC), (ta, CTA)):
        at = window(ref, cstate[slot, 4:20], CHALO, soff, at, JUMP_LINES)
    at = 0
    for ref, held, count in zip((h, jump1, jump2), (base, j1, j2), JUMPS):
        at = window(ref, held[...].reshape(CROWS, CCH, 128), count, off, at, 0)
    s[...] = g[...] + h[...]
    masks = column_masks(CCH)
    mats = restrict_mats()
    mine = slice(CHALO, bottom)
    fix[...] = jnp.zeros_like(fix)
    now_m[...] = h[mine]
    lo_mat, hi_mat = prolong_mats()

    def spread_out(value, field, target, target_hbm, first, keep=None):
        value = value.reshape(CROWS * CCH, 128)
        halves = [times(value, mat).reshape(CROWS, CCH, 128) for mat in (lo_mat, hi_mat)]
        wide = jnp.concatenate(halves, axis=1).reshape(CROWS, 1, CH, 128)
        total = (field[...].reshape(CROWS, 2, CH, 128) + wide).reshape(ROWS, CH, 128)
        if keep is not None:
            total = jnp.where(m == 0, keep, total)
        fine[...] = total.reshape(ROWS * CH, 128)
        copies = []
        for r in range(0, ROWS, 8):
            for k in range(CH):
                target[r : r + 8, k * 128 : k * 128 + 128] = fine[pl.ds(r * CH + line_of(k), 8, stride=CH), :]
            copy = pltpu.make_async_copy(target.at[r : r + 8], target_hbm.at[r : r + 8], sems.at[first + r // 8])
            copy.start()
            copies.append(copy)
        return copies

    edge = 0
    waits = []
    for k, jump in ((1, jump1), (2, jump2), (3, None)):
        if k == 3:
            coarse_before = restrict(before[...].reshape(ROWS, CH, 128), mats)
            waits += spread_out(now_m[...] - coarse_before, before, nxt, nxt_hbm, 0,
                                own[...].reshape(ROWS, CH, 128))
        for now, later in ((s, s2), (s2, s)):
            edge += 2

            def emit(a, b, value, later=later):
                h[a:b] = value
                later[a:b] = value + g[a:b]

            flow(h, now, g, c, ta, d, dy, edge, CWIN - edge, masks, COARSE_GAIN, COARSE_CAP, 8, emit)

        @pl.when(m == k)
        def _():
            fix[...] = h[mine] - prev[...].reshape(CROWS, CCH, 128)

        if jump is not None:
            for a in range(edge, CWIN - edge, 8):
                b = min(a + 8, CWIN - edge)
                emit_value = h[a:b] + jump[a:b]
                h[a:b] = emit_value
                s[a:b] = emit_value + g[a:b]

            @pl.when(m == k + 1)
            def _():
                now_m[...] = h[mine]

    waits += spread_out(fix[...], end, out, out_hbm, 4)
    for copy in waits:
        copy.wait()


def lines(n):
    return jax.ShapeDtypeStruct((n, 128), F32)


VMEM, SMEM, HBM = pltpu.VMEM, pltpu.SMEM, pltpu.HBM


def call(kernel, name, ins, outs, scratch=(), in_spaces=None, out_space=VMEM, limit=16):
    spaces = {"s": SMEM, "h": HBM, "v": VMEM}
    return pl.pallas_call(
        kernel,
        out_shape=outs,
        in_specs=[pl.BlockSpec(memory_space=spaces[letter]) for letter in in_spaces],
        out_specs=[pl.BlockSpec(memory_space=out_space)] * len(outs),
        scratch_shapes=[pltpu.VMEM(item, F32) if isinstance(item, tuple) else item for item in scratch],
        compiler_params=pltpu.CompilerParams(vmem_limit_bytes=limit * 2**20),
        name=name,
    )(*ins)


def shifted(x, by):
    devices = lax.axis_size("tm")
    return lax.ppermute(x, "tm", [(i, (i + by) % devices) for i in range(devices)])


def far_swap(x):
    devices = lax.axis_size("space")
    pairs = [(i, (i + 1) % devices) for i in range(1, devices, 2)]
    return lax.ppermute(x, "space", pairs + [(j, i) for i, j in pairs])


def near_swap(x):
    devices = lax.axis_size("space")
    return lax.ppermute(x, "space", [(i, i ^ 1) for i in range(devices)])


def per_device(thickness, bed_class, ice_mask, zone_index, bed_levels, balance_rates):
    place = lax.axis_index("tm").astype(jnp.int32).reshape(1)
    space = lax.axis_index("space").astype(jnp.int32).reshape(1)
    last = jnp.full((1,), lax.axis_size("space") - 1, jnp.int32)
    raw = (space,) + tuple(
        pltpu.with_memory_space_constraint(x, HBM)
        for x in (thickness[0], bed_class, ice_mask, zone_index, bed_levels, balance_rates)
    )
    coarse_lines = CROWS * CCH
    tables = [pltpu.SMEM((16,), F32), pltpu.SMEM((8,), F32)]
    maps = [jax.ShapeDtypeStruct((ROWS, CH * 128), t) for t in (F32, jnp.int32, jnp.int32, jnp.int32)]
    maps.append(lines(24))
    off, inside, *maps = call(
        edge_kernel, "edges", raw, [lines(EDGE_LINES)] * 2 + maps,
        tables + [(2, 8 * CH, 128)] * 4 + [pltpu.SemaphoreType.DMA((14,))],
        "shhhhhh",
    )
    off, inside = far_swap(off), near_swap(inside)
    own, mid, rims, cstate, soff = call(
        inner_kernel, "inner", (space, *maps),
        [lines(ROWS * CH), lines(16 * CH), jax.ShapeDtypeStruct((len(KEPT), 2 * RIM, CH, 128), F32)]
        + [jax.ShapeDtypeStruct((7, 24, CCH, 128), F32)] + [lines(STATIC_LINES)],
        [(ROWS * CH, 128)] * 3 + [(12, WIN, CH, 128)] + [(WIN, CH, 128)] * 2,
        "svvvvv",
    )
    end, prev, payload = call(
        outer_kernel, "outer", (place, space, last, off, inside, mid, rims, cstate),
        [lines(ROWS * CH)] + [lines(coarse_lines)] * 2,
        [(12, WIN, CH, 128), (7, 24, CCH, 128)] + [(WIN, CH, 128)] * 2,
        "sssvvvvv",
    )
    soff = far_swap(soff)
    d1, d2, d3 = (shifted(payload, k) for k in (1, 2, 3))
    d1, d2, d3, soff = lax.optimization_barrier((d1, d2, d3, soff))
    base, j1, j2, off, inside = call(
        gather_kernel, "gather", (place, space, cstate, d1, d2, d3),
        [lines(coarse_lines)] * 3 + [lines(JUMP_LINES), lines(JUMP_LINES + STATIC_LINES)], (), "ssvvvv",
    )
    before = shifted(end, 1)
    off, inside = far_swap(off), near_swap(inside)
    out, nxt = call(
        chain_kernel, "chain",
        (place, space, last, own, cstate, end, prev, before, base, j1, j2, off, inside, soff),
        [jax.ShapeDtypeStruct((ROWS, CH * 128), F32)] * 2,
        [(CWIN, CCH, 128)] * 10 + [(CROWS, CCH, 128)] * 2 + [(ROWS * CH, 128)]
        + [(ROWS, CH * 128)] * 2 + [pltpu.SemaphoreType.DMA((8,))],
        "sss" + "v" * 11, out_space=HBM,
    )
    return out[None], nxt[None]


def solution(mesh):
    placed = (
        P("tm", "space", None),
        P("space", None),
        P("space", None),
        P("space", None),
        P(),
        P(),
    )
    return jax.shard_map(
        per_device,
        mesh=mesh,
        in_specs=placed,
        out_specs=(P("tm", "space", None), P("tm", "space", None)),
        check_vma=False,
    )
```

```python
import jax
import jax.numpy as jnp
from jax import lax
from jax.experimental import pallas as pl
from jax.experimental.pallas import tpu as pltpu
from jax.sharding import PartitionSpec as P

ROWS = 32
CH = 16
CROWS = ROWS // 2
CCH = CH // 2
HALO = 8
WIN = ROWS + 2 * HALO
RIM = 10
CHALO = 12
CWIN = CROWS + 2 * CHALO
F32 = jnp.float32
BF16 = jnp.bfloat16

FINE_GAIN, FINE_CAP = 0.5 / 4.0 * 0.1, 0.1
COARSE_GAIN, COARSE_CAP = 0.5 / 16.0 * 0.05, 0.05
FINE_TAU, COARSE_TAU = 0.2, 0.4


def column_masks(chunks):
    lane = lax.broadcasted_iota(jnp.int32, (8, 128), 1)
    sub = lax.broadcasted_iota(jnp.int32, (8, 128), 0)
    left, right = lane == 0, lane == 127
    return chunks, left, left & (sub == 0), right, right & (sub == 7)


def line_of(k):
    return (k % 2) * 8 + k // 2


def from_left(x, masks, fill):
    chunks, edge, border, _, _ = masks
    a = pltpu.roll(x, 1, axis=2)
    if chunks == CCH:
        return jnp.where(border[None], fill, jnp.where(edge[None], pltpu.roll(a, 1, axis=1), a))
    even, odd = a[:, :8], a[:, 8:]
    if not isinstance(fill, float):
        fill = fill[:, :8]
    first = jnp.where(border[None], fill, jnp.where(edge[None], pltpu.roll(odd, 1, axis=1), even))
    return jnp.concatenate([first, jnp.where(edge[None], even, odd)], axis=1)


def from_right(x, masks, fill):
    chunks, _, _, edge, border = masks
    a = pltpu.roll(x, 127, axis=2)
    if chunks == CCH:
        return jnp.where(border[None], fill, jnp.where(edge[None], pltpu.roll(a, 7, axis=1), a))
    even, odd = a[:, :8], a[:, 8:]
    second = jnp.where(border[None], fill, jnp.where(edge[None], pltpu.roll(even, 7, axis=1), odd))
    return jnp.concatenate([jnp.where(edge[None], odd, even), second], axis=1)


def flow(h, s, g, c, ta, d, dy, lo, hi, masks, gain, cap, block, emit):
    for a in range(lo - 1, hi + 1, block):
        b = min(a + block, hi + 1)
        level = s[a:b]
        right = from_right(level, masks, 0.0)
        left = from_left(level, masks, 0.0)
        sx = s[a + 1 : b + 1] - s[a - 1 : b - 1]
        sy = right - left
        t = h[a:b]
        t2 = t * t
        fifth = t2 * t2 * t
        d[a:b] = jnp.minimum(fifth * gain * (sx * sx + sy * sy), cap)
        dy[a:b] = right - level
    for a in range(lo, hi, block):
        b = min(a + block, hi)
        dd = d[a - 1 : b + 1]
        ss = s[a - 1 : b + 1]
        fx = (dd[1:] + dd[:-1]) * (ss[1:] - ss[:-1])
        mid = dd[1:-1]
        fy = (mid + from_right(mid, masks, 0.0)) * dy[a:b]
        fy_left = from_left(fy, masks, mid * ss[1:-1])
        new = h[a:b] + (fx[1:] - fx[:-1] + fy - fy_left + ta[a:b])
        emit(a, b, jnp.maximum(new, 0.0) * c[a:b])


def split3(x):
    hi = x.astype(BF16)
    r = x - hi.astype(F32)
    mid = r.astype(BF16)
    lo = (r - mid.astype(F32)).astype(BF16)
    return hi, mid, lo


def times(x, m):
    parts = [jnp.dot(p, m, preferred_element_type=F32) for p in split3(x)]
    return parts[0] + (parts[1] + parts[2])


def restrict_mats():
    i = lax.broadcasted_iota(jnp.int32, (128, 128), 0)
    j = lax.broadcasted_iota(jnp.int32, (128, 128), 1)
    half = lax.shift_right_logical(i, 1)
    lo = jnp.where(j == half, 0.25, 0.0).astype(BF16)
    hi = jnp.where(j == half + 64, 0.25, 0.0).astype(BF16)
    return lo, hi


def prolong_mats():
    i = lax.broadcasted_iota(jnp.int32, (128, 128), 0)
    j = lax.broadcasted_iota(jnp.int32, (128, 128), 1)
    half = lax.shift_right_logical(j, 1)
    lo = jnp.where(i == half, 1.0, 0.0).astype(BF16)
    hi = jnp.where(i == half + 64, 1.0, 0.0).astype(BF16)
    return lo, hi


def restrict(x, mats):
    n = x.shape[0] // 2
    y = x.reshape(n, 2, CH, 128)
    y = y[:, 0] + y[:, 1]
    even, odd = y[:, :8].reshape(n * CCH, 128), y[:, 8:].reshape(n * CCH, 128)
    return (times(even, mats[0]) + times(odd, mats[1])).reshape(n, CCH, 128)


def look_up(index, table, size):
    values = [table[k] for k in range(size)]
    bit = 0
    while len(values) > 1:
        on = (lax.shift_right_logical(index, bit) & 1) == 1
        values = [jnp.where(on, values[k + 1], values[k]) for k in range(0, len(values), 2)]
        bit += 1
    return values[0]


EDGE = (8, 8, 6, 6)
EDGE_LINES = sum(EDGE) * CH
STATIC_LINES = 3 * CHALO * CCH
JUMPS = (12, 8, 4)
JUMP_LINES = sum(JUMPS) * CCH
H0, S0, G, C, TA = 0, 5, 9, 10, 11
KEPT = (0, 1, 2, 3, 4, 9, 10, 11)
CH0, CS0, CG, CC, CTA = 0, 2, 4, 5, 6


def fetch(pairs, sems):
    copies = [pltpu.make_async_copy(src, dst, sems.at[i]) for i, (src, dst) in enumerate(pairs)]
    for copy in copies:
        copy.start()
    return copies


def edge_kernel(space, thick, bed, mask, zone, levels, rates, off, inside, tv, bv, mv, zv, tab,
                lev, rat, hx, gx, cx, tx, sems):
    pairs = [(levels, lev), (rates, rat)]
    maps = ((bed, bv), (zone, zv), (thick, tv), (mask, mv))
    for r, count in ((0, 8), (ROWS - 8, 8), (8, ROWS - 16)):
        pairs += [(src.at[r : r + count], dst.at[r : r + count]) for src, dst in maps]
    copies = fetch(pairs, sems)
    for copy in copies[:10]:
        copy.wait()
    for k in range(16):
        tab[k : k + 1] = jnp.full((1, 128), lev[k], F32)
    for k in range(8):
        tab[16 + k : 17 + k] = jnp.full((1, 128), rat[k], F32)
    for half in range(2):
        r = slice(half * (ROWS - 8), half * (ROWS - 8) + 8)
        for k in range(CH):
            cols = slice(k * 128, k * 128 + 128)
            there = (half, pl.ds(line_of(k), 8, stride=CH), slice(None))
            hx[there] = tv[r, cols]
            gx[there] = look_up(bv[r, cols], lev, 16)
            cx[there] = mv[r, cols].astype(F32)
            tx[there] = look_up(zv[r, cols], rat, 8) * FINE_TAU
    odd = space[0] & 1
    at = 0
    for ref, count in zip((hx, gx, cx, tx), EDGE):
        n = count * CH
        skip = (8 - count) * CH
        off[at : at + n] = ref[odd, pl.ds(odd * skip, n)]
        inside[at : at + n] = ref[1 - odd, pl.ds((1 - odd) * skip, n)]
        at += n
    inside[at : at + 8] = jnp.zeros((8, 128), F32)
    for copy in copies[10:]:
        copy.wait()


def inner_kernel(space, tv, bv, mv, zv, tab, own, mid, rims, cstate, off, gl, cl, tl, state, d, dy):
    table = [jnp.broadcast_to(tab[k : k + 1], (8, 128)) for k in range(24)]
    lev, rat = table[:16], table[16:]
    for r in range(0, ROWS, 8):
        for k in range(CH):
            here = (slice(r, r + 8), slice(k * 128, k * 128 + 128))
            there = (pl.ds(r * CH + line_of(k), 8, stride=CH), slice(None))
            own[there] = tv[here]
            gl[there] = look_up(bv[here], lev, 16)
            cl[there] = mv[here].astype(F32)
            tl[there] = look_up(zv[here], rat, 8) * FINE_TAU
    mats = restrict_mats()
    mine = slice(HALO, HALO + ROWS)
    ratio = COARSE_TAU / FINE_TAU
    odd = space[0] & 1
    n = CHALO * CCH
    coarse = {}
    for ref, slot, cslot in ((own, H0, CH0), (gl, G, CG), (cl, C, CC), (tl, TA, CTA)):
        fine = ref[...].reshape(ROWS, CH, 128)
        state[slot, mine] = fine
        value = restrict(fine, mats)
        coarse[cslot] = value * ratio if cslot == CTA else value
        cstate[cslot, 4:20] = coarse[cslot]
    cstate[CS0, 4:20] = coarse[CG] + coarse[CH0]
    state[S0, mine] = state[G, mine] + state[H0, mine]
    for at, cslot in enumerate((CG, CC, CTA)):
        off[at * n : at * n + n] = cstate[cslot, pl.ds(4 + odd * (CROWS - CHALO), CHALO)].reshape(n, 128)
    coarse_steps(cstate, d, dy, ((6, 18), (8, 16)))
    fine_steps(state, d, dy, [(HALO + 2 * k, WIN - HALO - 2 * k) for k in (1, 2, 3, 4)])
    mid[...] = state[H0 + 4, 2 * HALO : WIN - 2 * HALO].reshape(16 * CH, 128)
    for at, slot in enumerate(KEPT):
        rims[at, 0:RIM] = state[slot, HALO : HALO + RIM]
        rims[at, RIM:] = state[slot, WIN - HALO - RIM : WIN - HALO]


def coarse_steps(cstate, d, dy, spans):
    masks = column_masks(CCH)
    cd, cdy = d.at[0:24, 0:CCH], dy.at[0:24, 0:CCH]
    for step, (lo, hi) in enumerate(spans):

        def emit(a, b, value, step=step):
            if step == 0:
                cstate[CH0 + 1, a:b] = value
                cstate[CS0 + 1, a:b] = value + cstate[CG, a:b]
            else:
                cstate[CH0, a:b] = value

        flow(cstate.at[CH0 + step], cstate.at[CS0 + step], cstate.at[CG], cstate.at[CC], cstate.at[CTA], cd, cdy,
             lo, hi, masks, COARSE_GAIN, COARSE_CAP, 8, emit)


def fine_steps(state, d, dy, spans):
    masks = column_masks(CH)
    for step, (lo, hi) in enumerate(spans):

        def emit(a, b, value, step=step):
            state[H0 + step + 1, a:b] = value
            if step < 3:
                state[S0 + step + 1, a:b] = value + state[G, a:b]

        flow(state.at[H0 + step], state.at[S0 + step], state.at[G], state.at[C], state.at[TA], d, dy,
             lo, hi, masks, FINE_GAIN, FINE_CAP, 4, emit)


def outer_kernel(place, space, last, off, inside, mid, rims, cstate_in, end, prev, payload, state, cstate, d, dy):
    for at, slot in enumerate(KEPT):
        state[slot, HALO : HALO + RIM] = rims[at, 0:RIM]
        state[slot, WIN - HALO - RIM : WIN - HALO] = rims[at, RIM:]
    for rim in (slice(HALO, HALO + RIM), slice(WIN - HALO - RIM, WIN - HALO)):
        for step in range(4):
            state[S0 + step, rim] = state[H0 + step, rim] + state[G, rim]
    cstate[:, 4:20] = cstate_in[:, 4:20]
    odd = space[0] & 1
    at_border = (space[0] == 0) | (space[0] == last[0])
    at = 0
    for slot, count in zip((H0, G, C, TA), EDGE):
        n = count * CH
        far = jnp.where(at_border, 0.0, off[at : at + n]).reshape(count, CH, 128)
        near = inside[at : at + n].reshape(count, CH, 128)
        state[slot, HALO - count : HALO] = jnp.where(odd == 1, near, far)
        state[slot, HALO + ROWS : HALO + ROWS + count] = jnp.where(odd == 1, far, near)
        at += n
    mats = restrict_mats()
    ratio = COARSE_TAU / FINE_TAU
    for lo, clo in ((0, 0), (40, 20)):
        state[S0, lo : lo + 8] = state[G, lo : lo + 8] + state[H0, lo : lo + 8]
        ground = restrict(state[G, lo : lo + 8], mats)
        thick = restrict(state[H0, lo : lo + 8], mats)
        cstate[CG, clo : clo + 4] = ground
        cstate[CH0, clo : clo + 4] = thick
        cstate[CS0, clo : clo + 4] = ground + thick
    for lo, clo in ((4, 2), (40, 20)):
        cstate[CC, clo : clo + 2] = restrict(state[C, lo : lo + 4], mats)
        cstate[CTA, clo : clo + 2] = restrict(state[TA, lo : lo + 4], mats) * ratio
    coarse_steps(cstate, d, dy, ((2, 6), (4, 8)))
    coarse_steps(cstate, d, dy, ((18, 22), (16, 20)))
    prev[...] = cstate[CH0, 4:20].reshape(CROWS * CCH, 128)
    fine_steps(state, d, dy, [(2 * k, HALO + 2 * k) for k in (1, 2, 3, 4)])
    fine_steps(state, d, dy, [(WIN - HALO - 2 * k, WIN - 2 * k) for k in (1, 2, 3, 4)])
    end[0 : 8 * CH] = state[H0 + 4, 8:16].reshape(8 * CH, 128)
    end[8 * CH : 24 * CH] = mid[...]
    end[24 * CH : 32 * CH] = state[H0 + 4, 32:40].reshape(8 * CH, 128)
    value = restrict(end[...].reshape(ROWS, CH, 128), mats).reshape(CROWS * CCH, 128)
    payload[...] = value - jnp.where(place[0] == 0, 0.0, prev[...])


def pack_kernel(source, target):
    target[...] = source[...]


def gather_kernel(place, space, cstate, d1, d2, d3, base, j1, j2, off, inside):
    m = place[0]
    base[...] = jnp.where(m == 1, d1[...], jnp.where(m == 2, d2[...], d3[...]))
    j1[...] = jnp.where(m == 2, d1[...], d2[...])
    j2[...] = d1[...]
    odd = space[0] & 1
    at = 0
    for ref, count in zip((base, j1, j2), JUMPS):
        n = count * CCH
        skip = CROWS * CCH - n
        off[at : at + n] = ref[pl.ds(odd * skip, n)]
        inside[at : at + n] = ref[pl.ds((1 - odd) * skip, n)]
        at += n
    n = CHALO * CCH
    for cslot in (CG, CC, CTA):
        inside[at : at + n] = cstate[cslot, pl.ds(4 + (1 - odd) * (CROWS - CHALO), CHALO)].reshape(n, 128)
        at += n


def chain_kernel(place, space, last, own, cstate, end, prev, before, base, j1, j2, off, inside, soff,
                 out_hbm, nxt_hbm, h, s, s2, g, c, ta, d, dy, jump1, jump2, fix, now_m, fine, out, nxt, sems):
    m = place[0]
    odd = space[0] & 1
    at_border = (space[0] == 0) | (space[0] == last[0])
    bottom = CHALO + CROWS

    def window(ref, own, count, far_ref, at, skip):
        n = count * CCH
        far = jnp.where(at_border, 0.0, far_ref[at : at + n]).reshape(count, CCH, 128)
        near = inside[skip + at : skip + at + n].reshape(count, CCH, 128)
        ref[CHALO - count : CHALO] = jnp.where(odd == 1, near, far)
        ref[CHALO:bottom] = own
        ref[bottom : bottom + count] = jnp.where(odd == 1, far, near)
        return at + n

    @pl.when(m > 0)
    def _():
        at = 0
        for ref, slot in ((g, CG), (c, CC), (ta, CTA)):
            at = window(ref, cstate[slot, 4:20], CHALO, soff, at, JUMP_LINES)
        at = 0
        for ref, held, count in zip((h, jump1, jump2), (base, j1, j2), JUMPS):
            at = window(ref, held[...].reshape(CROWS, CCH, 128), count, off, at, 0)
        s[...] = g[...] + h[...]
        now_m[...] = h[CHALO:bottom]

    masks = column_masks(CCH)
    mats = restrict_mats()
    mine = slice(CHALO, bottom)
    fix[...] = jnp.zeros_like(fix)
    lo_mat, hi_mat = prolong_mats()

    def spread_out(value, field, target, target_hbm, first, keep=None):
        value = value.reshape(CROWS * CCH, 128)
        halves = [times(value, mat).reshape(CROWS, CCH, 128) for mat in (lo_mat, hi_mat)]
        wide = jnp.concatenate(halves, axis=1).reshape(CROWS, 1, CH, 128)
        total = (field[...].reshape(CROWS, 2, CH, 128) + wide).reshape(ROWS, CH, 128)
        if keep is not None:
            total = jnp.where(m == 0, keep, total)
        fine[...] = total.reshape(ROWS * CH, 128)
        copies = []
        for r in range(0, ROWS, 8):
            for k in range(CH):
                target[r : r + 8, k * 128 : k * 128 + 128] = fine[pl.ds(r * CH + line_of(k), 8, stride=CH), :]
            copy = pltpu.make_async_copy(target.at[r : r + 8], target_hbm.at[r : r + 8], sems.at[first + r // 8])
            copy.start()
            copies.append(copy)
        return copies

    edge = 0
    waits = []
    for k, jump in ((1, jump1), (2, jump2), (3, None)):
        if k == 3:
            coarse_before = restrict(before[...].reshape(ROWS, CH, 128), mats)
            waits += spread_out(now_m[...] - coarse_before, before, nxt, nxt_hbm, 0,
                                own[...].reshape(ROWS, CH, 128))
        first_edge = edge
        edge += 4

        @pl.when(m >= k)
        def _(k=k, jump=jump, first_edge=first_edge):
            for step, (now, later) in enumerate(((s, s2), (s2, s))):
                lo = first_edge + 2 * (step + 1)

                def emit(a, b, value, later=later):
                    h[a:b] = value
                    later[a:b] = value + g[a:b]

                flow(h, now, g, c, ta, d, dy, lo, CWIN - lo, masks, COARSE_GAIN, COARSE_CAP, 8, emit)

            @pl.when(m == k)
            def _():
                fix[...] = h[mine] - prev[...].reshape(CROWS, CCH, 128)

            if jump is not None:
                lo = first_edge + 4
                for a in range(lo, CWIN - lo, 8):
                    b = min(a + 8, CWIN - lo)
                    value = h[a:b] + jump[a:b]
                    h[a:b] = value
                    s[a:b] = value + g[a:b]

                @pl.when(m == k + 1)
                def _():
                    now_m[...] = h[mine]

    waits += spread_out(fix[...], end, out, out_hbm, 4)
    for copy in waits:
        copy.wait()


def lines(n):
    return jax.ShapeDtypeStruct((n, 128), F32)


VMEM, SMEM, HBM = pltpu.VMEM, pltpu.SMEM, pltpu.HBM


def call(kernel, name, ins, outs, scratch=(), in_spaces=None, out_space=VMEM, limit=16):
    spaces = {"s": SMEM, "h": HBM, "v": VMEM}
    return pl.pallas_call(
        kernel,
        out_shape=outs,
        in_specs=[pl.BlockSpec(memory_space=spaces[letter]) for letter in in_spaces],
        out_specs=[pl.BlockSpec(memory_space=out_space)] * len(outs),
        scratch_shapes=[pltpu.VMEM(item, F32) if isinstance(item, tuple) else item for item in scratch],
        compiler_params=pltpu.CompilerParams(vmem_limit_bytes=limit * 2**20),
        name=name,
    )(*ins)


def shifted(x, by):
    devices = lax.axis_size("tm")
    return lax.ppermute(x, "tm", [(i, (i + by) % devices) for i in range(devices)])


def far_swap(x):
    devices = lax.axis_size("space")
    pairs = [(i, (i + 1) % devices) for i in range(1, devices, 2)]
    return lax.ppermute(x, "space", pairs + [(j, i) for i, j in pairs])


def near_swap(x):
    devices = lax.axis_size("space")
    return lax.ppermute(x, "space", [(i, i ^ 1) for i in range(devices)])


def per_device(thickness, bed_class, ice_mask, zone_index, bed_levels, balance_rates):
    place = lax.axis_index("tm").astype(jnp.int32).reshape(1)
    space = lax.axis_index("space").astype(jnp.int32).reshape(1)
    last = jnp.full((1,), lax.axis_size("space") - 1, jnp.int32)
    raw = (space,) + tuple(
        pltpu.with_memory_space_constraint(x, HBM)
        for x in (thickness[0], bed_class, ice_mask, zone_index, bed_levels, balance_rates)
    )
    coarse_lines = CROWS * CCH
    tables = [pltpu.SMEM((16,), F32), pltpu.SMEM((8,), F32)]
    maps = [jax.ShapeDtypeStruct((ROWS, CH * 128), t) for t in (F32, jnp.int32, jnp.int32, jnp.int32)]
    maps.append(lines(24))
    off, inside, *maps = call(
        edge_kernel, "edges", raw, [lines(EDGE_LINES), lines(EDGE_LINES + 8)] + maps,
        tables + [(2, 8 * CH, 128)] * 4 + [pltpu.SemaphoreType.DMA((14,))],
        "shhhhhh",
    )
    off, inside = far_swap(off), near_swap(inside)
    own, mid, rims, cstate, soff = call(
        inner_kernel, "inner", (space, *maps),
        [lines(ROWS * CH), lines(16 * CH), jax.ShapeDtypeStruct((len(KEPT), 2 * RIM, CH, 128), F32)]
        + [jax.ShapeDtypeStruct((7, 24, CCH, 128), F32)] + [lines(STATIC_LINES)],
        [(ROWS * CH, 128)] * 3 + [(12, WIN, CH, 128)] + [(WIN, CH, 128)] * 2,
        "svvvvv",
    )
    end, prev, payload = call(
        outer_kernel, "outer", (place, space, last, off, inside, mid, rims, cstate),
        [lines(ROWS * CH)] + [lines(coarse_lines)] * 2,
        [(12, WIN, CH, 128), (7, 24, CCH, 128)] + [(WIN, CH, 128)] * 2,
        "sssvvvvv",
    )
    soff = far_swap(soff)
    d1, d2, d3 = (shifted(payload, k) for k in (1, 2, 3))
    d1, d2, d3, soff = lax.optimization_barrier((d1, d2, d3, soff))
    base, j1, j2, off, inside = call(
        gather_kernel, "gather", (place, space, cstate, d1, d2, d3),
        [lines(coarse_lines)] * 3 + [lines(JUMP_LINES), lines(JUMP_LINES + STATIC_LINES)], (), "ssvvvv",
    )
    before = shifted(end, 1)
    off, inside = far_swap(off), near_swap(inside)
    out, nxt = call(
        chain_kernel, "chain",
        (place, space, last, own, cstate, end, prev, before, base, j1, j2, off, inside, soff),
        [jax.ShapeDtypeStruct((ROWS, CH * 128), F32)] * 2,
        [(CWIN, CCH, 128)] * 10 + [(CROWS, CCH, 128)] * 2 + [(ROWS * CH, 128)]
        + [(ROWS, CH * 128)] * 2 + [pltpu.SemaphoreType.DMA((8,))],
        "sss" + "v" * 11, out_space=HBM,
    )
    return out[None], nxt[None]


def solution(mesh):
    placed = (
        P("tm", "space", None),
        P("space", None),
        P("space", None),
        P("space", None),
        P(),
        P(),
    )
    return jax.shard_map(
        per_device,
        mesh=mesh,
        in_specs=placed,
        out_specs=(P("tm", "space", None), P("tm", "space", None)),
        check_vma=False,
    )
```

```python
import jax
import jax.numpy as jnp
from jax import lax
from jax.experimental import pallas as pl
from jax.experimental.pallas import tpu as pltpu
from jax.sharding import PartitionSpec as P

ROWS = 32
CH = 16
CROWS = ROWS // 2
CCH = CH // 2
HALO = 8
WIN = ROWS + 2 * HALO
RIM = 10
CHALO = 12
CWIN = CROWS + 2 * CHALO
F32 = jnp.float32
BF16 = jnp.bfloat16

FINE_GAIN, FINE_CAP = 0.5 / 4.0 * 0.1, 0.1
COARSE_GAIN, COARSE_CAP = 0.5 / 16.0 * 0.05, 0.05
FINE_TAU, COARSE_TAU = 0.2, 0.4


def column_masks(chunks):
    lane = lax.broadcasted_iota(jnp.int32, (8, 128), 1)
    sub = lax.broadcasted_iota(jnp.int32, (8, 128), 0)
    left, right = lane == 0, lane == 127
    return chunks, left, left & (sub == 0), right, right & (sub == 7)


def line_of(k):
    return (k % 2) * 8 + k // 2


def from_left(x, masks, fill):
    chunks, edge, border, _, _ = masks
    a = pltpu.roll(x, 1, axis=2)
    if chunks == CCH:
        return jnp.where(border[None], fill, jnp.where(edge[None], pltpu.roll(a, 1, axis=1), a))
    even, odd = a[:, :8], a[:, 8:]
    if not isinstance(fill, float):
        fill = fill[:, :8]
    first = jnp.where(border[None], fill, jnp.where(edge[None], pltpu.roll(odd, 1, axis=1), even))
    return jnp.concatenate([first, jnp.where(edge[None], even, odd)], axis=1)


def from_right(x, masks, fill):
    chunks, _, _, edge, border = masks
    a = pltpu.roll(x, 127, axis=2)
    if chunks == CCH:
        return jnp.where(border[None], fill, jnp.where(edge[None], pltpu.roll(a, 7, axis=1), a))
    even, odd = a[:, :8], a[:, 8:]
    second = jnp.where(border[None], fill, jnp.where(edge[None], pltpu.roll(even, 7, axis=1), odd))
    return jnp.concatenate([jnp.where(edge[None], odd, even), second], axis=1)


def flow(h, s, g, c, ta, d, dy, lo, hi, masks, gain, cap, block, emit):
    for a in range(lo - 1, hi + 1, block):
        b = min(a + block, hi + 1)
        level = s[a:b]
        right = from_right(level, masks, 0.0)
        left = from_left(level, masks, 0.0)
        sx = s[a + 1 : b + 1] - s[a - 1 : b - 1]
        sy = right - left
        t = h[a:b]
        t2 = t * t
        fifth = t2 * t2 * t
        d[a:b] = jnp.minimum(fifth * gain * (sx * sx + sy * sy), cap)
        dy[a:b] = right - level
    for a in range(lo, hi, block):
        b = min(a + block, hi)
        dd = d[a - 1 : b + 1]
        ss = s[a - 1 : b + 1]
        fx = (dd[1:] + dd[:-1]) * (ss[1:] - ss[:-1])
        mid = dd[1:-1]
        fy = (mid + from_right(mid, masks, 0.0)) * dy[a:b]
        fy_left = from_left(fy, masks, mid * ss[1:-1])
        new = h[a:b] + (fx[1:] - fx[:-1] + fy - fy_left + ta[a:b])
        emit(a, b, jnp.maximum(new, 0.0) * c[a:b])


def split3(x):
    hi = x.astype(BF16)
    r = x - hi.astype(F32)
    mid = r.astype(BF16)
    lo = (r - mid.astype(F32)).astype(BF16)
    return hi, mid, lo


def times(x, m):
    parts = [jnp.dot(p, m, preferred_element_type=F32) for p in split3(x)]
    return parts[0] + (parts[1] + parts[2])


def restrict_mats():
    i = lax.broadcasted_iota(jnp.int32, (128, 128), 0)
    j = lax.broadcasted_iota(jnp.int32, (128, 128), 1)
    half = lax.shift_right_logical(i, 1)
    lo = jnp.where(j == half, 0.25, 0.0).astype(BF16)
    hi = jnp.where(j == half + 64, 0.25, 0.0).astype(BF16)
    return lo, hi


def prolong_mats():
    i = lax.broadcasted_iota(jnp.int32, (128, 128), 0)
    j = lax.broadcasted_iota(jnp.int32, (128, 128), 1)
    half = lax.shift_right_logical(j, 1)
    lo = jnp.where(i == half, 1.0, 0.0).astype(BF16)
    hi = jnp.where(i == half + 64, 1.0, 0.0).astype(BF16)
    return lo, hi


def restrict(x, mats):
    n = x.shape[0] // 2
    y = x.reshape(n, 2, CH, 128)
    y = y[:, 0] + y[:, 1]
    even, odd = y[:, :8].reshape(n * CCH, 128), y[:, 8:].reshape(n * CCH, 128)
    return (times(even, mats[0]) + times(odd, mats[1])).reshape(n, CCH, 128)


def look_up(index, table, size):
    values = [table[k] for k in range(size)]
    bit = 0
    while len(values) > 1:
        on = (lax.shift_right_logical(index, bit) & 1) == 1
        values = [jnp.where(on, values[k + 1], values[k]) for k in range(0, len(values), 2)]
        bit += 1
    return values[0]


EDGE = (8, 8, 6, 6)
EDGE_LINES = sum(EDGE) * CH
STATIC_LINES = 3 * CHALO * CCH
JUMPS = (12, 8, 4)
JUMP_LINES = sum(JUMPS) * CCH
H0, S0, G, C, TA = 0, 5, 9, 10, 11
KEPT = (0, 1, 2, 3, 4, 9, 10, 11)
CH0, CS0, CG, CC, CTA = 0, 2, 4, 5, 6


def fetch(pairs, sems):
    copies = [pltpu.make_async_copy(src, dst, sems.at[i]) for i, (src, dst) in enumerate(pairs)]
    for copy in copies:
        copy.start()
    return copies


def edge_kernel(space, thick, bed, mask, zone, levels, rates, off, inside, tv, bv, mv, zv, tab,
                lev, rat, hx, gx, cx, tx, sems):
    pairs = [(levels, lev), (rates, rat)]
    maps = ((bed, bv), (zone, zv), (thick, tv), (mask, mv))
    for r, count in ((0, 8), (ROWS - 8, 8), (8, ROWS - 16)):
        pairs += [(src.at[r : r + count], dst.at[r : r + count]) for src, dst in maps]
    copies = fetch(pairs, sems)
    for copy in copies[:10]:
        copy.wait()
    for k in range(16):
        tab[k : k + 1] = jnp.full((1, 128), lev[k], F32)
    for k in range(8):
        tab[16 + k : 17 + k] = jnp.full((1, 128), rat[k], F32)
    for half in range(2):
        r = slice(half * (ROWS - 8), half * (ROWS - 8) + 8)
        for k in range(CH):
            cols = slice(k * 128, k * 128 + 128)
            there = (half, pl.ds(line_of(k), 8, stride=CH), slice(None))
            hx[there] = tv[r, cols]
            gx[there] = look_up(bv[r, cols], lev, 16)
            cx[there] = mv[r, cols].astype(F32)
            tx[there] = look_up(zv[r, cols], rat, 8) * FINE_TAU
    odd = space[0] & 1
    at = 0
    for ref, count in zip((hx, gx, cx, tx), EDGE):
        n = count * CH
        skip = (8 - count) * CH
        off[at : at + n] = ref[odd, pl.ds(odd * skip, n)]
        inside[at : at + n] = ref[1 - odd, pl.ds((1 - odd) * skip, n)]
        at += n
    inside[at : at + 8] = jnp.zeros((8, 128), F32)
    for copy in copies[10:]:
        copy.wait()


def inner_kernel(space, tv, bv, mv, zv, tab, own, mid, rims, cstate, off, gl, cl, tl, state, d, dy):
    table = [jnp.broadcast_to(tab[k : k + 1], (8, 128)) for k in range(24)]
    lev, rat = table[:16], table[16:]
    for r in range(0, ROWS, 8):
        for k in range(CH):
            here = (slice(r, r + 8), slice(k * 128, k * 128 + 128))
            there = (pl.ds(r * CH + line_of(k), 8, stride=CH), slice(None))
            own[there] = tv[here]
            gl[there] = look_up(bv[here], lev, 16)
            cl[there] = mv[here].astype(F32)
            tl[there] = look_up(zv[here], rat, 8) * FINE_TAU
    mats = restrict_mats()
    mine = slice(HALO, HALO + ROWS)
    ratio = COARSE_TAU / FINE_TAU
    odd = space[0] & 1
    n = CHALO * CCH
    coarse = {}
    for ref, slot, cslot in ((own, H0, CH0), (gl, G, CG), (cl, C, CC), (tl, TA, CTA)):
        fine = ref[...].reshape(ROWS, CH, 128)
        state[slot, mine] = fine
        value = restrict(fine, mats)
        coarse[cslot] = value * ratio if cslot == CTA else value
        cstate[cslot, 4:20] = coarse[cslot]
    cstate[CS0, 4:20] = coarse[CG] + coarse[CH0]
    state[S0, mine] = state[G, mine] + state[H0, mine]
    for at, cslot in enumerate((CG, CC, CTA)):
        off[at * n : at * n + n] = cstate[cslot, pl.ds(4 + odd * (CROWS - CHALO), CHALO)].reshape(n, 128)
    coarse_steps(cstate, d, dy, ((6, 18), (8, 16)))
    fine_steps(state, d, dy, [(HALO + 2 * k, WIN - HALO - 2 * k) for k in (1, 2, 3, 4)])
    mid[...] = state[H0 + 4, 2 * HALO : WIN - 2 * HALO].reshape(16 * CH, 128)
    for at, slot in enumerate(KEPT):
        rims[at, 0:RIM] = state[slot, HALO : HALO + RIM]
        rims[at, RIM:] = state[slot, WIN - HALO - RIM : WIN - HALO]


def coarse_steps(cstate, d, dy, spans):
    masks = column_masks(CCH)
    cd, cdy = d.at[0:24, 0:CCH], dy.at[0:24, 0:CCH]
    for step, (lo, hi) in enumerate(spans):

        def emit(a, b, value, step=step):
            if step == 0:
                cstate[CH0 + 1, a:b] = value
                cstate[CS0 + 1, a:b] = value + cstate[CG, a:b]
            else:
                cstate[CH0, a:b] = value

        flow(cstate.at[CH0 + step], cstate.at[CS0 + step], cstate.at[CG], cstate.at[CC], cstate.at[CTA], cd, cdy,
             lo, hi, masks, COARSE_GAIN, COARSE_CAP, 8, emit)


def fine_steps(state, d, dy, spans):
    masks = column_masks(CH)
    for step, (lo, hi) in enumerate(spans):

        def emit(a, b, value, step=step):
            state[H0 + step + 1, a:b] = value
            if step < 3:
                state[S0 + step + 1, a:b] = value + state[G, a:b]

        flow(state.at[H0 + step], state.at[S0 + step], state.at[G], state.at[C], state.at[TA], d, dy,
             lo, hi, masks, FINE_GAIN, FINE_CAP, 4, emit)


def outer_kernel(place, space, last, off, inside, mid, rims, cstate_in, end, prev, payload, state, cstate, d, dy):
    for at, slot in enumerate(KEPT):
        state[slot, HALO : HALO + RIM] = rims[at, 0:RIM]
        state[slot, WIN - HALO - RIM : WIN - HALO] = rims[at, RIM:]
    for rim in (slice(HALO, HALO + RIM), slice(WIN - HALO - RIM, WIN - HALO)):
        for step in range(4):
            state[S0 + step, rim] = state[H0 + step, rim] + state[G, rim]
    cstate[:, 4:20] = cstate_in[:, 4:20]
    odd = space[0] & 1
    at_border = (space[0] == 0) | (space[0] == last[0])
    at = 0
    for slot, count in zip((H0, G, C, TA), EDGE):
        n = count * CH
        far = jnp.where(at_border, 0.0, off[at : at + n]).reshape(count, CH, 128)
        near = inside[at : at + n].reshape(count, CH, 128)
        state[slot, HALO - count : HALO] = jnp.where(odd == 1, near, far)
        state[slot, HALO + ROWS : HALO + ROWS + count] = jnp.where(odd == 1, far, near)
        at += n
    mats = restrict_mats()
    ratio = COARSE_TAU / FINE_TAU
    for lo, clo in ((0, 0), (40, 20)):
        state[S0, lo : lo + 8] = state[G, lo : lo + 8] + state[H0, lo : lo + 8]
        ground = restrict(state[G, lo : lo + 8], mats)
        thick = restrict(state[H0, lo : lo + 8], mats)
        cstate[CG, clo : clo + 4] = ground
        cstate[CH0, clo : clo + 4] = thick
        cstate[CS0, clo : clo + 4] = ground + thick
    for lo, clo in ((4, 2), (40, 20)):
        cstate[CC, clo : clo + 2] = restrict(state[C, lo : lo + 4], mats)
        cstate[CTA, clo : clo + 2] = restrict(state[TA, lo : lo + 4], mats) * ratio
    coarse_steps(cstate, d, dy, ((2, 6), (4, 8)))
    coarse_steps(cstate, d, dy, ((18, 22), (16, 20)))
    prev[...] = cstate[CH0, 4:20].reshape(CROWS * CCH, 128)
    fine_steps(state, d, dy, [(2 * k, HALO + 2 * k) for k in (1, 2, 3, 4)])
    fine_steps(state, d, dy, [(WIN - HALO - 2 * k, WIN - 2 * k) for k in (1, 2, 3, 4)])
    end[0 : 8 * CH] = state[H0 + 4, 8:16].reshape(8 * CH, 128)
    end[8 * CH : 24 * CH] = mid[...]
    end[24 * CH : 32 * CH] = state[H0 + 4, 32:40].reshape(8 * CH, 128)
    value = restrict(end[...].reshape(ROWS, CH, 128), mats).reshape(CROWS * CCH, 128)
    payload[...] = value - jnp.where(place[0] == 0, 0.0, prev[...])


def pack_kernel(source, target):
    target[...] = source[...]


def gather_kernel(place, space, cstate, d1, d2, d3, base, j1, j2, off, inside):
    m = place[0]
    base[...] = jnp.where(m == 1, d1[...], jnp.where(m == 2, d2[...], d3[...]))
    j1[...] = jnp.where(m == 2, d1[...], d2[...])
    j2[...] = d1[...]
    odd = space[0] & 1
    at = 0
    for ref, count in zip((base, j1, j2), JUMPS):
        n = count * CCH
        skip = CROWS * CCH - n
        off[at : at + n] = ref[pl.ds(odd * skip, n)]
        inside[at : at + n] = ref[pl.ds((1 - odd) * skip, n)]
        at += n
    n = CHALO * CCH
    for cslot in (CG, CC, CTA):
        inside[at : at + n] = cstate[cslot, pl.ds(4 + (1 - odd) * (CROWS - CHALO), CHALO)].reshape(n, 128)
        at += n


def chain_kernel(place, space, last, own, cstate, end, prev, before, base, j1, j2, off, inside, soff,
                 out_hbm, nxt_hbm, h, s, s2, g, c, ta, d, dy, jump1, jump2, fix, now_m, fine, out, nxt, sems):
    m = place[0]
    odd = space[0] & 1
    at_border = (space[0] == 0) | (space[0] == last[0])
    bottom = CHALO + CROWS

    def window(ref, own, count, far_ref, at, skip):
        n = count * CCH
        far = jnp.where(at_border, 0.0, far_ref[at : at + n]).reshape(count, CCH, 128)
        near = inside[skip + at : skip + at + n].reshape(count, CCH, 128)
        ref[CHALO - count : CHALO] = jnp.where(odd == 1, near, far)
        ref[CHALO:bottom] = own
        ref[bottom : bottom + count] = jnp.where(odd == 1, far, near)
        return at + n

    @pl.when(m > 0)
    def _():
        at = 0
        for ref, slot in ((g, CG), (c, CC), (ta, CTA)):
            at = window(ref, cstate[slot, 4:20], CHALO, soff, at, JUMP_LINES)
        at = 0
        for ref, held, count in zip((h, jump1, jump2), (base, j1, j2), JUMPS):
            at = window(ref, held[...].reshape(CROWS, CCH, 128), count, off, at, 0)
        s[...] = g[...] + h[...]
        now_m[...] = h[CHALO:bottom]

    masks = column_masks(CCH)
    mats = restrict_mats()
    mine = slice(CHALO, bottom)
    fix[...] = jnp.zeros_like(fix)
    lo_mat, hi_mat = prolong_mats()

    def spread_out(value, field, target, target_hbm, first, keep=None):
        value = value.reshape(CROWS * CCH, 128)
        halves = [times(value, mat).reshape(CROWS, CCH, 128) for mat in (lo_mat, hi_mat)]
        wide = jnp.concatenate(halves, axis=1).reshape(CROWS, 1, CH, 128)
        total = (field[...].reshape(CROWS, 2, CH, 128) + wide).reshape(ROWS, CH, 128)
        if keep is not None:
            total = jnp.where(m == 0, keep, total)
        fine[...] = total.reshape(ROWS * CH, 128)
        copies = []
        for r in range(0, ROWS, 8):
            for k in range(CH):
                target[r : r + 8, k * 128 : k * 128 + 128] = fine[pl.ds(r * CH + line_of(k), 8, stride=CH), :]
            copy = pltpu.make_async_copy(target.at[r : r + 8], target_hbm.at[r : r + 8], sems.at[first + r // 8])
            copy.start()
            copies.append(copy)
        return copies

    edge = 0
    waits = []
    for k, jump in ((1, jump1), (2, jump2), (3, None)):
        if k == 3:
            coarse_before = restrict(before[...].reshape(ROWS, CH, 128), mats)
            waits += spread_out(now_m[...] - coarse_before, before, nxt, nxt_hbm, 0,
                                own[...].reshape(ROWS, CH, 128))
        first_edge = edge
        edge += 4

        @pl.when(m >= k)
        def _(k=k, jump=jump, first_edge=first_edge):
            for step, (now, later) in enumerate(((s, s2), (s2, s))):
                lo = first_edge + 2 * (step + 1)

                def emit(a, b, value, later=later):
                    h[a:b] = value
                    later[a:b] = value + g[a:b]

                flow(h, now, g, c, ta, d, dy, lo, CWIN - lo, masks, COARSE_GAIN, COARSE_CAP, 8, emit)

            @pl.when(m == k)
            def _():
                fix[...] = h[mine] - prev[...].reshape(CROWS, CCH, 128)

            if jump is not None:
                lo = first_edge + 4
                for a in range(lo, CWIN - lo, 8):
                    b = min(a + 8, CWIN - lo)
                    value = h[a:b] + jump[a:b]
                    h[a:b] = value
                    s[a:b] = value + g[a:b]

                @pl.when(m == k + 1)
                def _():
                    now_m[...] = h[mine]

    waits += spread_out(fix[...], end, out, out_hbm, 4)
    for copy in waits:
        copy.wait()


def lines(n):
    return jax.ShapeDtypeStruct((n, 128), F32)


VMEM, SMEM, HBM = pltpu.VMEM, pltpu.SMEM, pltpu.HBM


def call(kernel, name, ins, outs, scratch=(), in_spaces=None, out_space=VMEM, limit=16):
    spaces = {"s": SMEM, "h": HBM, "v": VMEM}
    return pl.pallas_call(
        kernel,
        out_shape=outs,
        in_specs=[pl.BlockSpec(memory_space=spaces[letter]) for letter in in_spaces],
        out_specs=[pl.BlockSpec(memory_space=out_space)] * len(outs),
        scratch_shapes=[pltpu.VMEM(item, F32) if isinstance(item, tuple) else item for item in scratch],
        compiler_params=pltpu.CompilerParams(vmem_limit_bytes=limit * 2**20),
        name=name,
    )(*ins)


def shifted(x, by):
    devices = lax.axis_size("tm")
    return lax.ppermute(x, "tm", [(i, (i + by) % devices) for i in range(devices)])


def far_swap(x):
    slices, devices = lax.axis_size("tm"), lax.axis_size("space")
    pairs = [(m * devices + i, m * devices + i + 1) for m in range(slices) for i in range(1, devices - 1, 2)]
    pairs += [(m * devices + i, (m + 1) * devices + i) for m in range(0, slices, 2) for i in (0, devices - 1)]
    return lax.ppermute(x, ("tm", "space"), pairs + [(j, i) for i, j in pairs])


def near_swap(x):
    devices = lax.axis_size("space")
    return lax.ppermute(x, "space", [(i, i ^ 1) for i in range(devices)])


def per_device(thickness, bed_class, ice_mask, zone_index, bed_levels, balance_rates):
    place = lax.axis_index("tm").astype(jnp.int32).reshape(1)
    space = lax.axis_index("space").astype(jnp.int32).reshape(1)
    last = jnp.full((1,), lax.axis_size("space") - 1, jnp.int32)
    raw = (space,) + tuple(
        pltpu.with_memory_space_constraint(x, HBM)
        for x in (thickness[0], bed_class, ice_mask, zone_index, bed_levels, balance_rates)
    )
    coarse_lines = CROWS * CCH
    tables = [pltpu.SMEM((16,), F32), pltpu.SMEM((8,), F32)]
    maps = [jax.ShapeDtypeStruct((ROWS, CH * 128), t) for t in (F32, jnp.int32, jnp.int32, jnp.int32)]
    maps.append(lines(24))
    off, inside, *maps = call(
        edge_kernel, "edges", raw, [lines(EDGE_LINES), lines(EDGE_LINES + 8)] + maps,
        tables + [(2, 8 * CH, 128)] * 4 + [pltpu.SemaphoreType.DMA((14,))],
        "shhhhhh",
    )
    off, inside = far_swap(off), near_swap(inside)
    own, mid, rims, cstate, soff = call(
        inner_kernel, "inner", (space, *maps),
        [lines(ROWS * CH), lines(16 * CH), jax.ShapeDtypeStruct((len(KEPT), 2 * RIM, CH, 128), F32)]
        + [jax.ShapeDtypeStruct((7, 24, CCH, 128), F32)] + [lines(STATIC_LINES)],
        [(ROWS * CH, 128)] * 3 + [(12, WIN, CH, 128)] + [(WIN, CH, 128)] * 2,
        "svvvvv",
    )
    end, prev, payload = call(
        outer_kernel, "outer", (place, space, last, off, inside, mid, rims, cstate),
        [lines(ROWS * CH)] + [lines(coarse_lines)] * 2,
        [(12, WIN, CH, 128), (7, 24, CCH, 128)] + [(WIN, CH, 128)] * 2,
        "sssvvvvv",
    )
    soff = far_swap(soff)
    d1, d2, d3 = (shifted(payload, k) for k in (1, 2, 3))
    d1, d2, d3, soff = lax.optimization_barrier((d1, d2, d3, soff))
    base, j1, j2, off, inside = call(
        gather_kernel, "gather", (place, space, cstate, d1, d2, d3),
        [lines(coarse_lines)] * 3 + [lines(JUMP_LINES), lines(JUMP_LINES + STATIC_LINES)], (), "ssvvvv",
    )
    before = shifted(end, 1)
    off, inside = far_swap(off), near_swap(inside)
    out, nxt = call(
        chain_kernel, "chain",
        (place, space, last, own, cstate, end, prev, before, base, j1, j2, off, inside, soff),
        [jax.ShapeDtypeStruct((ROWS, CH * 128), F32)] * 2,
        [(CWIN, CCH, 128)] * 10 + [(CROWS, CCH, 128)] * 2 + [(ROWS * CH, 128)]
        + [(ROWS, CH * 128)] * 2 + [pltpu.SemaphoreType.DMA((8,))],
        "sss" + "v" * 11, out_space=HBM,
    )
    return out[None], nxt[None]


def solution(mesh):
    placed = (
        P("tm", "space", None),
        P("space", None),
        P("space", None),
        P("space", None),
        P(),
        P(),
    )
    return jax.shard_map(
        per_device,
        mesh=mesh,
        in_specs=placed,
        out_specs=(P("tm", "space", None), P("tm", "space", None)),
        check_vma=False,
    )
```

```python
import jax
import jax.numpy as jnp
from jax import lax
from jax.experimental import pallas as pl
from jax.experimental.pallas import tpu as pltpu
from jax.sharding import PartitionSpec as P

ROWS = 32
CH = 16
CROWS = ROWS // 2
CCH = CH // 2
HALO = 8
WIN = ROWS + 2 * HALO
RIM = 10
CHALO = 12
CWIN = CROWS + 2 * CHALO
F32 = jnp.float32
BF16 = jnp.bfloat16

FINE_GAIN, FINE_CAP = 0.5 / 4.0 * 0.1, 0.1
COARSE_GAIN, COARSE_CAP = 0.5 / 16.0 * 0.05, 0.05
FINE_TAU, COARSE_TAU = 0.2, 0.4


def column_masks(chunks):
    lane = lax.broadcasted_iota(jnp.int32, (8, 128), 1)
    sub = lax.broadcasted_iota(jnp.int32, (8, 128), 0)
    left, right = lane == 0, lane == 127
    return chunks, left, left & (sub == 0), right, right & (sub == 7)


def line_of(k):
    return (k % 2) * 8 + k // 2


def from_left(x, masks, fill):
    chunks, edge, border, _, _ = masks
    a = pltpu.roll(x, 1, axis=2)
    if chunks == CCH:
        return jnp.where(border[None], fill, jnp.where(edge[None], pltpu.roll(a, 1, axis=1), a))
    even, odd = a[:, :8], a[:, 8:]
    if not isinstance(fill, float):
        fill = fill[:, :8]
    first = jnp.where(border[None], fill, jnp.where(edge[None], pltpu.roll(odd, 1, axis=1), even))
    return jnp.concatenate([first, jnp.where(edge[None], even, odd)], axis=1)


def from_right(x, masks, fill):
    chunks, _, _, edge, border = masks
    a = pltpu.roll(x, 127, axis=2)
    if chunks == CCH:
        return jnp.where(border[None], fill, jnp.where(edge[None], pltpu.roll(a, 7, axis=1), a))
    even, odd = a[:, :8], a[:, 8:]
    second = jnp.where(border[None], fill, jnp.where(edge[None], pltpu.roll(even, 7, axis=1), odd))
    return jnp.concatenate([jnp.where(edge[None], odd, even), second], axis=1)


def flow(h, s, g, c, ta, d, dy, lo, hi, masks, gain, cap, block, emit):
    for a in range(lo - 1, hi + 1, block):
        b = min(a + block, hi + 1)
        level = s[a:b]
        right = from_right(level, masks, 0.0)
        left = from_left(level, masks, 0.0)
        sx = s[a + 1 : b + 1] - s[a - 1 : b - 1]
        sy = right - left
        t = h[a:b]
        t2 = t * t
        fifth = t2 * t2 * t
        d[a:b] = jnp.minimum(fifth * gain * (sx * sx + sy * sy), cap)
        dy[a:b] = right - level
    for a in range(lo, hi, block):
        b = min(a + block, hi)
        dd = d[a - 1 : b + 1]
        ss = s[a - 1 : b + 1]
        fx = (dd[1:] + dd[:-1]) * (ss[1:] - ss[:-1])
        mid = dd[1:-1]
        fy = (mid + from_right(mid, masks, 0.0)) * dy[a:b]
        fy_left = from_left(fy, masks, mid * ss[1:-1])
        new = h[a:b] + (fx[1:] - fx[:-1] + fy - fy_left + ta[a:b])
        emit(a, b, jnp.maximum(new, 0.0) * c[a:b])


def split3(x):
    hi = x.astype(BF16)
    r = x - hi.astype(F32)
    mid = r.astype(BF16)
    lo = (r - mid.astype(F32)).astype(BF16)
    return hi, mid, lo


def times(x, m):
    parts = [jnp.dot(p, m, preferred_element_type=F32) for p in split3(x)]
    return parts[0] + (parts[1] + parts[2])


def restrict_mats():
    i = lax.broadcasted_iota(jnp.int32, (128, 128), 0)
    j = lax.broadcasted_iota(jnp.int32, (128, 128), 1)
    half = lax.shift_right_logical(i, 1)
    lo = jnp.where(j == half, 0.25, 0.0).astype(BF16)
    hi = jnp.where(j == half + 64, 0.25, 0.0).astype(BF16)
    return lo, hi


def prolong_mats():
    i = lax.broadcasted_iota(jnp.int32, (128, 128), 0)
    j = lax.broadcasted_iota(jnp.int32, (128, 128), 1)
    half = lax.shift_right_logical(j, 1)
    lo = jnp.where(i == half, 1.0, 0.0).astype(BF16)
    hi = jnp.where(i == half + 64, 1.0, 0.0).astype(BF16)
    return lo, hi


def restrict(x, mats):
    n = x.shape[0] // 2
    y = x.reshape(n, 2, CH, 128)
    y = y[:, 0] + y[:, 1]
    even, odd = y[:, :8].reshape(n * CCH, 128), y[:, 8:].reshape(n * CCH, 128)
    return (times(even, mats[0]) + times(odd, mats[1])).reshape(n, CCH, 128)


def look_up(index, table, size):
    values = [table[k] for k in range(size)]
    bit = 0
    while len(values) > 1:
        on = (lax.shift_right_logical(index, bit) & 1) == 1
        values = [jnp.where(on, values[k + 1], values[k]) for k in range(0, len(values), 2)]
        bit += 1
    return values[0]


EDGE = (8, 8, 6, 6)
EDGE_LINES = sum(EDGE) * CH
STATIC_LINES = 3 * CHALO * CCH
JUMPS = (12, 8, 4)
JUMP_LINES = sum(JUMPS) * CCH
H0, S0, G, C, TA = 0, 5, 9, 10, 11
KEPT = (0, 1, 2, 3, 4, 9, 10, 11)
CH0, CS0, CG, CC, CTA = 0, 2, 4, 5, 6


def fetch(pairs, sems):
    copies = [pltpu.make_async_copy(src, dst, sems.at[i]) for i, (src, dst) in enumerate(pairs)]
    for copy in copies:
        copy.start()
    return copies


def edge_kernel(space, thick, bed, mask, zone, levels, rates, off, inside, tv, bv, mv, zv, tab,
                lev, rat, hx, gx, cx, tx, sems):
    pairs = [(levels, lev), (rates, rat)]
    maps = ((bed, bv), (zone, zv), (thick, tv), (mask, mv))
    for r, count in ((0, 8), (ROWS - 8, 8), (8, ROWS - 16)):
        pairs += [(src.at[r : r + count], dst.at[r : r + count]) for src, dst in maps]
    copies = fetch(pairs, sems)
    for copy in copies[:10]:
        copy.wait()
    for k in range(16):
        tab[k : k + 1] = jnp.full((1, 128), lev[k], F32)
    for k in range(8):
        tab[16 + k : 17 + k] = jnp.full((1, 128), rat[k], F32)
    for half in range(2):
        r = slice(half * (ROWS - 8), half * (ROWS - 8) + 8)
        for k in range(CH):
            cols = slice(k * 128, k * 128 + 128)
            there = (half, pl.ds(line_of(k), 8, stride=CH), slice(None))
            hx[there] = tv[r, cols]
            gx[there] = look_up(bv[r, cols], lev, 16)
            cx[there] = mv[r, cols].astype(F32)
            tx[there] = look_up(zv[r, cols], rat, 8) * FINE_TAU
    odd = space[0] & 1
    at = 0
    for ref, count in zip((hx, gx, cx, tx), EDGE):
        n = count * CH
        skip = (8 - count) * CH
        off[at : at + n] = ref[odd, pl.ds(odd * skip, n)]
        inside[at : at + n] = ref[1 - odd, pl.ds((1 - odd) * skip, n)]
        at += n
    inside[at : at + 8] = jnp.zeros((8, 128), F32)
    for copy in copies[10:]:
        copy.wait()


def inner_kernel(space, tv, bv, mv, zv, tab, own, mid, rims, cstate, off, gl, cl, tl, state, d, dy):
    table = [jnp.broadcast_to(tab[k : k + 1], (8, 128)) for k in range(24)]
    lev, rat = table[:16], table[16:]
    for r in range(0, ROWS, 8):
        for k in range(CH):
            here = (slice(r, r + 8), slice(k * 128, k * 128 + 128))
            there = (pl.ds(r * CH + line_of(k), 8, stride=CH), slice(None))
            own[there] = tv[here]
            gl[there] = look_up(bv[here], lev, 16)
            cl[there] = mv[here].astype(F32)
            tl[there] = look_up(zv[here], rat, 8) * FINE_TAU
    mats = restrict_mats()
    mine = slice(HALO, HALO + ROWS)
    ratio = COARSE_TAU / FINE_TAU
    odd = space[0] & 1
    n = CHALO * CCH
    coarse = {}
    for ref, slot, cslot in ((own, H0, CH0), (gl, G, CG), (cl, C, CC), (tl, TA, CTA)):
        fine = ref[...].reshape(ROWS, CH, 128)
        state[slot, mine] = fine
        value = restrict(fine, mats)
        coarse[cslot] = value * ratio if cslot == CTA else value
        cstate[cslot, 4:20] = coarse[cslot]
    cstate[CS0, 4:20] = coarse[CG] + coarse[CH0]
    state[S0, mine] = state[G, mine] + state[H0, mine]
    for at, cslot in enumerate((CG, CC, CTA)):
        off[at * n : at * n + n] = cstate[cslot, pl.ds(4 + odd * (CROWS - CHALO), CHALO)].reshape(n, 128)
    coarse_steps(cstate, d, dy, ((6, 18), (8, 16)))
    fine_steps(state, d, dy, [(HALO + 2 * k, WIN - HALO - 2 * k) for k in (1, 2, 3, 4)])
    mid[...] = state[H0 + 4, 2 * HALO : WIN - 2 * HALO].reshape(16 * CH, 128)
    for at, slot in enumerate(KEPT):
        rims[at, 0:RIM] = state[slot, HALO : HALO + RIM]
        rims[at, RIM:] = state[slot, WIN - HALO - RIM : WIN - HALO]


def coarse_steps(cstate, d, dy, spans):
    masks = column_masks(CCH)
    cd, cdy = d.at[0:24, 0:CCH], dy.at[0:24, 0:CCH]
    for step, (lo, hi) in enumerate(spans):

        def emit(a, b, value, step=step):
            if step == 0:
                cstate[CH0 + 1, a:b] = value
                cstate[CS0 + 1, a:b] = value + cstate[CG, a:b]
            else:
                cstate[CH0, a:b] = value

        flow(cstate.at[CH0 + step], cstate.at[CS0 + step], cstate.at[CG], cstate.at[CC], cstate.at[CTA], cd, cdy,
             lo, hi, masks, COARSE_GAIN, COARSE_CAP, 8, emit)


def fine_steps(state, d, dy, spans):
    masks = column_masks(CH)
    for step, (lo, hi) in enumerate(spans):

        def emit(a, b, value, step=step):
            state[H0 + step + 1, a:b] = value
            if step < 3:
                state[S0 + step + 1, a:b] = value + state[G, a:b]

        flow(state.at[H0 + step], state.at[S0 + step], state.at[G], state.at[C], state.at[TA], d, dy,
             lo, hi, masks, FINE_GAIN, FINE_CAP, 4, emit)


def outer_kernel(place, space, last, off, inside, mid, rims, cstate_in, end, prev, payload, state, cstate, d, dy):
    for at, slot in enumerate(KEPT):
        state[slot, HALO : HALO + RIM] = rims[at, 0:RIM]
        state[slot, WIN - HALO - RIM : WIN - HALO] = rims[at, RIM:]
    for rim in (slice(HALO, HALO + RIM), slice(WIN - HALO - RIM, WIN - HALO)):
        for step in range(4):
            state[S0 + step, rim] = state[H0 + step, rim] + state[G, rim]
    cstate[:, 4:20] = cstate_in[:, 4:20]
    odd = space[0] & 1
    at_border = (space[0] == 0) | (space[0] == last[0])
    at = 0
    for slot, count in zip((H0, G, C, TA), EDGE):
        n = count * CH
        far = jnp.where(at_border, 0.0, off[at : at + n]).reshape(count, CH, 128)
        near = inside[at : at + n].reshape(count, CH, 128)
        state[slot, HALO - count : HALO] = jnp.where(odd == 1, near, far)
        state[slot, HALO + ROWS : HALO + ROWS + count] = jnp.where(odd == 1, far, near)
        at += n
    mats = restrict_mats()
    ratio = COARSE_TAU / FINE_TAU
    for lo, clo in ((0, 0), (40, 20)):
        state[S0, lo : lo + 8] = state[G, lo : lo + 8] + state[H0, lo : lo + 8]
        ground = restrict(state[G, lo : lo + 8], mats)
        thick = restrict(state[H0, lo : lo + 8], mats)
        cstate[CG, clo : clo + 4] = ground
        cstate[CH0, clo : clo + 4] = thick
        cstate[CS0, clo : clo + 4] = ground + thick
    for lo, clo in ((4, 2), (40, 20)):
        cstate[CC, clo : clo + 2] = restrict(state[C, lo : lo + 4], mats)
        cstate[CTA, clo : clo + 2] = restrict(state[TA, lo : lo + 4], mats) * ratio
    coarse_steps(cstate, d, dy, ((2, 6), (4, 8)))
    coarse_steps(cstate, d, dy, ((18, 22), (16, 20)))
    prev[...] = cstate[CH0, 4:20].reshape(CROWS * CCH, 128)
    fine_steps(state, d, dy, [(2 * k, HALO + 2 * k) for k in (1, 2, 3, 4)])
    fine_steps(state, d, dy, [(WIN - HALO - 2 * k, WIN - 2 * k) for k in (1, 2, 3, 4)])
    end[0 : 8 * CH] = state[H0 + 4, 8:16].reshape(8 * CH, 128)
    end[8 * CH : 24 * CH] = mid[...]
    end[24 * CH : 32 * CH] = state[H0 + 4, 32:40].reshape(8 * CH, 128)
    value = restrict(end[...].reshape(ROWS, CH, 128), mats).reshape(CROWS * CCH, 128)
    payload[...] = value - jnp.where(place[0] == 0, 0.0, prev[...])


def pack_kernel(source, target):
    target[...] = source[...]


def gather_kernel(place, space, cstate, d1, d2, d3, base, j1, j2, off, inside):
    m = place[0]
    base[...] = jnp.where(m == 1, d1[...], jnp.where(m == 2, d2[...], d3[...]))
    j1[...] = jnp.where(m == 2, d1[...], d2[...])
    j2[...] = d1[...]
    odd = space[0] & 1
    at = 0
    for ref, count in zip((base, j1, j2), JUMPS):
        n = count * CCH
        skip = CROWS * CCH - n
        off[at : at + n] = ref[pl.ds(odd * skip, n)]
        inside[at : at + n] = ref[pl.ds((1 - odd) * skip, n)]
        at += n
    n = CHALO * CCH
    for cslot in (CG, CC, CTA):
        inside[at : at + n] = cstate[cslot, pl.ds(4 + (1 - odd) * (CROWS - CHALO), CHALO)].reshape(n, 128)
        at += n


def chain_kernel(place, space, last, own, cstate, end, prev, before, base, j1, j2, off, inside, soff,
                 out_hbm, nxt_hbm, h, s, s2, g, c, ta, d, dy, jump1, jump2, fix, now_m, fine, out, nxt, sems):
    m = place[0]
    odd = space[0] & 1
    at_border = (space[0] == 0) | (space[0] == last[0])
    bottom = CHALO + CROWS

    def window(ref, own, count, far_ref, at, skip):
        n = count * CCH
        far = jnp.where(at_border, 0.0, far_ref[at : at + n]).reshape(count, CCH, 128)
        near = inside[skip + at : skip + at + n].reshape(count, CCH, 128)
        ref[CHALO - count : CHALO] = jnp.where(odd == 1, near, far)
        ref[CHALO:bottom] = own
        ref[bottom : bottom + count] = jnp.where(odd == 1, far, near)
        return at + n

    @pl.when(m > 0)
    def _():
        at = 0
        for ref, slot in ((g, CG), (c, CC), (ta, CTA)):
            at = window(ref, cstate[slot, 4:20], CHALO, soff, at, JUMP_LINES)
        at = 0
        for ref, held, count in zip((h, jump1, jump2), (base, j1, j2), JUMPS):
            at = window(ref, held[...].reshape(CROWS, CCH, 128), count, off, at, 0)
        s[...] = g[...] + h[...]
        now_m[...] = h[CHALO:bottom]

    masks = column_masks(CCH)
    mats = restrict_mats()
    mine = slice(CHALO, bottom)
    fix[...] = jnp.zeros_like(fix)
    lo_mat, hi_mat = prolong_mats()

    def spread_out(value, field, target, target_hbm, first, keep=None):
        value = value.reshape(CROWS * CCH, 128)
        halves = [times(value, mat).reshape(CROWS, CCH, 128) for mat in (lo_mat, hi_mat)]
        wide = jnp.concatenate(halves, axis=1).reshape(CROWS, 1, CH, 128)
        total = (field[...].reshape(CROWS, 2, CH, 128) + wide).reshape(ROWS, CH, 128)
        if keep is not None:
            total = jnp.where(m == 0, keep, total)
        fine[...] = total.reshape(ROWS * CH, 128)
        copies = []
        for r in range(0, ROWS, 8):
            for k in range(CH):
                target[r : r + 8, k * 128 : k * 128 + 128] = fine[pl.ds(r * CH + line_of(k), 8, stride=CH), :]
            copy = pltpu.make_async_copy(target.at[r : r + 8], target_hbm.at[r : r + 8], sems.at[first + r // 8])
            copy.start()
            copies.append(copy)
        return copies

    edge = 0
    waits = []
    for k, jump in ((1, jump1), (2, jump2), (3, None)):
        if k == 3:
            coarse_before = restrict(before[...].reshape(ROWS, CH, 128), mats)
            waits += spread_out(now_m[...] - coarse_before, before, nxt, nxt_hbm, 0,
                                own[...].reshape(ROWS, CH, 128))
        first_edge = edge
        edge += 4

        @pl.when(m >= k)
        def _(k=k, jump=jump, first_edge=first_edge):
            for step, (now, later) in enumerate(((s, s2), (s2, s))):
                lo = first_edge + 2 * (step + 1)

                def emit(a, b, value, later=later):
                    h[a:b] = value
                    later[a:b] = value + g[a:b]

                flow(h, now, g, c, ta, d, dy, lo, CWIN - lo, masks, COARSE_GAIN, COARSE_CAP, 8, emit)

            @pl.when(m == k)
            def _():
                fix[...] = h[mine] - prev[...].reshape(CROWS, CCH, 128)

            if jump is not None:
                lo = first_edge + 4
                for a in range(lo, CWIN - lo, 8):
                    b = min(a + 8, CWIN - lo)
                    value = h[a:b] + jump[a:b]
                    h[a:b] = value
                    s[a:b] = value + g[a:b]

                @pl.when(m == k + 1)
                def _():
                    now_m[...] = h[mine]

    waits += spread_out(fix[...], end, out, out_hbm, 4)
    for copy in waits:
        copy.wait()


def lines(n):
    return jax.ShapeDtypeStruct((n, 128), F32)


VMEM, SMEM, HBM = pltpu.VMEM, pltpu.SMEM, pltpu.HBM


def call(kernel, name, ins, outs, scratch=(), in_spaces=None, out_space=VMEM, limit=16):
    spaces = {"s": SMEM, "h": HBM, "v": VMEM}
    return pl.pallas_call(
        kernel,
        out_shape=outs,
        in_specs=[pl.BlockSpec(memory_space=spaces[letter]) for letter in in_spaces],
        out_specs=[pl.BlockSpec(memory_space=out_space)] * len(outs),
        scratch_shapes=[pltpu.VMEM(item, F32) if isinstance(item, tuple) else item for item in scratch],
        compiler_params=pltpu.CompilerParams(vmem_limit_bytes=limit * 2**20),
        name=name,
    )(*ins)


def shifted(x, by):
    devices = lax.axis_size("tm")
    return lax.ppermute(x, "tm", [(i, (i + by) % devices) for i in range(devices)])


def far_swap(x):
    slices, devices = lax.axis_size("tm"), lax.axis_size("space")
    pairs = [(m * devices + i, m * devices + i + 1) for m in range(slices) for i in range(1, devices - 1, 2)]
    pairs += [(m * devices + i, (m + 1) * devices + i) for m in range(0, slices, 2) for i in (0, devices - 1)]
    return lax.ppermute(x, ("tm", "space"), pairs + [(j, i) for i, j in pairs])


def far_swap_later(x):
    slices, devices = lax.axis_size("tm"), lax.axis_size("space")
    pairs = [(m * devices + i, m * devices + i + 1) for m in range(1, slices) for i in range(1, devices - 1, 2)]
    pairs += [(i, i + 1) for i in range(0, devices, 2)]
    ring = [(m * devices + i, (m % (slices - 1) + 1) * devices + i) for m in range(1, slices) for i in (0, devices - 1)]
    return lax.ppermute(x, ("tm", "space"), pairs + [(j, i) for i, j in pairs] + ring)


def near_swap(x):
    devices = lax.axis_size("space")
    return lax.ppermute(x, "space", [(i, i ^ 1) for i in range(devices)])


def per_device(thickness, bed_class, ice_mask, zone_index, bed_levels, balance_rates):
    place = lax.axis_index("tm").astype(jnp.int32).reshape(1)
    space = lax.axis_index("space").astype(jnp.int32).reshape(1)
    last = jnp.full((1,), lax.axis_size("space") - 1, jnp.int32)
    raw = (space,) + tuple(
        pltpu.with_memory_space_constraint(x, HBM)
        for x in (thickness[0], bed_class, ice_mask, zone_index, bed_levels, balance_rates)
    )
    coarse_lines = CROWS * CCH
    tables = [pltpu.SMEM((16,), F32), pltpu.SMEM((8,), F32)]
    maps = [jax.ShapeDtypeStruct((ROWS, CH * 128), t) for t in (F32, jnp.int32, jnp.int32, jnp.int32)]
    maps.append(lines(24))
    off, inside, *maps = call(
        edge_kernel, "edges", raw, [lines(EDGE_LINES), lines(EDGE_LINES + 8)] + maps,
        tables + [(2, 8 * CH, 128)] * 4 + [pltpu.SemaphoreType.DMA((14,))],
        "shhhhhh",
    )
    off, inside = far_swap(off), near_swap(inside)
    own, mid, rims, cstate, soff = call(
        inner_kernel, "inner", (space, *maps),
        [lines(ROWS * CH), lines(16 * CH), jax.ShapeDtypeStruct((len(KEPT), 2 * RIM, CH, 128), F32)]
        + [jax.ShapeDtypeStruct((7, 24, CCH, 128), F32)] + [lines(STATIC_LINES)],
        [(ROWS * CH, 128)] * 3 + [(12, WIN, CH, 128)] + [(WIN, CH, 128)] * 2,
        "svvvvv",
    )
    end, prev, payload = call(
        outer_kernel, "outer", (place, space, last, off, inside, mid, rims, cstate),
        [lines(ROWS * CH)] + [lines(coarse_lines)] * 2,
        [(12, WIN, CH, 128), (7, 24, CCH, 128)] + [(WIN, CH, 128)] * 2,
        "sssvvvvv",
    )
    soff = far_swap_later(soff)
    d1, d2, d3 = (shifted(payload, k) for k in (1, 2, 3))
    d1, d2, d3, soff = lax.optimization_barrier((d1, d2, d3, soff))
    base, j1, j2, off, inside = call(
        gather_kernel, "gather", (place, space, cstate, d1, d2, d3),
        [lines(coarse_lines)] * 3 + [lines(JUMP_LINES), lines(JUMP_LINES + STATIC_LINES)], (), "ssvvvv",
    )
    before = shifted(end, 1)
    off, inside = far_swap_later(off), near_swap(inside)
    out, nxt = call(
        chain_kernel, "chain",
        (place, space, last, own, cstate, end, prev, before, base, j1, j2, off, inside, soff),
        [jax.ShapeDtypeStruct((ROWS, CH * 128), F32)] * 2,
        [(CWIN, CCH, 128)] * 10 + [(CROWS, CCH, 128)] * 2 + [(ROWS * CH, 128)]
        + [(ROWS, CH * 128)] * 2 + [pltpu.SemaphoreType.DMA((8,))],
        "sss" + "v" * 11, out_space=HBM,
    )
    return out[None], nxt[None]


def solution(mesh):
    placed = (
        P("tm", "space", None),
        P("space", None),
        P("space", None),
        P("space", None),
        P(),
        P(),
    )
    return jax.shard_map(
        per_device,
        mesh=mesh,
        in_specs=placed,
        out_specs=(P("tm", "space", None), P("tm", "space", None)),
        check_vma=False,
    )
```

```python
import jax
import jax.numpy as jnp
from jax import lax
from jax.experimental import pallas as pl
from jax.experimental.pallas import tpu as pltpu
from jax.sharding import PartitionSpec as P

ROWS = 32
CH = 16
CROWS = ROWS // 2
CCH = CH // 2
HALO = 8
WIN = ROWS + 2 * HALO
RIM = 10
CHALO = 12
CWIN = CROWS + 2 * CHALO
F32 = jnp.float32
BF16 = jnp.bfloat16

FINE_GAIN, FINE_CAP = 0.5 / 4.0 * 0.1, 0.1
COARSE_GAIN, COARSE_CAP = 0.5 / 16.0 * 0.05, 0.05
FINE_TAU, COARSE_TAU = 0.2, 0.4


def column_masks(chunks):
    lane = lax.broadcasted_iota(jnp.int32, (8, 128), 1)
    sub = lax.broadcasted_iota(jnp.int32, (8, 128), 0)
    left, right = lane == 0, lane == 127
    return chunks, left, left & (sub == 0), right, right & (sub == 7)


def line_of(k):
    return (k % 2) * 8 + k // 2


def from_left(x, masks, fill):
    chunks, edge, border, _, _ = masks
    a = pltpu.roll(x, 1, axis=2)
    if chunks == CCH:
        return jnp.where(border[None], fill, jnp.where(edge[None], pltpu.roll(a, 1, axis=1), a))
    even, odd = a[:, :8], a[:, 8:]
    if not isinstance(fill, float):
        fill = fill[:, :8]
    first = jnp.where(border[None], fill, jnp.where(edge[None], pltpu.roll(odd, 1, axis=1), even))
    return jnp.concatenate([first, jnp.where(edge[None], even, odd)], axis=1)


def from_right(x, masks, fill):
    chunks, _, _, edge, border = masks
    a = pltpu.roll(x, 127, axis=2)
    if chunks == CCH:
        return jnp.where(border[None], fill, jnp.where(edge[None], pltpu.roll(a, 7, axis=1), a))
    even, odd = a[:, :8], a[:, 8:]
    second = jnp.where(border[None], fill, jnp.where(edge[None], pltpu.roll(even, 7, axis=1), odd))
    return jnp.concatenate([jnp.where(edge[None], odd, even), second], axis=1)


def flow(h, s, g, c, ta, d, dy, lo, hi, masks, gain, cap, block, emit):
    for a in range(lo - 1, hi + 1, block):
        b = min(a + block, hi + 1)
        level = s[a:b]
        right = from_right(level, masks, 0.0)
        left = from_left(level, masks, 0.0)
        sx = s[a + 1 : b + 1] - s[a - 1 : b - 1]
        sy = right - left
        t = h[a:b]
        t2 = t * t
        fifth = t2 * t2 * t
        d[a:b] = jnp.minimum(fifth * gain * (sx * sx + sy * sy), cap)
        dy[a:b] = right - level
    for a in range(lo, hi, block):
        b = min(a + block, hi)
        dd = d[a - 1 : b + 1]
        ss = s[a - 1 : b + 1]
        fx = (dd[1:] + dd[:-1]) * (ss[1:] - ss[:-1])
        mid = dd[1:-1]
        fy = (mid + from_right(mid, masks, 0.0)) * dy[a:b]
        fy_left = from_left(fy, masks, mid * ss[1:-1])
        new = h[a:b] + (fx[1:] - fx[:-1] + fy - fy_left + ta[a:b])
        emit(a, b, jnp.maximum(new, 0.0) * c[a:b])


def split3(x):
    hi = x.astype(BF16)
    r = x - hi.astype(F32)
    mid = r.astype(BF16)
    lo = (r - mid.astype(F32)).astype(BF16)
    return hi, mid, lo


def times(x, m):
    parts = [jnp.dot(p, m, preferred_element_type=F32) for p in split3(x)]
    return parts[0] + (parts[1] + parts[2])


def restrict_mats():
    i = lax.broadcasted_iota(jnp.int32, (128, 128), 0)
    j = lax.broadcasted_iota(jnp.int32, (128, 128), 1)
    half = lax.shift_right_logical(i, 1)
    lo = jnp.where(j == half, 0.25, 0.0).astype(BF16)
    hi = jnp.where(j == half + 64, 0.25, 0.0).astype(BF16)
    return lo, hi


def prolong_mats():
    i = lax.broadcasted_iota(jnp.int32, (128, 128), 0)
    j = lax.broadcasted_iota(jnp.int32, (128, 128), 1)
    half = lax.shift_right_logical(j, 1)
    lo = jnp.where(i == half, 1.0, 0.0).astype(BF16)
    hi = jnp.where(i == half + 64, 1.0, 0.0).astype(BF16)
    return lo, hi


def restrict(x, mats):
    n = x.shape[0] // 2
    y = x.reshape(n, 2, CH, 128)
    y = y[:, 0] + y[:, 1]
    even, odd = y[:, :8].reshape(n * CCH, 128), y[:, 8:].reshape(n * CCH, 128)
    return (times(even, mats[0]) + times(odd, mats[1])).reshape(n, CCH, 128)


def look_up(index, table, size):
    values = [table[k] for k in range(size)]
    bit = 0
    while len(values) > 1:
        on = (lax.shift_right_logical(index, bit) & 1) == 1
        values = [jnp.where(on, values[k + 1], values[k]) for k in range(0, len(values), 2)]
        bit += 1
    return values[0]


EDGE = (8, 8, 6, 6)
EDGE_LINES = sum(EDGE) * CH
STATIC_LINES = 3 * CHALO * CCH
JUMPS = (12, 8, 4)
JUMP_LINES = sum(JUMPS) * CCH
H0, S0, G, C, TA = 0, 5, 9, 10, 11
KEPT = (0, 1, 2, 3, 4, 9, 10, 11)
CH0, CS0, CG, CC, CTA = 0, 2, 4, 5, 6


def fetch(pairs, sems):
    copies = [pltpu.make_async_copy(src, dst, sems.at[i]) for i, (src, dst) in enumerate(pairs)]
    for copy in copies:
        copy.start()
    return copies


def edge_kernel(space, thick, bed, mask, zone, levels, rates, off, inside, tv, bv, mv, zv, tab,
                lev, rat, hx, gx, cx, tx, sems):
    pairs = [(levels, lev), (rates, rat)]
    maps = ((bed, bv), (zone, zv), (thick, tv), (mask, mv))
    for r, count in ((0, 8), (ROWS - 8, 8), (8, ROWS - 16)):
        pairs += [(src.at[r : r + count], dst.at[r : r + count]) for src, dst in maps]
    copies = fetch(pairs, sems)
    for copy in copies[:10]:
        copy.wait()
    for k in range(16):
        tab[k : k + 1] = jnp.full((1, 128), lev[k], F32)
    for k in range(8):
        tab[16 + k : 17 + k] = jnp.full((1, 128), rat[k], F32)
    for half in range(2):
        r = slice(half * (ROWS - 8), half * (ROWS - 8) + 8)
        for k in range(CH):
            cols = slice(k * 128, k * 128 + 128)
            there = (half, pl.ds(line_of(k), 8, stride=CH), slice(None))
            hx[there] = tv[r, cols]
            gx[there] = look_up(bv[r, cols], lev, 16)
            cx[there] = mv[r, cols].astype(F32)
            tx[there] = look_up(zv[r, cols], rat, 8) * FINE_TAU
    odd = space[0] & 1
    at = 0
    for ref, count in zip((hx, gx, cx, tx), EDGE):
        n = count * CH
        skip = (8 - count) * CH
        off[at : at + n] = ref[odd, pl.ds(odd * skip, n)]
        inside[at : at + n] = ref[1 - odd, pl.ds((1 - odd) * skip, n)]
        at += n
    inside[at : at + 8] = jnp.zeros((8, 128), F32)
    for copy in copies[10:]:
        copy.wait()


def inner_kernel(space, tv, bv, mv, zv, tab, own, mid, rims, cstate, off, gl, cl, tl, state, d, dy):
    table = [jnp.broadcast_to(tab[k : k + 1], (8, 128)) for k in range(24)]
    lev, rat = table[:16], table[16:]
    for r in range(0, ROWS, 8):
        for k in range(CH):
            here = (slice(r, r + 8), slice(k * 128, k * 128 + 128))
            there = (pl.ds(r * CH + line_of(k), 8, stride=CH), slice(None))
            own[there] = tv[here]
            gl[there] = look_up(bv[here], lev, 16)
            cl[there] = mv[here].astype(F32)
            tl[there] = look_up(zv[here], rat, 8) * FINE_TAU
    mats = restrict_mats()
    mine = slice(HALO, HALO + ROWS)
    ratio = COARSE_TAU / FINE_TAU
    odd = space[0] & 1
    n = CHALO * CCH
    coarse = {}
    for ref, slot, cslot in ((own, H0, CH0), (gl, G, CG), (cl, C, CC), (tl, TA, CTA)):
        fine = ref[...].reshape(ROWS, CH, 128)
        state[slot, mine] = fine
        value = restrict(fine, mats)
        coarse[cslot] = value * ratio if cslot == CTA else value
        cstate[cslot, 4:20] = coarse[cslot]
    cstate[CS0, 4:20] = coarse[CG] + coarse[CH0]
    state[S0, mine] = state[G, mine] + state[H0, mine]
    for at, cslot in enumerate((CG, CC, CTA)):
        off[at * n : at * n + n] = cstate[cslot, pl.ds(4 + odd * (CROWS - CHALO), CHALO)].reshape(n, 128)
    coarse_steps(cstate, d, dy, ((6, 18), (8, 16)))
    fine_steps(state, d, dy, [(HALO + 2 * k, WIN - HALO - 2 * k) for k in (1, 2, 3, 4)])
    mid[...] = state[H0 + 4, 2 * HALO : WIN - 2 * HALO].reshape(16 * CH, 128)
    for at, slot in enumerate(KEPT):
        rims[at, 0:RIM] = state[slot, HALO : HALO + RIM]
        rims[at, RIM:] = state[slot, WIN - HALO - RIM : WIN - HALO]


def coarse_steps(cstate, d, dy, spans):
    masks = column_masks(CCH)
    cd, cdy = d.at[0:24, 0:CCH], dy.at[0:24, 0:CCH]
    for step, (lo, hi) in enumerate(spans):

        def emit(a, b, value, step=step):
            if step == 0:
                cstate[CH0 + 1, a:b] = value
                cstate[CS0 + 1, a:b] = value + cstate[CG, a:b]
            else:
                cstate[CH0, a:b] = value

        flow(cstate.at[CH0 + step], cstate.at[CS0 + step], cstate.at[CG], cstate.at[CC], cstate.at[CTA], cd, cdy,
             lo, hi, masks, COARSE_GAIN, COARSE_CAP, 8, emit)


def fine_steps(state, d, dy, spans):
    masks = column_masks(CH)
    for step, (lo, hi) in enumerate(spans):

        def emit(a, b, value, step=step):
            state[H0 + step + 1, a:b] = value
            if step < 3:
                state[S0 + step + 1, a:b] = value + state[G, a:b]

        flow(state.at[H0 + step], state.at[S0 + step], state.at[G], state.at[C], state.at[TA], d, dy,
             lo, hi, masks, FINE_GAIN, FINE_CAP, 4, emit)


def outer_kernel(place, space, last, off, inside, mid, rims, cstate_in, end, prev, payload, state, cstate, d, dy):
    for at, slot in enumerate(KEPT):
        state[slot, HALO : HALO + RIM] = rims[at, 0:RIM]
        state[slot, WIN - HALO - RIM : WIN - HALO] = rims[at, RIM:]
    for rim in (slice(HALO, HALO + RIM), slice(WIN - HALO - RIM, WIN - HALO)):
        for step in range(4):
            state[S0 + step, rim] = state[H0 + step, rim] + state[G, rim]
    cstate[:, 4:20] = cstate_in[:, 4:20]
    odd = space[0] & 1
    at_border = (space[0] == 0) | (space[0] == last[0])
    at = 0
    for slot, count in zip((H0, G, C, TA), EDGE):
        n = count * CH
        far = jnp.where(at_border, 0.0, off[at : at + n]).reshape(count, CH, 128)
        near = inside[at : at + n].reshape(count, CH, 128)
        state[slot, HALO - count : HALO] = jnp.where(odd == 1, near, far)
        state[slot, HALO + ROWS : HALO + ROWS + count] = jnp.where(odd == 1, far, near)
        at += n
    mats = restrict_mats()
    ratio = COARSE_TAU / FINE_TAU
    for lo, clo in ((0, 0), (40, 20)):
        state[S0, lo : lo + 8] = state[G, lo : lo + 8] + state[H0, lo : lo + 8]
        ground = restrict(state[G, lo : lo + 8], mats)
        thick = restrict(state[H0, lo : lo + 8], mats)
        cstate[CG, clo : clo + 4] = ground
        cstate[CH0, clo : clo + 4] = thick
        cstate[CS0, clo : clo + 4] = ground + thick
    for lo, clo in ((4, 2), (40, 20)):
        cstate[CC, clo : clo + 2] = restrict(state[C, lo : lo + 4], mats)
        cstate[CTA, clo : clo + 2] = restrict(state[TA, lo : lo + 4], mats) * ratio
    coarse_steps(cstate, d, dy, ((2, 6), (4, 8)))
    coarse_steps(cstate, d, dy, ((18, 22), (16, 20)))
    prev[...] = cstate[CH0, 4:20].reshape(CROWS * CCH, 128)
    fine_steps(state, d, dy, [(2 * k, HALO + 2 * k) for k in (1, 2, 3, 4)])
    fine_steps(state, d, dy, [(WIN - HALO - 2 * k, WIN - 2 * k) for k in (1, 2, 3, 4)])
    end[0 : 8 * CH] = state[H0 + 4, 8:16].reshape(8 * CH, 128)
    end[8 * CH : 24 * CH] = mid[...]
    end[24 * CH : 32 * CH] = state[H0 + 4, 32:40].reshape(8 * CH, 128)
    value = restrict(end[...].reshape(ROWS, CH, 128), mats).reshape(CROWS * CCH, 128)
    payload[...] = value - jnp.where(place[0] == 0, 0.0, prev[...])


def pack_kernel(source, target):
    target[...] = source[...]


def gather_kernel(place, space, cstate, near1, near2, far, base, j1, j2, off, inside):
    m = place[0]
    base[...] = jnp.where(m == 1, near1[...], jnp.where(m == 2, near2[...], far[...]))
    j1[...] = jnp.where(m == 2, far[...], near2[...])
    j2[...] = near1[...]
    odd = space[0] & 1
    at = 0
    for ref, count in zip((base, j1, j2), JUMPS):
        n = count * CCH
        skip = CROWS * CCH - n
        off[at : at + n] = ref[pl.ds(odd * skip, n)]
        inside[at : at + n] = ref[pl.ds((1 - odd) * skip, n)]
        at += n
    n = CHALO * CCH
    for cslot in (CG, CC, CTA):
        inside[at : at + n] = cstate[cslot, pl.ds(4 + (1 - odd) * (CROWS - CHALO), CHALO)].reshape(n, 128)
        at += n


def chain_kernel(place, space, last, own, cstate, end, prev, before, base, j1, j2, off, inside, soff,
                 out_hbm, nxt_hbm, h, s, s2, g, c, ta, d, dy, jump1, jump2, fix, now_m, fine, out, nxt, sems):
    m = place[0]
    odd = space[0] & 1
    at_border = (space[0] == 0) | (space[0] == last[0])
    bottom = CHALO + CROWS

    def window(ref, own, count, far_ref, at, skip):
        n = count * CCH
        far = jnp.where(at_border, 0.0, far_ref[at : at + n]).reshape(count, CCH, 128)
        near = inside[skip + at : skip + at + n].reshape(count, CCH, 128)
        ref[CHALO - count : CHALO] = jnp.where(odd == 1, near, far)
        ref[CHALO:bottom] = own
        ref[bottom : bottom + count] = jnp.where(odd == 1, far, near)
        return at + n

    @pl.when(m > 0)
    def _():
        at = 0
        for ref, slot in ((g, CG), (c, CC), (ta, CTA)):
            at = window(ref, cstate[slot, 4:20], CHALO, soff, at, JUMP_LINES)
        at = 0
        for ref, held, count in zip((h, jump1, jump2), (base, j1, j2), JUMPS):
            at = window(ref, held[...].reshape(CROWS, CCH, 128), count, off, at, 0)
        s[...] = g[...] + h[...]
        now_m[...] = h[CHALO:bottom]

    masks = column_masks(CCH)
    mats = restrict_mats()
    mine = slice(CHALO, bottom)
    fix[...] = jnp.zeros_like(fix)
    lo_mat, hi_mat = prolong_mats()

    def spread_out(value, field, target, target_hbm, first, keep=None):
        value = value.reshape(CROWS * CCH, 128)
        halves = [times(value, mat).reshape(CROWS, CCH, 128) for mat in (lo_mat, hi_mat)]
        wide = jnp.concatenate(halves, axis=1).reshape(CROWS, 1, CH, 128)
        total = (field[...].reshape(CROWS, 2, CH, 128) + wide).reshape(ROWS, CH, 128)
        if keep is not None:
            total = jnp.where(m == 0, keep, total)
        fine[...] = total.reshape(ROWS * CH, 128)
        copies = []
        for r in range(0, ROWS, 8):
            for k in range(CH):
                target[r : r + 8, k * 128 : k * 128 + 128] = fine[pl.ds(r * CH + line_of(k), 8, stride=CH), :]
            copy = pltpu.make_async_copy(target.at[r : r + 8], target_hbm.at[r : r + 8], sems.at[first + r // 8])
            copy.start()
            copies.append(copy)
        return copies

    edge = 0
    waits = []
    for k, jump in ((1, jump1), (2, jump2), (3, None)):
        if k == 3:
            coarse_before = restrict(before[...].reshape(ROWS, CH, 128), mats)
            waits += spread_out(now_m[...] - coarse_before, before, nxt, nxt_hbm, 0,
                                own[...].reshape(ROWS, CH, 128))
        first_edge = edge
        edge += 4

        @pl.when(m >= k)
        def _(k=k, jump=jump, first_edge=first_edge):
            for step, (now, later) in enumerate(((s, s2), (s2, s))):
                lo = first_edge + 2 * (step + 1)

                def emit(a, b, value, later=later):
                    h[a:b] = value
                    later[a:b] = value + g[a:b]

                flow(h, now, g, c, ta, d, dy, lo, CWIN - lo, masks, COARSE_GAIN, COARSE_CAP, 8, emit)

            @pl.when(m == k)
            def _():
                fix[...] = h[mine] - prev[...].reshape(CROWS, CCH, 128)

            if jump is not None:
                lo = first_edge + 4
                for a in range(lo, CWIN - lo, 8):
                    b = min(a + 8, CWIN - lo)
                    value = h[a:b] + jump[a:b]
                    h[a:b] = value
                    s[a:b] = value + g[a:b]

                @pl.when(m == k + 1)
                def _():
                    now_m[...] = h[mine]

    waits += spread_out(fix[...], end, out, out_hbm, 4)
    for copy in waits:
        copy.wait()


def lines(n):
    return jax.ShapeDtypeStruct((n, 128), F32)


VMEM, SMEM, HBM = pltpu.VMEM, pltpu.SMEM, pltpu.HBM


def call(kernel, name, ins, outs, scratch=(), in_spaces=None, out_space=VMEM, limit=16):
    spaces = {"s": SMEM, "h": HBM, "v": VMEM}
    return pl.pallas_call(
        kernel,
        out_shape=outs,
        in_specs=[pl.BlockSpec(memory_space=spaces[letter]) for letter in in_spaces],
        out_specs=[pl.BlockSpec(memory_space=out_space)] * len(outs),
        scratch_shapes=[pltpu.VMEM(item, F32) if isinstance(item, tuple) else item for item in scratch],
        compiler_params=pltpu.CompilerParams(vmem_limit_bytes=limit * 2**20),
        name=name,
    )(*ins)


def shifted(x, by):
    devices = lax.axis_size("tm")
    return lax.ppermute(x, "tm", [(i, (i + by) % devices) for i in range(devices)])


def far_swap(x):
    slices, devices = lax.axis_size("tm"), lax.axis_size("space")
    pairs = [(m * devices + i, m * devices + i + 1) for m in range(slices) for i in range(1, devices - 1, 2)]
    pairs += [(m * devices + i, (m + 1) * devices + i) for m in range(0, slices, 2) for i in (0, devices - 1)]
    return lax.ppermute(x, ("tm", "space"), pairs + [(j, i) for i, j in pairs])


def far_swap_later(x):
    slices, devices = lax.axis_size("tm"), lax.axis_size("space")
    pairs = [(m * devices + i, m * devices + i + 1) for m in range(1, slices) for i in range(1, devices - 1, 2)]
    pairs += [(i, i + 1) for i in range(0, devices, 2)]
    ring = [(m * devices + i, (m % (slices - 1) + 1) * devices + i) for m in range(1, slices) for i in (0, devices - 1)]
    return lax.ppermute(x, ("tm", "space"), pairs + [(j, i) for i, j in pairs] + ring)


def near_swap(x):
    devices = lax.axis_size("space")
    return lax.ppermute(x, "space", [(i, i ^ 1) for i in range(devices)])


def per_device(thickness, bed_class, ice_mask, zone_index, bed_levels, balance_rates):
    place = lax.axis_index("tm").astype(jnp.int32).reshape(1)
    space = lax.axis_index("space").astype(jnp.int32).reshape(1)
    last = jnp.full((1,), lax.axis_size("space") - 1, jnp.int32)
    raw = (space,) + tuple(
        pltpu.with_memory_space_constraint(x, HBM)
        for x in (thickness[0], bed_class, ice_mask, zone_index, bed_levels, balance_rates)
    )
    coarse_lines = CROWS * CCH
    tables = [pltpu.SMEM((16,), F32), pltpu.SMEM((8,), F32)]
    maps = [jax.ShapeDtypeStruct((ROWS, CH * 128), t) for t in (F32, jnp.int32, jnp.int32, jnp.int32)]
    maps.append(lines(24))
    off, inside, *maps = call(
        edge_kernel, "edges", raw, [lines(EDGE_LINES), lines(EDGE_LINES + 8)] + maps,
        tables + [(2, 8 * CH, 128)] * 4 + [pltpu.SemaphoreType.DMA((14,))],
        "shhhhhh",
    )
    off, inside = far_swap(off), near_swap(inside)
    own, mid, rims, cstate, soff = call(
        inner_kernel, "inner", (space, *maps),
        [lines(ROWS * CH), lines(16 * CH), jax.ShapeDtypeStruct((len(KEPT), 2 * RIM, CH, 128), F32)]
        + [jax.ShapeDtypeStruct((7, 24, CCH, 128), F32)] + [lines(STATIC_LINES)],
        [(ROWS * CH, 128)] * 3 + [(12, WIN, CH, 128)] + [(WIN, CH, 128)] * 2,
        "svvvvv",
    )
    end, prev, payload = call(
        outer_kernel, "outer", (place, space, last, off, inside, mid, rims, cstate),
        [lines(ROWS * CH)] + [lines(coarse_lines)] * 2,
        [(12, WIN, CH, 128), (7, 24, CCH, 128)] + [(WIN, CH, 128)] * 2,
        "sssvvvvv",
    )
    soff = far_swap_later(soff)
    rounds = [lax.ppermute(payload, "tm", [(i, i ^ k) for i in range(lax.axis_size("tm"))]) for k in (1, 2, 3)]
    *rounds, soff = lax.optimization_barrier((*rounds, soff))
    base, j1, j2, off, inside = call(
        gather_kernel, "gather", (place, space, cstate, *rounds),
        [lines(coarse_lines)] * 3 + [lines(JUMP_LINES), lines(JUMP_LINES + STATIC_LINES)], (), "ssvvvv",
    )
    before = shifted(end, 1)
    off, inside = far_swap_later(off), near_swap(inside)
    out, nxt = call(
        chain_kernel, "chain",
        (place, space, last, own, cstate, end, prev, before, base, j1, j2, off, inside, soff),
        [jax.ShapeDtypeStruct((ROWS, CH * 128), F32)] * 2,
        [(CWIN, CCH, 128)] * 10 + [(CROWS, CCH, 128)] * 2 + [(ROWS * CH, 128)]
        + [(ROWS, CH * 128)] * 2 + [pltpu.SemaphoreType.DMA((8,))],
        "sss" + "v" * 11, out_space=HBM,
    )
    return out[None], nxt[None]


def solution(mesh):
    placed = (
        P("tm", "space", None),
        P("space", None),
        P("space", None),
        P("space", None),
        P(),
        P(),
    )
    return jax.shard_map(
        per_device,
        mesh=mesh,
        in_specs=placed,
        out_specs=(P("tm", "space", None), P("tm", "space", None)),
        check_vma=False,
    )
```

```python
import jax
import jax.numpy as jnp
from jax import lax
from jax.experimental import pallas as pl
from jax.experimental.pallas import tpu as pltpu
from jax.sharding import PartitionSpec as P

ROWS = 32
CH = 16
CROWS = ROWS // 2
CCH = CH // 2
HALO = 8
WIN = ROWS + 2 * HALO
RIM = 10
CHALO = 12
CWIN = CROWS + 2 * CHALO
F32 = jnp.float32
BF16 = jnp.bfloat16

FINE_GAIN, FINE_CAP = 0.5 / 4.0 * 0.1, 0.1
COARSE_GAIN, COARSE_CAP = 0.5 / 16.0 * 0.05, 0.05
FINE_TAU, COARSE_TAU = 0.2, 0.4


def column_masks(chunks):
    lane = lax.broadcasted_iota(jnp.int32, (8, 128), 1)
    sub = lax.broadcasted_iota(jnp.int32, (8, 128), 0)
    left, right = lane == 0, lane == 127
    return chunks, left, left & (sub == 0), right, right & (sub == 7)


def line_of(k):
    return (k % 2) * 8 + k // 2


def from_left(x, masks, fill):
    chunks, edge, border, _, _ = masks
    a = pltpu.roll(x, 1, axis=2)
    if chunks == CCH:
        return jnp.where(border[None], fill, jnp.where(edge[None], pltpu.roll(a, 1, axis=1), a))
    even, odd = a[:, :8], a[:, 8:]
    if not isinstance(fill, float):
        fill = fill[:, :8]
    first = jnp.where(border[None], fill, jnp.where(edge[None], pltpu.roll(odd, 1, axis=1), even))
    return jnp.concatenate([first, jnp.where(edge[None], even, odd)], axis=1)


def from_right(x, masks, fill):
    chunks, _, _, edge, border = masks
    a = pltpu.roll(x, 127, axis=2)
    if chunks == CCH:
        return jnp.where(border[None], fill, jnp.where(edge[None], pltpu.roll(a, 7, axis=1), a))
    even, odd = a[:, :8], a[:, 8:]
    second = jnp.where(border[None], fill, jnp.where(edge[None], pltpu.roll(even, 7, axis=1), odd))
    return jnp.concatenate([jnp.where(edge[None], odd, even), second], axis=1)


def flow(h, s, g, c, ta, d, dy, lo, hi, masks, gain, cap, block, emit):
    for a in range(lo - 1, hi + 1, block):
        b = min(a + block, hi + 1)
        level = s[a:b]
        right = from_right(level, masks, 0.0)
        left = from_left(level, masks, 0.0)
        sx = s[a + 1 : b + 1] - s[a - 1 : b - 1]
        sy = right - left
        t = h[a:b]
        t2 = t * t
        fifth = t2 * t2 * t
        d[a:b] = jnp.minimum(fifth * gain * (sx * sx + sy * sy), cap)
        dy[a:b] = right - level
    for a in range(lo, hi, block):
        b = min(a + block, hi)
        dd = d[a - 1 : b + 1]
        ss = s[a - 1 : b + 1]
        fx = (dd[1:] + dd[:-1]) * (ss[1:] - ss[:-1])
        mid = dd[1:-1]
        fy = (mid + from_right(mid, masks, 0.0)) * dy[a:b]
        fy_left = from_left(fy, masks, mid * ss[1:-1])
        new = h[a:b] + (fx[1:] - fx[:-1] + fy - fy_left + ta[a:b])
        emit(a, b, jnp.maximum(new, 0.0) * c[a:b])


def split3(x):
    hi = x.astype(BF16)
    r = x - hi.astype(F32)
    mid = r.astype(BF16)
    lo = (r - mid.astype(F32)).astype(BF16)
    return hi, mid, lo


def times(x, m):
    parts = [jnp.dot(p, m, preferred_element_type=F32) for p in split3(x)]
    return parts[0] + (parts[1] + parts[2])


def restrict_mats():
    i = lax.broadcasted_iota(jnp.int32, (128, 128), 0)
    j = lax.broadcasted_iota(jnp.int32, (128, 128), 1)
    half = lax.shift_right_logical(i, 1)
    lo = jnp.where(j == half, 0.25, 0.0).astype(BF16)
    hi = jnp.where(j == half + 64, 0.25, 0.0).astype(BF16)
    return lo, hi


def prolong_mats():
    i = lax.broadcasted_iota(jnp.int32, (128, 128), 0)
    j = lax.broadcasted_iota(jnp.int32, (128, 128), 1)
    half = lax.shift_right_logical(j, 1)
    lo = jnp.where(i == half, 1.0, 0.0).astype(BF16)
    hi = jnp.where(i == half + 64, 1.0, 0.0).astype(BF16)
    return lo, hi


def restrict(x, mats):
    n = x.shape[0] // 2
    y = x.reshape(n, 2, CH, 128)
    y = y[:, 0] + y[:, 1]
    even, odd = y[:, :8].reshape(n * CCH, 128), y[:, 8:].reshape(n * CCH, 128)
    return (times(even, mats[0]) + times(odd, mats[1])).reshape(n, CCH, 128)


def look_up(index, table, size):
    values = [table[k] for k in range(size)]
    bit = 0
    while len(values) > 1:
        on = (lax.shift_right_logical(index, bit) & 1) == 1
        values = [jnp.where(on, values[k + 1], values[k]) for k in range(0, len(values), 2)]
        bit += 1
    return values[0]


EDGE = (8, 8, 6, 6)
EDGE_LINES = sum(EDGE) * CH
STATIC_LINES = 3 * CHALO * CCH
JUMPS = (12, 8, 4)
JUMP_LINES = sum(JUMPS) * CCH
H0, S0, G, C, TA = 0, 5, 9, 10, 11
KEPT = (0, 1, 2, 3, 4, 9, 10, 11)
CH0, CS0, CG, CC, CTA = 0, 2, 4, 5, 6


def fetch(pairs, sems):
    copies = [pltpu.make_async_copy(src, dst, sems.at[i]) for i, (src, dst) in enumerate(pairs)]
    for copy in copies:
        copy.start()
    return copies


def edge_kernel(space, thick, bed, mask, zone, levels, rates, off, inside, tv, bv, mv, zv, tab,
                lev, rat, hx, gx, cx, tx, sems):
    pairs = [(levels, lev), (rates, rat)]
    maps = ((bed, bv), (zone, zv), (thick, tv), (mask, mv))
    for r, count in ((0, 8), (ROWS - 8, 8), (8, ROWS - 16)):
        pairs += [(src.at[r : r + count], dst.at[r : r + count]) for src, dst in maps]
    copies = fetch(pairs, sems)
    for copy in copies[:10]:
        copy.wait()
    for k in range(16):
        tab[k : k + 1] = jnp.full((1, 128), lev[k], F32)
    for k in range(8):
        tab[16 + k : 17 + k] = jnp.full((1, 128), rat[k], F32)
    for half in range(2):
        r = slice(half * (ROWS - 8), half * (ROWS - 8) + 8)
        for k in range(CH):
            cols = slice(k * 128, k * 128 + 128)
            there = (half, pl.ds(line_of(k), 8, stride=CH), slice(None))
            hx[there] = tv[r, cols]
            gx[there] = look_up(bv[r, cols], lev, 16)
            cx[there] = mv[r, cols].astype(F32)
            tx[there] = look_up(zv[r, cols], rat, 8) * FINE_TAU
    odd = space[0] & 1
    at = 0
    for ref, count in zip((hx, gx, cx, tx), EDGE):
        n = count * CH
        skip = (8 - count) * CH
        off[at : at + n] = ref[odd, pl.ds(odd * skip, n)]
        inside[at : at + n] = ref[1 - odd, pl.ds((1 - odd) * skip, n)]
        at += n
    inside[at : at + 8] = jnp.zeros((8, 128), F32)
    for copy in copies[10:]:
        copy.wait()


def inner_kernel(space, tv, bv, mv, zv, tab, own, mid, rims, cstate, off, gl, cl, tl, state, d, dy):
    table = [jnp.broadcast_to(tab[k : k + 1], (8, 128)) for k in range(24)]
    lev, rat = table[:16], table[16:]
    for r in range(0, ROWS, 8):
        for k in range(CH):
            here = (slice(r, r + 8), slice(k * 128, k * 128 + 128))
            there = (pl.ds(r * CH + line_of(k), 8, stride=CH), slice(None))
            own[there] = tv[here]
            gl[there] = look_up(bv[here], lev, 16)
            cl[there] = mv[here].astype(F32)
            tl[there] = look_up(zv[here], rat, 8) * FINE_TAU
    mats = restrict_mats()
    mine = slice(HALO, HALO + ROWS)
    ratio = COARSE_TAU / FINE_TAU
    odd = space[0] & 1
    n = CHALO * CCH
    coarse = {}
    for ref, slot, cslot in ((own, H0, CH0), (gl, G, CG), (cl, C, CC), (tl, TA, CTA)):
        fine = ref[...].reshape(ROWS, CH, 128)
        state[slot, mine] = fine
        value = restrict(fine, mats)
        coarse[cslot] = value * ratio if cslot == CTA else value
        cstate[cslot, 4:20] = coarse[cslot]
    cstate[CS0, 4:20] = coarse[CG] + coarse[CH0]
    state[S0, mine] = state[G, mine] + state[H0, mine]
    for at, cslot in enumerate((CG, CC, CTA)):
        off[at * n : at * n + n] = cstate[cslot, pl.ds(4 + odd * (CROWS - CHALO), CHALO)].reshape(n, 128)
    coarse_steps(cstate, d, dy, ((6, 18), (8, 16)))
    fine_steps(state, d, dy, [(HALO + 2 * k, WIN - HALO - 2 * k) for k in (1, 2, 3, 4)])
    mid[...] = state[H0 + 4, 2 * HALO : WIN - 2 * HALO].reshape(16 * CH, 128)
    for at, slot in enumerate(KEPT):
        rims[at, 0:RIM] = state[slot, HALO : HALO + RIM]
        rims[at, RIM:] = state[slot, WIN - HALO - RIM : WIN - HALO]


def coarse_steps(cstate, d, dy, spans):
    masks = column_masks(CCH)
    cd, cdy = d.at[0:24, 0:CCH], dy.at[0:24, 0:CCH]
    for step, (lo, hi) in enumerate(spans):

        def emit(a, b, value, step=step):
            if step == 0:
                cstate[CH0 + 1, a:b] = value
                cstate[CS0 + 1, a:b] = value + cstate[CG, a:b]
            else:
                cstate[CH0, a:b] = value

        flow(cstate.at[CH0 + step], cstate.at[CS0 + step], cstate.at[CG], cstate.at[CC], cstate.at[CTA], cd, cdy,
             lo, hi, masks, COARSE_GAIN, COARSE_CAP, 8, emit)


def fine_steps(state, d, dy, spans):
    masks = column_masks(CH)
    for step, (lo, hi) in enumerate(spans):

        def emit(a, b, value, step=step):
            state[H0 + step + 1, a:b] = value
            if step < 3:
                state[S0 + step + 1, a:b] = value + state[G, a:b]

        flow(state.at[H0 + step], state.at[S0 + step], state.at[G], state.at[C], state.at[TA], d, dy,
             lo, hi, masks, FINE_GAIN, FINE_CAP, 4, emit)


def outer_kernel(place, space, last, off, inside, mid, rims, cstate_in, end, prev, payload, state, cstate, d, dy):
    for at, slot in enumerate(KEPT):
        state[slot, HALO : HALO + RIM] = rims[at, 0:RIM]
        state[slot, WIN - HALO - RIM : WIN - HALO] = rims[at, RIM:]
    for rim in (slice(HALO, HALO + RIM), slice(WIN - HALO - RIM, WIN - HALO)):
        for step in range(4):
            state[S0 + step, rim] = state[H0 + step, rim] + state[G, rim]
    cstate[:, 4:20] = cstate_in[:, 4:20]
    odd = space[0] & 1
    at_border = (space[0] == 0) | (space[0] == last[0])
    at = 0
    for slot, count in zip((H0, G, C, TA), EDGE):
        n = count * CH
        far = jnp.where(at_border, 0.0, off[at : at + n]).reshape(count, CH, 128)
        near = inside[at : at + n].reshape(count, CH, 128)
        state[slot, HALO - count : HALO] = jnp.where(odd == 1, near, far)
        state[slot, HALO + ROWS : HALO + ROWS + count] = jnp.where(odd == 1, far, near)
        at += n
    mats = restrict_mats()
    ratio = COARSE_TAU / FINE_TAU
    for lo, clo in ((0, 0), (40, 20)):
        state[S0, lo : lo + 8] = state[G, lo : lo + 8] + state[H0, lo : lo + 8]
        ground = restrict(state[G, lo : lo + 8], mats)
        thick = restrict(state[H0, lo : lo + 8], mats)
        cstate[CG, clo : clo + 4] = ground
        cstate[CH0, clo : clo + 4] = thick
        cstate[CS0, clo : clo + 4] = ground + thick
    for lo, clo in ((4, 2), (40, 20)):
        cstate[CC, clo : clo + 2] = restrict(state[C, lo : lo + 4], mats)
        cstate[CTA, clo : clo + 2] = restrict(state[TA, lo : lo + 4], mats) * ratio
    coarse_steps(cstate, d, dy, ((2, 6), (4, 8)))
    coarse_steps(cstate, d, dy, ((18, 22), (16, 20)))
    prev[...] = cstate[CH0, 4:20].reshape(CROWS * CCH, 128)
    fine_steps(state, d, dy, [(2 * k, HALO + 2 * k) for k in (1, 2, 3, 4)])
    fine_steps(state, d, dy, [(WIN - HALO - 2 * k, WIN - 2 * k) for k in (1, 2, 3, 4)])
    end[0 : 8 * CH] = state[H0 + 4, 8:16].reshape(8 * CH, 128)
    end[8 * CH : 24 * CH] = mid[...]
    end[24 * CH : 32 * CH] = state[H0 + 4, 32:40].reshape(8 * CH, 128)
    value = restrict(end[...].reshape(ROWS, CH, 128), mats).reshape(CROWS * CCH, 128)
    payload[...] = value - jnp.where(place[0] == 0, 0.0, prev[...])


def pack_kernel(source, target):
    target[...] = source[...]


def gather_kernel(place, space, cstate, far, near2, near1, base, j1, j2, off, inside):
    m = place[0]
    base[...] = jnp.where(m == 1, near1[...], jnp.where(m == 2, near2[...], far[...]))
    j1[...] = jnp.where(m == 2, far[...], near2[...])
    j2[...] = near1[...]
    odd = space[0] & 1
    at = 0
    for ref, count in zip((base, j1, j2), JUMPS):
        n = count * CCH
        skip = CROWS * CCH - n
        off[at : at + n] = ref[pl.ds(odd * skip, n)]
        inside[at : at + n] = ref[pl.ds((1 - odd) * skip, n)]
        at += n
    n = CHALO * CCH
    for cslot in (CG, CC, CTA):
        inside[at : at + n] = cstate[cslot, pl.ds(4 + (1 - odd) * (CROWS - CHALO), CHALO)].reshape(n, 128)
        at += n


def chain_kernel(place, space, last, own, cstate, end, prev, before, base, j1, j2, off, inside, soff,
                 out_hbm, nxt_hbm, h, s, s2, g, c, ta, d, dy, jump1, jump2, fix, now_m, fine, out, nxt, sems):
    m = place[0]
    odd = space[0] & 1
    at_border = (space[0] == 0) | (space[0] == last[0])
    bottom = CHALO + CROWS

    def window(ref, own, count, far_ref, at, skip):
        n = count * CCH
        far = jnp.where(at_border, 0.0, far_ref[at : at + n]).reshape(count, CCH, 128)
        near = inside[skip + at : skip + at + n].reshape(count, CCH, 128)
        ref[CHALO - count : CHALO] = jnp.where(odd == 1, near, far)
        ref[CHALO:bottom] = own
        ref[bottom : bottom + count] = jnp.where(odd == 1, far, near)
        return at + n

    @pl.when(m > 0)
    def _():
        at = 0
        for ref, slot in ((g, CG), (c, CC), (ta, CTA)):
            at = window(ref, cstate[slot, 4:20], CHALO, soff, at, JUMP_LINES)
        at = 0
        for ref, held, count in zip((h, jump1, jump2), (base, j1, j2), JUMPS):
            at = window(ref, held[...].reshape(CROWS, CCH, 128), count, off, at, 0)
        s[...] = g[...] + h[...]
        now_m[...] = h[CHALO:bottom]

    masks = column_masks(CCH)
    mats = restrict_mats()
    mine = slice(CHALO, bottom)
    fix[...] = jnp.zeros_like(fix)
    lo_mat, hi_mat = prolong_mats()

    def spread_out(value, field, target, target_hbm, first, keep=None):
        value = value.reshape(CROWS * CCH, 128)
        halves = [times(value, mat).reshape(CROWS, CCH, 128) for mat in (lo_mat, hi_mat)]
        wide = jnp.concatenate(halves, axis=1).reshape(CROWS, 1, CH, 128)
        total = (field[...].reshape(CROWS, 2, CH, 128) + wide).reshape(ROWS, CH, 128)
        if keep is not None:
            total = jnp.where(m == 0, keep, total)
        fine[...] = total.reshape(ROWS * CH, 128)
        copies = []
        for r in range(0, ROWS, 8):
            for k in range(CH):
                target[r : r + 8, k * 128 : k * 128 + 128] = fine[pl.ds(r * CH + line_of(k), 8, stride=CH), :]
            copy = pltpu.make_async_copy(target.at[r : r + 8], target_hbm.at[r : r + 8], sems.at[first + r // 8])
            copy.start()
            copies.append(copy)
        return copies

    edge = 0
    waits = []
    for k, jump in ((1, jump1), (2, jump2), (3, None)):
        if k == 3:
            coarse_before = restrict(before[...].reshape(ROWS, CH, 128), mats)
            waits += spread_out(now_m[...] - coarse_before, before, nxt, nxt_hbm, 0,
                                own[...].reshape(ROWS, CH, 128))
        first_edge = edge
        edge += 4

        @pl.when(m >= k)
        def _(k=k, jump=jump, first_edge=first_edge):
            for step, (now, later) in enumerate(((s, s2), (s2, s))):
                lo = first_edge + 2 * (step + 1)

                def emit(a, b, value, later=later):
                    h[a:b] = value
                    later[a:b] = value + g[a:b]

                flow(h, now, g, c, ta, d, dy, lo, CWIN - lo, masks, COARSE_GAIN, COARSE_CAP, 8, emit)

            @pl.when(m == k)
            def _():
                fix[...] = h[mine] - prev[...].reshape(CROWS, CCH, 128)

            if jump is not None:
                lo = first_edge + 4
                for a in range(lo, CWIN - lo, 8):
                    b = min(a + 8, CWIN - lo)
                    value = h[a:b] + jump[a:b]
                    h[a:b] = value
                    s[a:b] = value + g[a:b]

                @pl.when(m == k + 1)
                def _():
                    now_m[...] = h[mine]

    waits += spread_out(fix[...], end, out, out_hbm, 4)
    for copy in waits:
        copy.wait()


def lines(n):
    return jax.ShapeDtypeStruct((n, 128), F32)


VMEM, SMEM, HBM = pltpu.VMEM, pltpu.SMEM, pltpu.HBM


def call(kernel, name, ins, outs, scratch=(), in_spaces=None, out_space=VMEM, limit=16):
    spaces = {"s": SMEM, "h": HBM, "v": VMEM}
    return pl.pallas_call(
        kernel,
        out_shape=outs,
        in_specs=[pl.BlockSpec(memory_space=spaces[letter]) for letter in in_spaces],
        out_specs=[pl.BlockSpec(memory_space=out_space)] * len(outs),
        scratch_shapes=[pltpu.VMEM(item, F32) if isinstance(item, tuple) else item for item in scratch],
        compiler_params=pltpu.CompilerParams(vmem_limit_bytes=limit * 2**20),
        name=name,
    )(*ins)


def shifted(x, by):
    devices = lax.axis_size("tm")
    return lax.ppermute(x, "tm", [(i, (i + by) % devices) for i in range(devices)])


def far_swap(x):
    slices, devices = lax.axis_size("tm"), lax.axis_size("space")
    pairs = [(m * devices + i, m * devices + i + 1) for m in range(slices) for i in range(1, devices - 1, 2)]
    pairs += [(m * devices + i, (m + 1) * devices + i) for m in range(0, slices, 2) for i in (0, devices - 1)]
    return lax.ppermute(x, ("tm", "space"), pairs + [(j, i) for i, j in pairs])


def far_swap_later(x):
    slices, devices = lax.axis_size("tm"), lax.axis_size("space")
    pairs = [(m * devices + i, m * devices + i + 1) for m in range(1, slices) for i in range(1, devices - 1, 2)]
    pairs += [(i, i + 1) for i in range(0, devices, 2)]
    ring = [(m * devices + i, (m % (slices - 1) + 1) * devices + i) for m in range(1, slices) for i in (0, devices - 1)]
    return lax.ppermute(x, ("tm", "space"), pairs + [(j, i) for i, j in pairs] + ring)


def near_swap(x):
    devices = lax.axis_size("space")
    return lax.ppermute(x, "space", [(i, i ^ 1) for i in range(devices)])


def per_device(thickness, bed_class, ice_mask, zone_index, bed_levels, balance_rates):
    place = lax.axis_index("tm").astype(jnp.int32).reshape(1)
    space = lax.axis_index("space").astype(jnp.int32).reshape(1)
    last = jnp.full((1,), lax.axis_size("space") - 1, jnp.int32)
    raw = (space,) + tuple(
        pltpu.with_memory_space_constraint(x, HBM)
        for x in (thickness[0], bed_class, ice_mask, zone_index, bed_levels, balance_rates)
    )
    coarse_lines = CROWS * CCH
    tables = [pltpu.SMEM((16,), F32), pltpu.SMEM((8,), F32)]
    maps = [jax.ShapeDtypeStruct((ROWS, CH * 128), t) for t in (F32, jnp.int32, jnp.int32, jnp.int32)]
    maps.append(lines(24))
    off, inside, *maps = call(
        edge_kernel, "edges", raw, [lines(EDGE_LINES), lines(EDGE_LINES + 8)] + maps,
        tables + [(2, 8 * CH, 128)] * 4 + [pltpu.SemaphoreType.DMA((14,))],
        "shhhhhh",
    )
    off, inside = far_swap(off), near_swap(inside)
    own, mid, rims, cstate, soff = call(
        inner_kernel, "inner", (space, *maps),
        [lines(ROWS * CH), lines(16 * CH), jax.ShapeDtypeStruct((len(KEPT), 2 * RIM, CH, 128), F32)]
        + [jax.ShapeDtypeStruct((7, 24, CCH, 128), F32)] + [lines(STATIC_LINES)],
        [(ROWS * CH, 128)] * 3 + [(12, WIN, CH, 128)] + [(WIN, CH, 128)] * 2,
        "svvvvv",
    )
    end, prev, payload = call(
        outer_kernel, "outer", (place, space, last, off, inside, mid, rims, cstate),
        [lines(ROWS * CH)] + [lines(coarse_lines)] * 2,
        [(12, WIN, CH, 128), (7, 24, CCH, 128)] + [(WIN, CH, 128)] * 2,
        "sssvvvvv",
    )
    soff = far_swap_later(soff)
    rounds = [lax.ppermute(payload, "tm", [(i, i ^ k) for i in range(lax.axis_size("tm"))]) for k in (3, 2, 1)]
    *rounds, soff = lax.optimization_barrier((*rounds, soff))
    base, j1, j2, off, inside = call(
        gather_kernel, "gather", (place, space, cstate, *rounds),
        [lines(coarse_lines)] * 3 + [lines(JUMP_LINES), lines(JUMP_LINES + STATIC_LINES)], (), "ssvvvv",
    )
    before = shifted(end, 1)
    off, inside = far_swap_later(off), near_swap(inside)
    out, nxt = call(
        chain_kernel, "chain",
        (place, space, last, own, cstate, end, prev, before, base, j1, j2, off, inside, soff),
        [jax.ShapeDtypeStruct((ROWS, CH * 128), F32)] * 2,
        [(CWIN, CCH, 128)] * 10 + [(CROWS, CCH, 128)] * 2 + [(ROWS * CH, 128)]
        + [(ROWS, CH * 128)] * 2 + [pltpu.SemaphoreType.DMA((8,))],
        "sss" + "v" * 11, out_space=HBM,
    )
    return out[None], nxt[None]


def solution(mesh):
    placed = (
        P("tm", "space", None),
        P("space", None),
        P("space", None),
        P("space", None),
        P(),
        P(),
    )
    return jax.shard_map(
        per_device,
        mesh=mesh,
        in_specs=placed,
        out_specs=(P("tm", "space", None), P("tm", "space", None)),
        check_vma=False,
    )
```

```python
import jax
import jax.numpy as jnp
from jax import lax
from jax.experimental import pallas as pl
from jax.experimental.pallas import tpu as pltpu
from jax.sharding import PartitionSpec as P

ROWS = 32
CH = 16
CROWS = ROWS // 2
CCH = CH // 2
HALO = 8
WIN = ROWS + 2 * HALO
RIM = 10
CHALO = 12
CWIN = CROWS + 2 * CHALO
F32 = jnp.float32
BF16 = jnp.bfloat16

FINE_GAIN, FINE_CAP = 0.5 / 4.0 * 0.1, 0.1
COARSE_GAIN, COARSE_CAP = 0.5 / 16.0 * 0.05, 0.05
FINE_TAU, COARSE_TAU = 0.2, 0.4


def column_masks(chunks):
    lane = lax.broadcasted_iota(jnp.int32, (8, 128), 1)
    sub = lax.broadcasted_iota(jnp.int32, (8, 128), 0)
    left, right = lane == 0, lane == 127
    return chunks, left, left & (sub == 0), right, right & (sub == 7)


def line_of(k):
    return (k % 2) * 8 + k // 2


def from_left(x, masks, fill):
    chunks, edge, border, _, _ = masks
    a = pltpu.roll(x, 1, axis=2)
    if chunks == CCH:
        return jnp.where(border[None], fill, jnp.where(edge[None], pltpu.roll(a, 1, axis=1), a))
    even, odd = a[:, :8], a[:, 8:]
    if not isinstance(fill, float):
        fill = fill[:, :8]
    first = jnp.where(border[None], fill, jnp.where(edge[None], pltpu.roll(odd, 1, axis=1), even))
    return jnp.concatenate([first, jnp.where(edge[None], even, odd)], axis=1)


def from_right(x, masks, fill):
    chunks, _, _, edge, border = masks
    a = pltpu.roll(x, 127, axis=2)
    if chunks == CCH:
        return jnp.where(border[None], fill, jnp.where(edge[None], pltpu.roll(a, 7, axis=1), a))
    even, odd = a[:, :8], a[:, 8:]
    second = jnp.where(border[None], fill, jnp.where(edge[None], pltpu.roll(even, 7, axis=1), odd))
    return jnp.concatenate([jnp.where(edge[None], odd, even), second], axis=1)


def flow(h, s, g, c, ta, d, dy, lo, hi, masks, gain, cap, block, emit):
    for a in range(lo - 1, hi + 1, block):
        b = min(a + block, hi + 1)
        level = s[a:b]
        right = from_right(level, masks, 0.0)
        left = from_left(level, masks, 0.0)
        sx = s[a + 1 : b + 1] - s[a - 1 : b - 1]
        sy = right - left
        t = h[a:b]
        t2 = t * t
        fifth = t2 * t2 * t
        d[a:b] = jnp.minimum(fifth * gain * (sx * sx + sy * sy), cap)
        dy[a:b] = right - level
    for a in range(lo, hi, block):
        b = min(a + block, hi)
        dd = d[a - 1 : b + 1]
        ss = s[a - 1 : b + 1]
        fx = (dd[1:] + dd[:-1]) * (ss[1:] - ss[:-1])
        mid = dd[1:-1]
        fy = (mid + from_right(mid, masks, 0.0)) * dy[a:b]
        fy_left = from_left(fy, masks, mid * ss[1:-1])
        new = h[a:b] + (fx[1:] - fx[:-1] + fy - fy_left + ta[a:b])
        emit(a, b, jnp.maximum(new, 0.0) * c[a:b])


def split3(x):
    hi = x.astype(BF16)
    r = x - hi.astype(F32)
    mid = r.astype(BF16)
    lo = (r - mid.astype(F32)).astype(BF16)
    return hi, mid, lo


def times(x, m):
    parts = [jnp.dot(p, m, preferred_element_type=F32) for p in split3(x)]
    return parts[0] + (parts[1] + parts[2])


def restrict_mats():
    i = lax.broadcasted_iota(jnp.int32, (128, 128), 0)
    j = lax.broadcasted_iota(jnp.int32, (128, 128), 1)
    half = lax.shift_right_logical(i, 1)
    lo = jnp.where(j == half, 0.25, 0.0).astype(BF16)
    hi = jnp.where(j == half + 64, 0.25, 0.0).astype(BF16)
    return lo, hi


def prolong_mats():
    i = lax.broadcasted_iota(jnp.int32, (128, 128), 0)
    j = lax.broadcasted_iota(jnp.int32, (128, 128), 1)
    half = lax.shift_right_logical(j, 1)
    lo = jnp.where(i == half, 1.0, 0.0).astype(BF16)
    hi = jnp.where(i == half + 64, 1.0, 0.0).astype(BF16)
    return lo, hi


def restrict(x, mats):
    n = x.shape[0] // 2
    y = x.reshape(n, 2, CH, 128)
    y = y[:, 0] + y[:, 1]
    even, odd = y[:, :8].reshape(n * CCH, 128), y[:, 8:].reshape(n * CCH, 128)
    return (times(even, mats[0]) + times(odd, mats[1])).reshape(n, CCH, 128)


def look_up(index, table, size):
    values = [table[k] for k in range(size)]
    bit = 0
    while len(values) > 1:
        on = (lax.shift_right_logical(index, bit) & 1) == 1
        values = [jnp.where(on, values[k + 1], values[k]) for k in range(0, len(values), 2)]
        bit += 1
    return values[0]


EDGE = (8, 8, 6, 6)
EDGE_LINES = sum(EDGE) * CH
STATIC_LINES = 3 * CHALO * CCH
JUMPS = (12, 8, 4)
JUMP_LINES = sum(JUMPS) * CCH
H0, S0, G, C, TA = 0, 5, 9, 10, 11
KEPT = (0, 1, 2, 3, 4, 9, 10, 11)
CH0, CS0, CG, CC, CTA = 0, 2, 4, 5, 6


def fetch(pairs, sems):
    copies = [pltpu.make_async_copy(src, dst, sems.at[i]) for i, (src, dst) in enumerate(pairs)]
    for copy in copies:
        copy.start()
    return copies


def edge_kernel(space, thick, bed, mask, zone, levels, rates, off, inside, tv, bv, mv, zv, tab,
                lev, rat, hx, gx, cx, tx, sems):
    pairs = [(levels, lev), (rates, rat)]
    maps = ((bed, bv), (zone, zv), (thick, tv), (mask, mv))
    for r, count in ((0, 8), (ROWS - 8, 8), (8, ROWS - 16)):
        pairs += [(src.at[r : r + count], dst.at[r : r + count]) for src, dst in maps]
    copies = fetch(pairs, sems)
    for copy in copies[:10]:
        copy.wait()
    for k in range(16):
        tab[k : k + 1] = jnp.full((1, 128), lev[k], F32)
    for k in range(8):
        tab[16 + k : 17 + k] = jnp.full((1, 128), rat[k], F32)
    for half in range(2):
        r = slice(half * (ROWS - 8), half * (ROWS - 8) + 8)
        for k in range(CH):
            cols = slice(k * 128, k * 128 + 128)
            there = (half, pl.ds(line_of(k), 8, stride=CH), slice(None))
            hx[there] = tv[r, cols]
            gx[there] = look_up(bv[r, cols], lev, 16)
            cx[there] = mv[r, cols].astype(F32)
            tx[there] = look_up(zv[r, cols], rat, 8) * FINE_TAU
    odd = space[0] & 1
    at = 0
    for ref, count in zip((hx, gx, cx, tx), EDGE):
        n = count * CH
        skip = (8 - count) * CH
        off[at : at + n] = ref[odd, pl.ds(odd * skip, n)]
        inside[at : at + n] = ref[1 - odd, pl.ds((1 - odd) * skip, n)]
        at += n
    for copy in copies[10:]:
        copy.wait()


def inner_kernel(space, tv, bv, mv, zv, tab, own, mid, rims, cstate, off, gl, cl, tl, state, d, dy):
    table = [jnp.broadcast_to(tab[k : k + 1], (8, 128)) for k in range(24)]
    lev, rat = table[:16], table[16:]
    for r in range(0, ROWS, 8):
        for k in range(CH):
            here = (slice(r, r + 8), slice(k * 128, k * 128 + 128))
            there = (pl.ds(r * CH + line_of(k), 8, stride=CH), slice(None))
            own[there] = tv[here]
            gl[there] = look_up(bv[here], lev, 16)
            cl[there] = mv[here].astype(F32)
            tl[there] = look_up(zv[here], rat, 8) * FINE_TAU
    mats = restrict_mats()
    mine = slice(HALO, HALO + ROWS)
    ratio = COARSE_TAU / FINE_TAU
    odd = space[0] & 1
    n = CHALO * CCH
    coarse = {}
    for ref, slot, cslot in ((own, H0, CH0), (gl, G, CG), (cl, C, CC), (tl, TA, CTA)):
        fine = ref[...].reshape(ROWS, CH, 128)
        state[slot, mine] = fine
        value = restrict(fine, mats)
        coarse[cslot] = value * ratio if cslot == CTA else value
        cstate[cslot, 4:20] = coarse[cslot]
    cstate[CS0, 4:20] = coarse[CG] + coarse[CH0]
    state[S0, mine] = state[G, mine] + state[H0, mine]
    for at, cslot in enumerate((CG, CC, CTA)):
        off[at * n : at * n + n] = cstate[cslot, pl.ds(4 + odd * (CROWS - CHALO), CHALO)].reshape(n, 128)
    coarse_steps(cstate, d, dy, ((6, 18), (8, 16)))
    fine_steps(state, d, dy, [(HALO + 2 * k, WIN - HALO - 2 * k) for k in (1, 2, 3, 4)])
    mid[...] = state[H0 + 4, 2 * HALO : WIN - 2 * HALO].reshape(16 * CH, 128)
    for at, slot in enumerate(KEPT):
        rims[at, 0:RIM] = state[slot, HALO : HALO + RIM]
        rims[at, RIM:] = state[slot, WIN - HALO - RIM : WIN - HALO]


def coarse_steps(cstate, d, dy, spans):
    masks = column_masks(CCH)
    cd, cdy = d.at[0:24, 0:CCH], dy.at[0:24, 0:CCH]
    for step, (lo, hi) in enumerate(spans):

        def emit(a, b, value, step=step):
            if step == 0:
                cstate[CH0 + 1, a:b] = value
                cstate[CS0 + 1, a:b] = value + cstate[CG, a:b]
            else:
                cstate[CH0, a:b] = value

        flow(cstate.at[CH0 + step], cstate.at[CS0 + step], cstate.at[CG], cstate.at[CC], cstate.at[CTA], cd, cdy,
             lo, hi, masks, COARSE_GAIN, COARSE_CAP, 8, emit)


def fine_steps(state, d, dy, spans):
    masks = column_masks(CH)
    for step, (lo, hi) in enumerate(spans):

        def emit(a, b, value, step=step):
            state[H0 + step + 1, a:b] = value
            if step < 3:
                state[S0 + step + 1, a:b] = value + state[G, a:b]

        flow(state.at[H0 + step], state.at[S0 + step], state.at[G], state.at[C], state.at[TA], d, dy,
             lo, hi, masks, FINE_GAIN, FINE_CAP, 4, emit)


def outer_kernel(place, space, last, off, inside, mid, rims, cstate_in, end, prev, payload, state, cstate, d, dy):
    for at, slot in enumerate(KEPT):
        state[slot, HALO : HALO + RIM] = rims[at, 0:RIM]
        state[slot, WIN - HALO - RIM : WIN - HALO] = rims[at, RIM:]
    for rim in (slice(HALO, HALO + RIM), slice(WIN - HALO - RIM, WIN - HALO)):
        for step in range(4):
            state[S0 + step, rim] = state[H0 + step, rim] + state[G, rim]
    cstate[:, 4:20] = cstate_in[:, 4:20]
    odd = space[0] & 1
    at_border = (space[0] == 0) | (space[0] == last[0])
    at = 0
    for slot, count in zip((H0, G, C, TA), EDGE):
        n = count * CH
        far = jnp.where(at_border, 0.0, off[at : at + n]).reshape(count, CH, 128)
        near = inside[at : at + n].reshape(count, CH, 128)
        state[slot, HALO - count : HALO] = jnp.where(odd == 1, near, far)
        state[slot, HALO + ROWS : HALO + ROWS + count] = jnp.where(odd == 1, far, near)
        at += n
    mats = restrict_mats()
    ratio = COARSE_TAU / FINE_TAU
    for lo, clo in ((0, 0), (40, 20)):
        state[S0, lo : lo + 8] = state[G, lo : lo + 8] + state[H0, lo : lo + 8]
        ground = restrict(state[G, lo : lo + 8], mats)
        thick = restrict(state[H0, lo : lo + 8], mats)
        cstate[CG, clo : clo + 4] = ground
        cstate[CH0, clo : clo + 4] = thick
        cstate[CS0, clo : clo + 4] = ground + thick
    for lo, clo in ((4, 2), (40, 20)):
        cstate[CC, clo : clo + 2] = restrict(state[C, lo : lo + 4], mats)
        cstate[CTA, clo : clo + 2] = restrict(state[TA, lo : lo + 4], mats) * ratio
    coarse_steps(cstate, d, dy, ((2, 6), (4, 8)))
    coarse_steps(cstate, d, dy, ((18, 22), (16, 20)))
    prev[...] = cstate[CH0, 4:20].reshape(CROWS * CCH, 128)
    fine_steps(state, d, dy, [(2 * k, HALO + 2 * k) for k in (1, 2, 3, 4)])
    fine_steps(state, d, dy, [(WIN - HALO - 2 * k, WIN - 2 * k) for k in (1, 2, 3, 4)])
    end[0 : 8 * CH] = state[H0 + 4, 8:16].reshape(8 * CH, 128)
    end[8 * CH : 24 * CH] = mid[...]
    end[24 * CH : 32 * CH] = state[H0 + 4, 32:40].reshape(8 * CH, 128)
    value = restrict(end[...].reshape(ROWS, CH, 128), mats).reshape(CROWS * CCH, 128)
    payload[...] = value - jnp.where(place[0] == 0, 0.0, prev[...])


def pack_kernel(source, target):
    target[...] = source[...]


def gather_kernel(place, space, cstate, far, near2, near1, base, j1, j2, off, inside):
    m = place[0]
    base[...] = jnp.where(m == 1, near1[...], jnp.where(m == 2, near2[...], far[...]))
    j1[...] = jnp.where(m == 2, far[...], near2[...])
    j2[...] = near1[...]
    odd = space[0] & 1
    at = 0
    for ref, count in zip((base, j1, j2), JUMPS):
        n = count * CCH
        skip = CROWS * CCH - n
        off[at : at + n] = ref[pl.ds(odd * skip, n)]
        inside[at : at + n] = ref[pl.ds((1 - odd) * skip, n)]
        at += n
    n = CHALO * CCH
    for cslot in (CG, CC, CTA):
        inside[at : at + n] = cstate[cslot, pl.ds(4 + (1 - odd) * (CROWS - CHALO), CHALO)].reshape(n, 128)
        at += n


def chain_kernel(place, space, last, own, cstate, end, prev, before, base, j1, j2, off, inside, soff,
                 out_hbm, nxt_hbm, h, s, s2, g, c, ta, d, dy, jump1, jump2, fix, now_m, fine, out, nxt, sems):
    m = place[0]
    odd = space[0] & 1
    at_border = (space[0] == 0) | (space[0] == last[0])
    bottom = CHALO + CROWS

    def window(ref, own, count, far_ref, at, skip):
        n = count * CCH
        far = jnp.where(at_border, 0.0, far_ref[at : at + n]).reshape(count, CCH, 128)
        near = inside[skip + at : skip + at + n].reshape(count, CCH, 128)
        ref[CHALO - count : CHALO] = jnp.where(odd == 1, near, far)
        ref[CHALO:bottom] = own
        ref[bottom : bottom + count] = jnp.where(odd == 1, far, near)
        return at + n

    @pl.when(m > 0)
    def _():
        at = 0
        for ref, slot in ((g, CG), (c, CC), (ta, CTA)):
            at = window(ref, cstate[slot, 4:20], CHALO, soff, at, JUMP_LINES)
        at = 0
        for ref, held, count in zip((h, jump1, jump2), (base, j1, j2), JUMPS):
            at = window(ref, held[...].reshape(CROWS, CCH, 128), count, off, at, 0)
        s[...] = g[...] + h[...]
        now_m[...] = h[CHALO:bottom]

    masks = column_masks(CCH)
    mats = restrict_mats()
    mine = slice(CHALO, bottom)
    fix[...] = jnp.zeros_like(fix)
    lo_mat, hi_mat = prolong_mats()

    def spread_out(value, field, target, target_hbm, first, keep=None):
        value = value.reshape(CROWS * CCH, 128)
        halves = [times(value, mat).reshape(CROWS, CCH, 128) for mat in (lo_mat, hi_mat)]
        wide = jnp.concatenate(halves, axis=1).reshape(CROWS, 1, CH, 128)
        total = (field[...].reshape(CROWS, 2, CH, 128) + wide).reshape(ROWS, CH, 128)
        if keep is not None:
            total = jnp.where(m == 0, keep, total)
        fine[...] = total.reshape(ROWS * CH, 128)
        copies = []
        for r in range(0, ROWS, 8):
            for k in range(CH):
                target[r : r + 8, k * 128 : k * 128 + 128] = fine[pl.ds(r * CH + line_of(k), 8, stride=CH), :]
            copy = pltpu.make_async_copy(target.at[r : r + 8], target_hbm.at[r : r + 8], sems.at[first + r // 8])
            copy.start()
            copies.append(copy)
        return copies

    edge = 0
    waits = []
    for k, jump in ((1, jump1), (2, jump2), (3, None)):
        if k == 3:
            coarse_before = restrict(before[...].reshape(ROWS, CH, 128), mats)
            waits += spread_out(now_m[...] - coarse_before, before, nxt, nxt_hbm, 0,
                                own[...].reshape(ROWS, CH, 128))
        first_edge = edge
        edge += 4

        @pl.when(m >= k)
        def _(k=k, jump=jump, first_edge=first_edge):
            for step, (now, later) in enumerate(((s, s2), (s2, s))):
                lo = first_edge + 2 * (step + 1)

                def emit(a, b, value, later=later):
                    h[a:b] = value
                    later[a:b] = value + g[a:b]

                flow(h, now, g, c, ta, d, dy, lo, CWIN - lo, masks, COARSE_GAIN, COARSE_CAP, 8, emit)

            @pl.when(m == k)
            def _():
                fix[...] = h[mine] - prev[...].reshape(CROWS, CCH, 128)

            if jump is not None:
                lo = first_edge + 4
                for a in range(lo, CWIN - lo, 8):
                    b = min(a + 8, CWIN - lo)
                    value = h[a:b] + jump[a:b]
                    h[a:b] = value
                    s[a:b] = value + g[a:b]

                @pl.when(m == k + 1)
                def _():
                    now_m[...] = h[mine]

    waits += spread_out(fix[...], end, out, out_hbm, 4)
    for copy in waits:
        copy.wait()


def lines(n):
    return jax.ShapeDtypeStruct((n, 128), F32)


VMEM, SMEM, HBM = pltpu.VMEM, pltpu.SMEM, pltpu.HBM


def call(kernel, name, ins, outs, scratch=(), in_spaces=None, out_space=VMEM, limit=16):
    spaces = {"s": SMEM, "h": HBM, "v": VMEM}
    return pl.pallas_call(
        kernel,
        out_shape=outs,
        in_specs=[pl.BlockSpec(memory_space=spaces[letter]) for letter in in_spaces],
        out_specs=[pl.BlockSpec(memory_space=out_space)] * len(outs),
        scratch_shapes=[pltpu.VMEM(item, F32) if isinstance(item, tuple) else item for item in scratch],
        compiler_params=pltpu.CompilerParams(vmem_limit_bytes=limit * 2**20),
        name=name,
    )(*ins)


def shifted(x, by):
    devices = lax.axis_size("tm")
    return lax.ppermute(x, "tm", [(i, (i + by) % devices) for i in range(devices)])


def far_swap(x):
    slices, devices = lax.axis_size("tm"), lax.axis_size("space")
    pairs = [(m * devices + i, m * devices + i + 1) for m in range(slices) for i in range(1, devices - 1, 2)]
    pairs += [(m * devices + i, (m + 1) * devices + i) for m in range(0, slices, 2) for i in (0, devices - 1)]
    return lax.ppermute(x, ("tm", "space"), pairs + [(j, i) for i, j in pairs])


def far_swap_later(x):
    slices, devices = lax.axis_size("tm"), lax.axis_size("space")
    pairs = [(m * devices + i, m * devices + i + 1) for m in range(1, slices) for i in range(1, devices - 1, 2)]
    pairs += [(i, i + 1) for i in range(0, devices, 2)]
    ring = [(m * devices + i, (m % (slices - 1) + 1) * devices + i) for m in range(1, slices) for i in (0, devices - 1)]
    return lax.ppermute(x, ("tm", "space"), pairs + [(j, i) for i, j in pairs] + ring)


def near_swap(x):
    devices = lax.axis_size("space")
    return lax.ppermute(x, "space", [(i, i ^ 1) for i in range(devices)])


def per_device(thickness, bed_class, ice_mask, zone_index, bed_levels, balance_rates):
    place = lax.axis_index("tm").astype(jnp.int32).reshape(1)
    space = lax.axis_index("space").astype(jnp.int32).reshape(1)
    last = jnp.full((1,), lax.axis_size("space") - 1, jnp.int32)
    raw = (space,) + tuple(
        pltpu.with_memory_space_constraint(x, HBM)
        for x in (thickness[0], bed_class, ice_mask, zone_index, bed_levels, balance_rates)
    )
    coarse_lines = CROWS * CCH
    tables = [pltpu.SMEM((16,), F32), pltpu.SMEM((8,), F32)]
    maps = [jax.ShapeDtypeStruct((ROWS, CH * 128), t) for t in (F32, jnp.int32, jnp.int32, jnp.int32)]
    maps.append(lines(24))
    off, inside, *maps = call(
        edge_kernel, "edges", raw, [lines(EDGE_LINES)] * 2 + maps,
        tables + [(2, 8 * CH, 128)] * 4 + [pltpu.SemaphoreType.DMA((14,))],
        "shhhhhh",
    )
    off, inside = far_swap(off), near_swap(inside)
    own, mid, rims, cstate, soff = call(
        inner_kernel, "inner", (space, *maps),
        [lines(ROWS * CH), lines(16 * CH), jax.ShapeDtypeStruct((len(KEPT), 2 * RIM, CH, 128), F32)]
        + [jax.ShapeDtypeStruct((7, 24, CCH, 128), F32)] + [lines(STATIC_LINES)],
        [(ROWS * CH, 128)] * 3 + [(12, WIN, CH, 128)] + [(WIN, CH, 128)] * 2,
        "svvvvv",
    )
    end, prev, payload = call(
        outer_kernel, "outer", (place, space, last, off, inside, mid, rims, cstate),
        [lines(ROWS * CH)] + [lines(coarse_lines)] * 2,
        [(12, WIN, CH, 128), (7, 24, CCH, 128)] + [(WIN, CH, 128)] * 2,
        "sssvvvvv",
    )
    soff = far_swap_later(soff)
    rounds = [lax.ppermute(payload, "tm", [(i, i ^ k) for i in range(lax.axis_size("tm"))]) for k in (3, 2, 1)]
    *rounds, soff = lax.optimization_barrier((*rounds, soff))
    base, j1, j2, off, inside = call(
        gather_kernel, "gather", (place, space, cstate, *rounds),
        [lines(coarse_lines)] * 3 + [lines(JUMP_LINES), lines(JUMP_LINES + STATIC_LINES)], (), "ssvvvv",
    )
    before = shifted(end, 1)
    off, inside = far_swap_later(off), near_swap(inside)
    out, nxt = call(
        chain_kernel, "chain",
        (place, space, last, own, cstate, end, prev, before, base, j1, j2, off, inside, soff),
        [jax.ShapeDtypeStruct((ROWS, CH * 128), F32)] * 2,
        [(CWIN, CCH, 128)] * 10 + [(CROWS, CCH, 128)] * 2 + [(ROWS * CH, 128)]
        + [(ROWS, CH * 128)] * 2 + [pltpu.SemaphoreType.DMA((8,))],
        "sss" + "v" * 11, out_space=HBM,
    )
    return out[None], nxt[None]


def solution(mesh):
    placed = (
        P("tm", "space", None),
        P("space", None),
        P("space", None),
        P("space", None),
        P(),
        P(),
    )
    return jax.shard_map(
        per_device,
        mesh=mesh,
        in_specs=placed,
        out_specs=(P("tm", "space", None), P("tm", "space", None)),
        check_vma=False,
    )
```

```python
import jax
import jax.numpy as jnp
from jax import lax
from jax.experimental import pallas as pl
from jax.experimental.pallas import tpu as pltpu
from jax.sharding import PartitionSpec as P

ROWS = 32
CH = 16
CROWS = ROWS // 2
CCH = CH // 2
HALO = 8
WIN = ROWS + 2 * HALO
RIM = 10
CHALO = 12
CWIN = CROWS + 2 * CHALO
F32 = jnp.float32
BF16 = jnp.bfloat16

FINE_GAIN, FINE_CAP = 0.5 / 4.0 * 0.1, 0.1
COARSE_GAIN, COARSE_CAP = 0.5 / 16.0 * 0.05, 0.05
FINE_TAU, COARSE_TAU = 0.2, 0.4


def column_masks(chunks):
    lane = lax.broadcasted_iota(jnp.int32, (8, 128), 1)
    sub = lax.broadcasted_iota(jnp.int32, (8, 128), 0)
    left, right = lane == 0, lane == 127
    return chunks, left, left & (sub == 0), right, right & (sub == 7)


def line_of(k):
    return (k % 2) * 8 + k // 2


def from_left(x, masks, fill):
    chunks, edge, border, _, _ = masks
    a = pltpu.roll(x, 1, axis=2)
    if chunks == CCH:
        return jnp.where(border[None], fill, jnp.where(edge[None], pltpu.roll(a, 1, axis=1), a))
    even, odd = a[:, :8], a[:, 8:]
    if not isinstance(fill, float):
        fill = fill[:, :8]
    first = jnp.where(border[None], fill, jnp.where(edge[None], pltpu.roll(odd, 1, axis=1), even))
    return jnp.concatenate([first, jnp.where(edge[None], even, odd)], axis=1)


def from_right(x, masks, fill):
    chunks, _, _, edge, border = masks
    a = pltpu.roll(x, 127, axis=2)
    if chunks == CCH:
        return jnp.where(border[None], fill, jnp.where(edge[None], pltpu.roll(a, 7, axis=1), a))
    even, odd = a[:, :8], a[:, 8:]
    second = jnp.where(border[None], fill, jnp.where(edge[None], pltpu.roll(even, 7, axis=1), odd))
    return jnp.concatenate([jnp.where(edge[None], odd, even), second], axis=1)


def flow(h, s, g, c, ta, d, dy, lo, hi, masks, gain, cap, block, emit):
    for a in range(lo - 1, hi + 1, block):
        b = min(a + block, hi + 1)
        level = s[a:b]
        right = from_right(level, masks, 0.0)
        left = from_left(level, masks, 0.0)
        sx = s[a + 1 : b + 1] - s[a - 1 : b - 1]
        sy = right - left
        t = h[a:b]
        t2 = t * t
        fifth = t2 * t2 * t
        d[a:b] = jnp.minimum(fifth * gain * (sx * sx + sy * sy), cap)
        dy[a:b] = right - level
    for a in range(lo, hi, block):
        b = min(a + block, hi)
        dd = d[a - 1 : b + 1]
        ss = s[a - 1 : b + 1]
        fx = (dd[1:] + dd[:-1]) * (ss[1:] - ss[:-1])
        mid = dd[1:-1]
        fy = (mid + from_right(mid, masks, 0.0)) * dy[a:b]
        fy_left = from_left(fy, masks, mid * ss[1:-1])
        new = h[a:b] + (fx[1:] - fx[:-1] + fy - fy_left + ta[a:b])
        emit(a, b, jnp.maximum(new, 0.0) * c[a:b])


def split3(x):
    hi = x.astype(BF16)
    r = x - hi.astype(F32)
    mid = r.astype(BF16)
    lo = (r - mid.astype(F32)).astype(BF16)
    return hi, mid, lo


def times(x, m):
    parts = [jnp.dot(p, m, preferred_element_type=F32) for p in split3(x)]
    return parts[0] + (parts[1] + parts[2])


def restrict_mats():
    i = lax.broadcasted_iota(jnp.int32, (128, 128), 0)
    j = lax.broadcasted_iota(jnp.int32, (128, 128), 1)
    half = lax.shift_right_logical(i, 1)
    lo = jnp.where(j == half, 0.25, 0.0).astype(BF16)
    hi = jnp.where(j == half + 64, 0.25, 0.0).astype(BF16)
    return lo, hi


def prolong_mats():
    i = lax.broadcasted_iota(jnp.int32, (128, 128), 0)
    j = lax.broadcasted_iota(jnp.int32, (128, 128), 1)
    half = lax.shift_right_logical(j, 1)
    lo = jnp.where(i == half, 1.0, 0.0).astype(BF16)
    hi = jnp.where(i == half + 64, 1.0, 0.0).astype(BF16)
    return lo, hi


def restrict(x, mats):
    n = x.shape[0] // 2
    y = x.reshape(n, 2, CH, 128)
    y = y[:, 0] + y[:, 1]
    even, odd = y[:, :8].reshape(n * CCH, 128), y[:, 8:].reshape(n * CCH, 128)
    return (times(even, mats[0]) + times(odd, mats[1])).reshape(n, CCH, 128)


def look_up(index, table, size):
    values = [table[k] for k in range(size)]
    bit = 0
    while len(values) > 1:
        on = (lax.shift_right_logical(index, bit) & 1) == 1
        values = [jnp.where(on, values[k + 1], values[k]) for k in range(0, len(values), 2)]
        bit += 1
    return values[0]


EDGE = (8, 8, 6, 6)
EDGE_LINES = sum(EDGE) * CH
STATIC_LINES = 3 * CHALO * CCH
JUMPS = (12, 8, 4)
JUMP_LINES = sum(JUMPS) * CCH
H0, S0, G, C, TA = 0, 5, 9, 10, 11
KEPT = (0, 1, 2, 3, 4, 9, 10, 11)
CH0, CS0, CG, CC, CTA = 0, 2, 4, 5, 6


def fetch(pairs, sems):
    copies = [pltpu.make_async_copy(src, dst, sems.at[i]) for i, (src, dst) in enumerate(pairs)]
    for copy in copies:
        copy.start()
    return copies


def edge_kernel(space, thick, bed, mask, zone, levels, rates, off, inside, tv, bv, mv, zv, tab,
                lev, rat, hx, gx, cx, tx, sems):
    pairs = [(levels, lev), (rates, rat)]
    maps = ((bed, bv), (zone, zv), (thick, tv), (mask, mv))
    for r, count in ((0, 8), (ROWS - 8, 8), (8, ROWS - 16)):
        pairs += [(src.at[r : r + count], dst.at[r : r + count]) for src, dst in maps]
    copies = fetch(pairs, sems)
    for copy in copies[:10]:
        copy.wait()
    for k in range(16):
        tab[k : k + 1] = jnp.full((1, 128), lev[k], F32)
    for k in range(8):
        tab[16 + k : 17 + k] = jnp.full((1, 128), rat[k], F32)
    for half in range(2):
        r = slice(half * (ROWS - 8), half * (ROWS - 8) + 8)
        for k in range(CH):
            cols = slice(k * 128, k * 128 + 128)
            there = (half, pl.ds(line_of(k), 8, stride=CH), slice(None))
            hx[there] = tv[r, cols]
            gx[there] = look_up(bv[r, cols], lev, 16)
            cx[there] = mv[r, cols].astype(F32)
            tx[there] = look_up(zv[r, cols], rat, 8) * FINE_TAU
    odd = space[0] & 1
    at = 0
    for ref, count in zip((hx, gx, cx, tx), EDGE):
        n = count * CH
        skip = (8 - count) * CH
        off[at : at + n] = ref[odd, pl.ds(odd * skip, n)]
        inside[at : at + n] = ref[1 - odd, pl.ds((1 - odd) * skip, n)]
        at += n
    for copy in copies[10:]:
        copy.wait()


def inner_kernel(space, tv, bv, mv, zv, tab, own, mid, rims, cstate, off, gl, cl, tl, state, d, dy):
    table = [jnp.broadcast_to(tab[k : k + 1], (8, 128)) for k in range(24)]
    lev, rat = table[:16], table[16:]
    for r in range(0, ROWS, 8):
        for k in range(CH):
            here = (slice(r, r + 8), slice(k * 128, k * 128 + 128))
            there = (pl.ds(r * CH + line_of(k), 8, stride=CH), slice(None))
            own[there] = tv[here]
            gl[there] = look_up(bv[here], lev, 16)
            cl[there] = mv[here].astype(F32)
            tl[there] = look_up(zv[here], rat, 8) * FINE_TAU
    mats = restrict_mats()
    mine = slice(HALO, HALO + ROWS)
    ratio = COARSE_TAU / FINE_TAU
    odd = space[0] & 1
    n = CHALO * CCH
    coarse = {}
    for ref, slot, cslot in ((own, H0, CH0), (gl, G, CG), (cl, C, CC), (tl, TA, CTA)):
        fine = ref[...].reshape(ROWS, CH, 128)
        state[slot, mine] = fine
        value = restrict(fine, mats)
        coarse[cslot] = value * ratio if cslot == CTA else value
        cstate[cslot, 4:20] = coarse[cslot]
    cstate[CS0, 4:20] = coarse[CG] + coarse[CH0]
    state[S0, mine] = state[G, mine] + state[H0, mine]
    for at, cslot in enumerate((CG, CC, CTA)):
        off[at * n : at * n + n] = cstate[cslot, pl.ds(4 + odd * (CROWS - CHALO), CHALO)].reshape(n, 128)
    coarse_steps(cstate, d, dy, ((0, 6, 18), (1, 8, 16)))
    fine_steps(state, d, dy, [(k - 1, HALO + 2 * k, WIN - HALO - 2 * k) for k in (1, 2, 3, 4)])
    mid[...] = state[H0 + 4, 2 * HALO : WIN - 2 * HALO].reshape(16 * CH, 128)
    for at, slot in enumerate(KEPT):
        rims[at, 0:RIM] = state[slot, HALO : HALO + RIM]
        rims[at, RIM:] = state[slot, WIN - HALO - RIM : WIN - HALO]


def coarse_steps(cstate, d, dy, spans):
    masks = column_masks(CCH)
    cd, cdy = d.at[0:24, 0:CCH], dy.at[0:24, 0:CCH]
    for step, lo, hi in spans:

        def emit(a, b, value, step=step):
            if step == 0:
                cstate[CH0 + 1, a:b] = value
                cstate[CS0 + 1, a:b] = value + cstate[CG, a:b]
            else:
                cstate[CH0, a:b] = value

        flow(cstate.at[CH0 + step], cstate.at[CS0 + step], cstate.at[CG], cstate.at[CC], cstate.at[CTA], cd, cdy,
             lo, hi, masks, COARSE_GAIN, COARSE_CAP, 8, emit)


def fine_steps(state, d, dy, spans):
    masks = column_masks(CH)
    for step, lo, hi in spans:

        def emit(a, b, value, step=step):
            state[H0 + step + 1, a:b] = value
            if step < 3:
                state[S0 + step + 1, a:b] = value + state[G, a:b]

        flow(state.at[H0 + step], state.at[S0 + step], state.at[G], state.at[C], state.at[TA], d, dy,
             lo, hi, masks, FINE_GAIN, FINE_CAP, 4, emit)


def outer_kernel(place, space, last, off, inside, mid, rims, cstate_in, end, prev, payload, state, cstate, d, dy):
    for at, slot in enumerate(KEPT):
        state[slot, HALO : HALO + RIM] = rims[at, 0:RIM]
        state[slot, WIN - HALO - RIM : WIN - HALO] = rims[at, RIM:]
    for rim in (slice(HALO, HALO + RIM), slice(WIN - HALO - RIM, WIN - HALO)):
        for step in range(4):
            state[S0 + step, rim] = state[H0 + step, rim] + state[G, rim]
    cstate[:, 4:20] = cstate_in[:, 4:20]
    odd = space[0] & 1
    at_border = (space[0] == 0) | (space[0] == last[0])
    at = 0
    for slot, count in zip((H0, G, C, TA), EDGE):
        n = count * CH
        far = jnp.where(at_border, 0.0, off[at : at + n]).reshape(count, CH, 128)
        near = inside[at : at + n].reshape(count, CH, 128)
        state[slot, HALO - count : HALO] = jnp.where(odd == 1, near, far)
        state[slot, HALO + ROWS : HALO + ROWS + count] = jnp.where(odd == 1, far, near)
        at += n
    mats = restrict_mats()
    ratio = COARSE_TAU / FINE_TAU
    for lo, clo in ((0, 0), (40, 20)):
        state[S0, lo : lo + 8] = state[G, lo : lo + 8] + state[H0, lo : lo + 8]
        ground = restrict(state[G, lo : lo + 8], mats)
        thick = restrict(state[H0, lo : lo + 8], mats)
        cstate[CG, clo : clo + 4] = ground
        cstate[CH0, clo : clo + 4] = thick
        cstate[CS0, clo : clo + 4] = ground + thick
    for lo, clo in ((4, 2), (40, 20)):
        cstate[CC, clo : clo + 2] = restrict(state[C, lo : lo + 4], mats)
        cstate[CTA, clo : clo + 2] = restrict(state[TA, lo : lo + 4], mats) * ratio
    coarse_steps(cstate, d, dy, ((0, 2, 6), (0, 18, 22), (1, 4, 8), (1, 16, 20)))
    prev[...] = cstate[CH0, 4:20].reshape(CROWS * CCH, 128)
    spans = []
    for k in (1, 2, 3, 4):
        spans += [(k - 1, 2 * k, HALO + 2 * k), (k - 1, WIN - HALO - 2 * k, WIN - 2 * k)]
    fine_steps(state, d, dy, spans)
    end[0 : 8 * CH] = state[H0 + 4, 8:16].reshape(8 * CH, 128)
    end[8 * CH : 24 * CH] = mid[...]
    end[24 * CH : 32 * CH] = state[H0 + 4, 32:40].reshape(8 * CH, 128)
    value = restrict(end[...].reshape(ROWS, CH, 128), mats).reshape(CROWS * CCH, 128)
    payload[...] = value - jnp.where(place[0] == 0, 0.0, prev[...])


def pack_kernel(source, target):
    target[...] = source[...]


def gather_kernel(place, space, cstate, far, near2, near1, base, j1, j2, off, inside):
    m = place[0]
    base[...] = jnp.where(m == 1, near1[...], jnp.where(m == 2, near2[...], far[...]))
    j1[...] = jnp.where(m == 2, far[...], near2[...])
    j2[...] = near1[...]
    odd = space[0] & 1
    at = 0
    for ref, count in zip((base, j1, j2), JUMPS):
        n = count * CCH
        skip = CROWS * CCH - n
        off[at : at + n] = ref[pl.ds(odd * skip, n)]
        inside[at : at + n] = ref[pl.ds((1 - odd) * skip, n)]
        at += n
    n = CHALO * CCH
    for cslot in (CG, CC, CTA):
        inside[at : at + n] = cstate[cslot, pl.ds(4 + (1 - odd) * (CROWS - CHALO), CHALO)].reshape(n, 128)
        at += n


def chain_kernel(place, space, last, own, cstate, end, prev, before, base, j1, j2, off, inside, soff,
                 out_hbm, nxt_hbm, h, s, s2, g, c, ta, d, dy, jump1, jump2, fix, now_m, fine, out, nxt, sems):
    m = place[0]
    odd = space[0] & 1
    at_border = (space[0] == 0) | (space[0] == last[0])
    bottom = CHALO + CROWS

    def window(ref, own, count, far_ref, at, skip):
        n = count * CCH
        far = jnp.where(at_border, 0.0, far_ref[at : at + n]).reshape(count, CCH, 128)
        near = inside[skip + at : skip + at + n].reshape(count, CCH, 128)
        ref[CHALO - count : CHALO] = jnp.where(odd == 1, near, far)
        ref[CHALO:bottom] = own
        ref[bottom : bottom + count] = jnp.where(odd == 1, far, near)
        return at + n

    @pl.when(m > 0)
    def _():
        at = 0
        for ref, slot in ((g, CG), (c, CC), (ta, CTA)):
            at = window(ref, cstate[slot, 4:20], CHALO, soff, at, JUMP_LINES)
        at = 0
        for ref, held, count in zip((h, jump1, jump2), (base, j1, j2), JUMPS):
            at = window(ref, held[...].reshape(CROWS, CCH, 128), count, off, at, 0)
        s[...] = g[...] + h[...]
        now_m[...] = h[CHALO:bottom]

    masks = column_masks(CCH)
    mats = restrict_mats()
    mine = slice(CHALO, bottom)
    fix[...] = jnp.zeros_like(fix)
    lo_mat, hi_mat = prolong_mats()

    def spread_out(value, field, target, target_hbm, first, keep=None):
        value = value.reshape(CROWS * CCH, 128)
        halves = [times(value, mat).reshape(CROWS, CCH, 128) for mat in (lo_mat, hi_mat)]
        wide = jnp.concatenate(halves, axis=1).reshape(CROWS, 1, CH, 128)
        total = (field[...].reshape(CROWS, 2, CH, 128) + wide).reshape(ROWS, CH, 128)
        if keep is not None:
            total = jnp.where(m == 0, keep, total)
        fine[...] = total.reshape(ROWS * CH, 128)
        copies = []
        for r in range(0, ROWS, 8):
            for k in range(CH):
                target[r : r + 8, k * 128 : k * 128 + 128] = fine[pl.ds(r * CH + line_of(k), 8, stride=CH), :]
            copy = pltpu.make_async_copy(target.at[r : r + 8], target_hbm.at[r : r + 8], sems.at[first + r // 8])
            copy.start()
            copies.append(copy)
        return copies

    edge = 0
    waits = []
    for k, jump in ((1, jump1), (2, jump2), (3, None)):
        if k == 3:
            coarse_before = restrict(before[...].reshape(ROWS, CH, 128), mats)
            waits += spread_out(now_m[...] - coarse_before, before, nxt, nxt_hbm, 0,
                                own[...].reshape(ROWS, CH, 128))
        first_edge = edge
        edge += 4

        @pl.when(m >= k)
        def _(k=k, jump=jump, first_edge=first_edge):
            for step, (now, later) in enumerate(((s, s2), (s2, s))):
                lo = first_edge + 2 * (step + 1)

                def emit(a, b, value, later=later):
                    h[a:b] = value
                    later[a:b] = value + g[a:b]

                flow(h, now, g, c, ta, d, dy, lo, CWIN - lo, masks, COARSE_GAIN, COARSE_CAP, 8, emit)

            @pl.when(m == k)
            def _():
                fix[...] = h[mine] - prev[...].reshape(CROWS, CCH, 128)

            if jump is not None:
                lo = first_edge + 4
                for a in range(lo, CWIN - lo, 8):
                    b = min(a + 8, CWIN - lo)
                    value = h[a:b] + jump[a:b]
                    h[a:b] = value
                    s[a:b] = value + g[a:b]

                @pl.when(m == k + 1)
                def _():
                    now_m[...] = h[mine]

    waits += spread_out(fix[...], end, out, out_hbm, 4)
    for copy in waits:
        copy.wait()


def lines(n):
    return jax.ShapeDtypeStruct((n, 128), F32)


VMEM, SMEM, HBM = pltpu.VMEM, pltpu.SMEM, pltpu.HBM


def call(kernel, name, ins, outs, scratch=(), in_spaces=None, out_space=VMEM, limit=16):
    spaces = {"s": SMEM, "h": HBM, "v": VMEM}
    return pl.pallas_call(
        kernel,
        out_shape=outs,
        in_specs=[pl.BlockSpec(memory_space=spaces[letter]) for letter in in_spaces],
        out_specs=[pl.BlockSpec(memory_space=out_space)] * len(outs),
        scratch_shapes=[pltpu.VMEM(item, F32) if isinstance(item, tuple) else item for item in scratch],
        compiler_params=pltpu.CompilerParams(vmem_limit_bytes=limit * 2**20),
        name=name,
    )(*ins)


def shifted(x, by):
    devices = lax.axis_size("tm")
    return lax.ppermute(x, "tm", [(i, (i + by) % devices) for i in range(devices)])


def far_swap(x):
    slices, devices = lax.axis_size("tm"), lax.axis_size("space")
    pairs = [(m * devices + i, m * devices + i + 1) for m in range(slices) for i in range(1, devices - 1, 2)]
    pairs += [(m * devices + i, (m + 1) * devices + i) for m in range(0, slices, 2) for i in (0, devices - 1)]
    return lax.ppermute(x, ("tm", "space"), pairs + [(j, i) for i, j in pairs])


def far_swap_later(x):
    slices, devices = lax.axis_size("tm"), lax.axis_size("space")
    pairs = [(m * devices + i, m * devices + i + 1) for m in range(1, slices) for i in range(1, devices - 1, 2)]
    pairs += [(i, i + 1) for i in range(0, devices, 2)]
    ring = [(m * devices + i, (m % (slices - 1) + 1) * devices + i) for m in range(1, slices) for i in (0, devices - 1)]
    return lax.ppermute(x, ("tm", "space"), pairs + [(j, i) for i, j in pairs] + ring)


def near_swap(x):
    devices = lax.axis_size("space")
    return lax.ppermute(x, "space", [(i, i ^ 1) for i in range(devices)])


def per_device(thickness, bed_class, ice_mask, zone_index, bed_levels, balance_rates):
    place = lax.axis_index("tm").astype(jnp.int32).reshape(1)
    space = lax.axis_index("space").astype(jnp.int32).reshape(1)
    last = jnp.full((1,), lax.axis_size("space") - 1, jnp.int32)
    raw = (space,) + tuple(
        pltpu.with_memory_space_constraint(x, HBM)
        for x in (thickness[0], bed_class, ice_mask, zone_index, bed_levels, balance_rates)
    )
    coarse_lines = CROWS * CCH
    tables = [pltpu.SMEM((16,), F32), pltpu.SMEM((8,), F32)]
    maps = [jax.ShapeDtypeStruct((ROWS, CH * 128), t) for t in (F32, jnp.int32, jnp.int32, jnp.int32)]
    maps.append(lines(24))
    off, inside, *maps = call(
        edge_kernel, "edges", raw, [lines(EDGE_LINES)] * 2 + maps,
        tables + [(2, 8 * CH, 128)] * 4 + [pltpu.SemaphoreType.DMA((14,))],
        "shhhhhh",
    )
    off, inside = far_swap(off), near_swap(inside)
    own, mid, rims, cstate, soff = call(
        inner_kernel, "inner", (space, *maps),
        [lines(ROWS * CH), lines(16 * CH), jax.ShapeDtypeStruct((len(KEPT), 2 * RIM, CH, 128), F32)]
        + [jax.ShapeDtypeStruct((7, 24, CCH, 128), F32)] + [lines(STATIC_LINES)],
        [(ROWS * CH, 128)] * 3 + [(12, WIN, CH, 128)] + [(WIN, CH, 128)] * 2,
        "svvvvv",
    )
    end, prev, payload = call(
        outer_kernel, "outer", (place, space, last, off, inside, mid, rims, cstate),
        [lines(ROWS * CH)] + [lines(coarse_lines)] * 2,
        [(12, WIN, CH, 128), (7, 24, CCH, 128)] + [(WIN, CH, 128)] * 2,
        "sssvvvvv",
    )
    soff = far_swap_later(soff)
    rounds = [lax.ppermute(payload, "tm", [(i, i ^ k) for i in range(lax.axis_size("tm"))]) for k in (3, 2, 1)]
    *rounds, soff = lax.optimization_barrier((*rounds, soff))
    base, j1, j2, off, inside = call(
        gather_kernel, "gather", (place, space, cstate, *rounds),
        [lines(coarse_lines)] * 3 + [lines(JUMP_LINES), lines(JUMP_LINES + STATIC_LINES)], (), "ssvvvv",
    )
    before = shifted(end, 1)
    off, inside = far_swap_later(off), near_swap(inside)
    out, nxt = call(
        chain_kernel, "chain",
        (place, space, last, own, cstate, end, prev, before, base, j1, j2, off, inside, soff),
        [jax.ShapeDtypeStruct((ROWS, CH * 128), F32)] * 2,
        [(CWIN, CCH, 128)] * 10 + [(CROWS, CCH, 128)] * 2 + [(ROWS * CH, 128)]
        + [(ROWS, CH * 128)] * 2 + [pltpu.SemaphoreType.DMA((8,))],
        "sss" + "v" * 11, out_space=HBM,
    )
    return out[None], nxt[None]


def solution(mesh):
    placed = (
        P("tm", "space", None),
        P("space", None),
        P("space", None),
        P("space", None),
        P(),
        P(),
    )
    return jax.shard_map(
        per_device,
        mesh=mesh,
        in_specs=placed,
        out_specs=(P("tm", "space", None), P("tm", "space", None)),
        check_vma=False,
    )
```
